32 devices in a mesh: dp: 8 (over z, x), key: 4 (over y, core).
Axes of the slice: x: 2, y: 2, z: 4, core: 2. Of those that a mesh axis runs over, the one named last changes fastest.
Arguments:
- ray_tokens: bfloat16 [16384, 768], P('dp'), may hold values from -6 to 6
- latents: bfloat16 [8, 4096, 768], P('dp', 'key'), may hold values from -6 to 6
- group_ids: int32 [8, 4096], P('dp', 'key'), may hold values from 0 to 15
- ln1_gain: bfloat16 [768], replicated, may hold values from 0.25 to 1.75
- ln1_shift: bfloat16 [768], replicated, may hold values from -3 to 3
- w_query: bfloat16 [768, 768], replicated, may hold values from -0.21875 to 0.21875
- w_key: bfloat16 [768, 768], replicated, may hold values from -0.21875 to 0.21875
- w_value: bfloat16 [768, 768], replicated, may hold values from -0.21875 to 0.21875
- w_out: bfloat16 [768, 768], replicated, may hold values from -6 to 6
- ln2_gain: bfloat16 [768], replicated, may hold values from 0.25 to 1.75
- ln2_shift: bfloat16 [768], replicated, may hold values from -3 to 3
- w_up: bfloat16 [768, 1536], replicated, may hold values from -0.21875 to 0.21875
- b_up: bfloat16 [1536], replicated, may hold values from -3 to 3
- w_down: bfloat16 [1536, 768], replicated, may hold values from -0.15625 to 0.15625
- b_down: bfloat16 [768], replicated, may hold values from -3 to 3
- intrinsics: bfloat16 [16, 768], replicated, may hold values from -3 to 3
- out_grad: bfloat16 [16384, 768], P(('dp', 'key')), may hold values from -6 to 6
Outputs:
- mixed: bfloat16 [16384, 768], P(('dp', 'key'))
- rays_grad: float32 [16384, 768], P(('dp', 'key'))
- latents_grad: float32 [8, 4096, 768], P('dp', 'key')
- ln1_gain_grad: float32 [768], replicated
- ln1_shift_grad: float32 [768], replicated
- w_query_grad: float32 [768, 768], replicated
- w_key_grad: float32 [768, 768], replicated
- w_value_grad: float32 [768, 768], replicated
- w_out_grad: float32 [768, 768], replicated
- ln2_gain_grad: float32 [768], replicated
- ln2_shift_grad: float32 [768], replicated
- w_up_grad: float32 [768, 1536], replicated
- b_up_grad: float32 [1536], replicated
- w_down_grad: float32 [1536, 768], replicated
- b_down_grad: float32 [768], replicated
- intrinsics_grad: float32 [16, 768], replicated
The draws below stay inside these ranges and needn't reach their ends.
All inputs are finite; a program needn't handle non-finite values.
Results may differ from the reference program's by a relative error of at most 0.023.
Values may be sent and summed in bfloat16 or wider, within the bound.
No kernel may reach another device: no remote copies, remote signals or barrier semaphores. Data moves between devices by JAX's collectives and lax.ppermute only.
A program may use at most 192 MiB of HBM per device.

```python
import jax
import jax.numpy as jnp
from jax import lax

D = 768
H = 12
HD = 64
FF = 1536
GROUPS = 16
SCENES = 8
RAYS = 16384
LATENTS = 4096


def with_ends(array, key, smallest, high):
    longest = array.shape.index(max(array.shape))
    spots = []
    for shift in (0, 1):
        where = [jax.random.randint(jax.random.fold_in(key, axis), (), 0, length) for axis, length in enumerate(array.shape)]
        where[longest] = (where[longest] + shift) % array.shape[longest]
        spots.append(tuple(where))
    return array.at[spots[0]].set(smallest).at[spots[1]].set(high)


def steps_of(stream_key, shape, cuts, low, largest):
    def one(dim, parts):
        draws = jax.random.uniform(jax.random.fold_in(jax.random.fold_in(stream_key, 6), dim), (parts,), jnp.float32, low / len(cuts), largest / len(cuts))
        return jnp.repeat(jnp.exp(draws), shape[dim] // parts).reshape((-1,) + (1,) * (len(shape) - dim - 1))

    gain = one(*cuts[0])
    for cut in cuts[1:]:
        gain = gain * one(*cut)
    return gain


def scatter_about(rng, extent, scale, limit, shards=(), kind=jnp.bfloat16):
    array = scale * jax.random.normal(rng, extent, jnp.float32)
    if shards:
        array = array * steps_of(rng, extent, shards, -0.22, 0.18)
    return jnp.clip(array, -limit, limit).astype(kind)


def setup_inputs(seed: int = 0) -> dict:
    splits = jax.random.split(jax.random.key(seed), 18)
    ray_tokens = scatter_about(splits[0], (RAYS, D), 1.0, 6.0, ((0, 8),))
    latents = scatter_about(splits[1], (SCENES, LATENTS, D), 1.0, 6.0, ((0, 8), (1, 4)))
    group_ids = with_ends(jax.random.randint(splits[2], (SCENES, LATENTS), 0, GROUPS), jax.random.fold_in(splits[2], 1), 0, GROUPS - 1).astype(jnp.int32)
    ln1_gain = jnp.clip(1.0 + 0.15 * jax.random.normal(splits[3], (D,), jnp.float32), 0.25, 1.75).astype(jnp.bfloat16)
    ln1_shift = scatter_about(splits[4], (D,), 0.5, 3.0)
    w_query = scatter_about(splits[5], (D, D), D ** -0.5, 0.21875)
    w_key = scatter_about(splits[6], (D, D), D ** -0.5, 0.21875)
    w_value = scatter_about(splits[7], (D, D), D ** -0.5, 0.21875)
    w_out = scatter_about(splits[8], (D, D), (max(1, 3 * D // LATENTS)) ** -0.5, 6.0)
    ln2_gain = jnp.clip(1.0 + 0.15 * jax.random.normal(splits[9], (D,), jnp.float32), 0.25, 1.75).astype(jnp.bfloat16)
    ln2_shift = scatter_about(splits[10], (D,), 0.5, 3.0)
    w_up = scatter_about(splits[11], (D, FF), D ** -0.5, 0.21875)
    b_up = scatter_about(splits[12], (FF,), 0.5, 3.0)
    w_down = scatter_about(splits[13], (FF, D), FF ** -0.5, 0.15625)
    b_down = scatter_about(splits[14], (D,), 0.5, 3.0)
    intrinsics = scatter_about(splits[15], (GROUPS, D), 0.5, 3.0)
    out_grad = scatter_about(splits[16], (RAYS, D), 1.0, 6.0, ((0, 32),))
    return {"ray_tokens": ray_tokens, "latents": latents, "group_ids": group_ids, "ln1_gain": ln1_gain, "ln1_shift": ln1_shift, "w_query": w_query, "w_key": w_key, "w_value": w_value, "w_out": w_out, "ln2_gain": ln2_gain, "ln2_shift": ln2_shift, "w_up": w_up, "b_up": b_up, "w_down": w_down, "b_down": b_down, "intrinsics": intrinsics, "out_grad": out_grad}


@jax.custom_vjp
def low(v):
    return lax.optimization_barrier(v.astype(jnp.bfloat16)).astype(jnp.float32)

@jax.custom_vjp
def low_back(v):
    return v

def low_keep(v):
    return (low(v), None)

def low_pass(kept, grad):
    return (grad,)

def back_keep(v):
    return (v, None)

def back_low(kept, grad):
    return (low(grad),)
low.defvjp(low_keep, low_pass)
low_back.defvjp(back_keep, back_low)
EPSILON = 1e-05
HIGHEST = lax.Precision.HIGHEST

def layer_norm(values, gain_vec, shift_vec):
    centre = values - lax.optimization_barrier(jnp.mean(values, axis=-1, keepdims=True))
    return centre * lax.rsqrt(lax.optimization_barrier(jnp.mean(centre * centre, axis=-1, keepdims=True)) + EPSILON) * gain_vec + shift_vec

def product(left, right):
    return jnp.dot(left, right, precision=HIGHEST)

def attend_block(queries, key_heads, value_heads):
    scores = low_back(jnp.einsum('qhd,khd->hqk', queries, key_heads, precision=HIGHEST) * HD ** (-0.5))
    maxima = lax.optimization_barrier(jnp.max(scores, axis=-1, keepdims=True))
    exponent = jnp.exp(scores - maxima)
    totals = lax.optimization_barrier(jnp.sum(exponent, axis=-1))
    blended = jnp.einsum('hqk,khd->qhd', low(exponent), value_heads, precision=HIGHEST)
    return blended / jnp.transpose(totals)[:, :, None]

def scene_forward(ray_block, latent_block, lookup, params):
    gain_one, shift_one, w_query, w_key, w_value, w_out, gain_two, shift_two, w_up, b_up, w_down, b_down, table = params
    row_count = ray_block.shape[0]
    block_rows = min(512, row_count)
    normed = low(layer_norm(ray_block, gain_one, shift_one))
    queries = low_back(low(product(normed, w_query))).reshape(row_count // block_rows, block_rows, H, HD)
    carried = low(latent_block + product(lookup, table))
    key_heads = low_back(low(product(carried, w_key))).reshape(-1, H, HD)
    value_heads = low_back(low(product(carried, w_value))).reshape(-1, H, HD)
    attended = lax.map(jax.checkpoint(lambda portion: attend_block(portion, key_heads, value_heads)), queries)
    attended = low_back(low(attended.reshape(row_count, H * HD)))
    middle = ray_block + low_back(product(attended, w_out))
    hidden = low_back(product(low(layer_norm(middle, gain_two, shift_two)), w_up) + b_up)
    active = low_back(low(jax.nn.gelu(hidden)))
    return middle + product(active, w_down) + b_down

def reference(ray_tokens, latents, group_ids, ln1_gain, ln1_shift, w_query, w_key, w_value, w_out, ln2_gain, ln2_shift, w_up, b_up, w_down, b_down, intrinsics, out_grad):
    params = tuple((weight.astype(jnp.float32) for weight in (ln1_gain, ln1_shift, w_query, w_key, w_value, w_out, ln2_gain, ln2_shift, w_up, b_up, w_down, b_down, intrinsics)))
    group_index = jnp.arange(intrinsics.shape[0], dtype=jnp.int32)
    scene_count = latents.shape[0]

    def scene_step(grad_sums, pieces):
        ray_block, latent_block, id_block, grad_block = pieces
        lookup = (id_block[:, None] == group_index[None, :]).astype(jnp.float32)
        result, pullback = jax.vjp(lambda rows_in, lat_in, weights: scene_forward(rows_in, lat_in, lookup, weights), ray_block.astype(jnp.float32), latent_block.astype(jnp.float32), params)
        grad_rays, grad_latents, grad_params = pullback(grad_block.astype(jnp.float32))
        grad_sums = jax.tree.map(jnp.add, grad_sums, grad_params)
        return (grad_sums, (result.astype(jnp.bfloat16), grad_rays, grad_latents))
    empty_sums = jax.tree.map(jnp.zeros_like, params)
    grad_sums, (outputs, grad_rays, grad_latents) = lax.scan(scene_step, empty_sums, (ray_tokens.reshape(scene_count, -1, D), latents, group_ids, out_grad.reshape(scene_count, -1, D)))
    return (outputs.reshape(-1, D), grad_rays.reshape(-1, D), grad_latents, grad_sums[0], grad_sums[1], grad_sums[2], grad_sums[3], grad_sums[4], grad_sums[5], grad_sums[6], grad_sums[7], grad_sums[8], grad_sums[9], grad_sums[10], grad_sums[11], grad_sums[12])
```

```python
import functools

import jax
import jax.numpy as jnp
from jax import lax
from jax.experimental import pallas as pl
from jax.experimental.pallas import tpu as pltpu
from jax.sharding import PartitionSpec as P

H = 12
HD = 64
PAIR = 2 * HD
EPSILON = 1e-05
HIGHEST = lax.Precision.HIGHEST
BF = jnp.bfloat16
F32 = jnp.float32
LOG2E = 1.4426950408889634
LN2 = 0.6931471805599453
VMEM = 60 * 1024 * 1024


def dot(a, b, dims=((1,), (0,))):
    return lax.dot_general(a, b, (dims, ((), ())), preferred_element_type=F32)


NT = ((1,), (1,))
TN = ((0,), (0,))


def params(**kw):
    return pltpu.CompilerParams(vmem_limit_bytes=VMEM, **kw)


def head_half(x, h, axis=1):
    i = lax.broadcasted_iota(jnp.int32, x.shape, axis)
    return jnp.where((i < HD) == (h == 0), x, jnp.zeros_like(x))


def norm_forward(values, gain_vec, shift_vec):
    centre = values - jnp.mean(values, axis=-1, keepdims=True)
    scaled = lax.rsqrt(jnp.mean(centre * centre, axis=-1, keepdims=True) + EPSILON)
    unit_rows = centre * scaled
    return (unit_rows * gain_vec + shift_vec, unit_rows, scaled)


def norm_backward(grad_rows, unit_rows, scaled, gain_vec):
    grad_unit = grad_rows * gain_vec
    centred_grad = (
        grad_unit
        - jnp.mean(grad_unit, axis=-1, keepdims=True)
        - unit_rows * jnp.mean(grad_unit * unit_rows, axis=-1, keepdims=True)
    )
    return (
        scaled * centred_grad,
        jnp.sum(grad_rows * unit_rows, axis=0),
        jnp.sum(grad_rows, axis=0),
    )


def query_kernel(order, rays, gain, shift, wq, normed, q):
    n, _, _ = norm_forward(rays[...].astype(F32), gain[...].astype(F32), shift[...].astype(F32))
    n = n.astype(BF)
    normed[...] = n
    q[...] = (dot(n, wq[...]) * (HD**-0.5 * LOG2E)).astype(BF)


def query_call(order, core, rays, gain, shift, wq, share):
    rows, width = rays.shape
    cols = width // 2
    blocks = rows // share
    pre = jnp.concatenate([order, core[None]])
    return pl.pallas_call(
        query_kernel,
        grid_spec=pltpu.PrefetchScalarGridSpec(
            num_scalar_prefetch=1,
            grid=(blocks,),
            in_specs=[
                pl.BlockSpec((share, width), lambda i, o: (o[i], 0)),
                pl.BlockSpec((1, width), lambda i, o: (0, 0)),
                pl.BlockSpec((1, width), lambda i, o: (0, 0)),
                pl.BlockSpec((width, cols), lambda i, o: (0, o[blocks])),
            ],
            out_specs=[
                pl.BlockSpec((share, width), lambda i, o: (i, 0)),
                pl.BlockSpec((share, cols), lambda i, o: (i, 0)),
            ],
        ),
        out_shape=[
            jax.ShapeDtypeStruct((rows, width), BF),
            jax.ShapeDtypeStruct((rows, cols), BF),
        ],
        compiler_params=params(),
        name="rays_query",
    )(pre, rays, gain.reshape(1, -1), shift.reshape(1, -1), wq)


def keyval_kernel(core, x, wk, wv, k, v, kt, vt):
    kk = dot(x[...], wk[...])
    vv = dot(x[...], wv[...])
    k[...] = kk.astype(BF)
    v[...] = vv.astype(BF)
    kt[...] = kk.T.astype(BF)
    vt[...] = vv.T.astype(BF)


def keyval_call(core, carried, wk, wv):
    rows, width = carried.shape
    cols = width // 2
    blk = 512
    return pl.pallas_call(
        keyval_kernel,
        grid_spec=pltpu.PrefetchScalarGridSpec(
            num_scalar_prefetch=1,
            grid=(rows // blk,),
            in_specs=[
                pl.BlockSpec((blk, width), lambda i, o: (i, 0)),
                pl.BlockSpec((width, cols), lambda i, o: (0, o[0])),
                pl.BlockSpec((width, cols), lambda i, o: (0, o[0])),
            ],
            out_specs=[
                pl.BlockSpec((blk, cols), lambda i, o: (i, 0)),
                pl.BlockSpec((blk, cols), lambda i, o: (i, 0)),
                pl.BlockSpec((cols, blk), lambda i, o: (0, i)),
                pl.BlockSpec((cols, blk), lambda i, o: (0, i)),
            ],
        ),
        out_shape=[
            jax.ShapeDtypeStruct((rows, cols), BF),
            jax.ShapeDtypeStruct((rows, cols), BF),
            jax.ShapeDtypeStruct((cols, rows), BF),
            jax.ShapeDtypeStruct((cols, rows), BF),
        ],
        compiler_params=params(),
        name="keys_values",
    )(core[None], carried, wk, wv)


def attend_kernel(qb, qn, k, vt, o, st, e, s0, s1, mx, *, tc):
    i = pl.program_id(0)
    tokens = k.shape[0]
    rb = qb.shape[0]
    sb = (s0, s1)

    def score_chunk(dst, q, h, c, m):
        r = slice(c * tc, (c + 1) * tc)
        s = dot(head_half(k[r, :], h), q[...], NT)
        dst[r, :] = s
        mc = jnp.max(s.reshape(tc // 8, 8, rb), axis=0)
        return mc if m is None else jnp.maximum(m, mc)

    @pl.when(i == 0)
    def _():
        m = None
        for c in range(tokens // tc):
            m = score_chunk(s0, qb, 0, c, m)
        mx[0:1, :] = jnp.max(m, axis=0, keepdims=True)

    mixed = []
    for h in (0, 1):
        m = mx[h : h + 1, :]
        mn = None
        ot = None
        l = None
        for c in range(tokens // tc):
            r = slice(c * tc, (c + 1) * tc)
            mn = score_chunk(sb[1 - h], qb if h == 0 else qn, 1 - h, c, mn)
            p = jnp.exp2(sb[h][r, :] - m)
            lc = jnp.sum(p.reshape(tc // 8, 8, rb), axis=0)
            l = lc if l is None else l + lc
            pb = p.astype(BF)
            e[h, r, :] = pb
            oc = dot(vt[h * HD : (h + 1) * HD, r], pb)
            ot = oc if ot is None else ot + oc
        mx[1 - h : 2 - h, :] = jnp.max(mn, axis=0, keepdims=True)
        l = jnp.sum(l, axis=0, keepdims=True)
        mixed.append(ot / l)
        st[h : h + 1, :] = m
        st[h + 2 : h + 3, :] = m + jnp.log2(l)
    o[...] = jnp.concatenate(mixed, 0).T.astype(BF)


def attend_call(q, k, vt, p, rb=256):
    rays = q.shape[0]
    tokens = k.shape[0]
    n = rays // rb
    return pl.pallas_call(
        functools.partial(attend_kernel, tc=min(1024, tokens)),
        grid=(n,),
        in_specs=[
            pl.BlockSpec((rb, PAIR), lambda i: (i, p)),
            pl.BlockSpec((rb, PAIR), lambda i: (jnp.minimum(i + 1, n - 1), p)),
            pl.BlockSpec((tokens, PAIR), lambda i: (0, p)),
            pl.BlockSpec((PAIR, tokens), lambda i: (p, 0)),
        ],
        out_specs=[
            pl.BlockSpec((rb, PAIR), lambda i: (i, 0)),
            pl.BlockSpec((8, rb), lambda i: (0, i)),
            pl.BlockSpec((2, tokens, rb), lambda i: (0, 0, i)),
        ],
        out_shape=[
            jax.ShapeDtypeStruct((rays, PAIR), BF),
            jax.ShapeDtypeStruct((8, rays), F32),
            jax.ShapeDtypeStruct((2, tokens, rays), BF),
        ],
        scratch_shapes=[
            pltpu.VMEM((tokens, rb), F32),
            pltpu.VMEM((tokens, rb), F32),
            pltpu.VMEM((8, rb), F32),
        ],
        compiler_params=params(),
        cost_estimate=pl.CostEstimate(
            flops=16 * rays * tokens * PAIR, bytes_accessed=4 * rays * tokens, transcendentals=0
        ),
        name=f"attend_{p}",
    )(q, q, k, vt)


def spread(rows2):
    rows = rows2.shape[1]
    return jnp.concatenate([jnp.broadcast_to(rows2[h : h + 1, :], (HD, rows)) for h in (0, 1)], 0)


def combine_kernel(*refs, parts):
    os, sts = refs[:parts], refs[parts : 2 * parts]
    att, low, lse = refs[2 * parts :]
    ls = [s[2:4, :] for s in sts]
    top = functools.reduce(jnp.maximum, ls)
    tot = top + jnp.log2(sum(jnp.exp2(x - top) for x in ls))
    acc = 0.0
    for o, x in zip(os, ls):
        acc = acc + o[...].astype(F32) * spread(jnp.exp2(x - tot)).T
    att[...] = acc
    low[...] = acc.astype(BF)
    lse[0:2, :] = tot


def combine_call(os, sts, rows):
    parts = len(os)
    blk = 512 if rows % 512 == 0 else rows
    return pl.pallas_call(
        functools.partial(combine_kernel, parts=parts),
        grid=(rows // blk,),
        in_specs=[pl.BlockSpec((blk, PAIR), lambda i: (i, 0))] * parts
        + [pl.BlockSpec((8, blk), lambda i: (0, i))] * parts,
        out_specs=[
            pl.BlockSpec((blk, PAIR), lambda i: (i, 0)),
            pl.BlockSpec((blk, PAIR), lambda i: (i, 0)),
            pl.BlockSpec((8, blk), lambda i: (0, i)),
        ],
        out_shape=[
            jax.ShapeDtypeStruct((rows, PAIR), F32),
            jax.ShapeDtypeStruct((rows, PAIR), BF),
            jax.ShapeDtypeStruct((8, rows), F32),
        ],
        compiler_params=params(),
        name="combine",
    )(*os, *sts)


def delta_kernel(do, a0, a1, a2, out):
    for p, a in enumerate((a0, a1, a2)):
        prod = (do[:, p * PAIR : (p + 1) * PAIR].astype(F32) * a[...]).T
        for h in (0, 1):
            out[2 * p + h : 2 * p + h + 1, :] = jnp.sum(
                prod[h * HD : (h + 1) * HD, :], axis=0, keepdims=True
            )


def delta_call(do, atts):
    rows = do.shape[0]
    return pl.pallas_call(
        delta_kernel,
        out_shape=jax.ShapeDtypeStruct((8, rows), F32),
        compiler_params=params(),
        name="deltas",
    )(do, *atts)


def backward_kernel(e, do, q, st, lse, dl, kt, v, *refs, p, first):
    if first:
        dq, dk, dv = refs
    else:
        dk0, dv0, dq, dk, dv = refs

    @pl.when(pl.program_id(0) == 0)
    def _():
        if first:
            dk[...] = jnp.zeros_like(dk)
            dv[...] = jnp.zeros_like(dv)
        else:
            dk[...] = dk0[...]
            dv[...] = dv0[...]

    sc = jnp.exp2(st[0:2, :] - lse[0:2, :])
    scw = spread(sc)
    sct = scw.T
    dos = (do[...].astype(F32) * sct).astype(BF)
    qs = (q[...].astype(F32) * (sct * LN2)).astype(BF)
    grads = []
    for h in (0, 1):
        dp = dot(head_half(v[...], h), do[...], NT)
        grads.append((e[h].astype(F32) * (dp - dl[2 * p + h : 2 * p + h + 1, :])).astype(BF))
    dqt = jnp.concatenate(
        [dot(kt[h * HD : (h + 1) * HD, :], grads[h]) for h in (0, 1)], 0
    )
    dq[...] = (dqt * (scw * HD**-0.5)).T.astype(BF)
    both = lambda a: jnp.concatenate([head_half(a, 0), head_half(a, 1)], 0)
    dv[...] += dot(jnp.concatenate([e[0], e[1]], 1), both(dos))
    dk[...] += dot(jnp.concatenate(grads, 1), both(qs))


def backward_call(e, do, q, st, lse, dl, kt, v, carry, p, first_row, rb=256):
    rows = do.shape[0]
    tokens = v.shape[0]
    rb = min(rb, rows)
    off = first_row // rb
    whole = pl.BlockSpec((tokens, PAIR), lambda i: (0, 0))
    return pl.pallas_call(
        functools.partial(backward_kernel, p=p, first=carry is None),
        grid=(rows // rb,),
        in_specs=[
            pl.BlockSpec((2, tokens, rb), lambda i: (0, 0, i + off)),
            pl.BlockSpec((rb, PAIR), lambda i: (i, p)),
            pl.BlockSpec((rb, PAIR), lambda i: (i + off, p)),
            pl.BlockSpec((8, rb), lambda i: (0, i + off)),
            pl.BlockSpec((8, rb), lambda i: (0, i)),
            pl.BlockSpec((8, rb), lambda i: (0, i)),
            pl.BlockSpec((PAIR, tokens), lambda i: (p, 0)),
            pl.BlockSpec((tokens, PAIR), lambda i: (0, p)),
        ]
        + ([] if carry is None else [whole, whole]),
        out_specs=[pl.BlockSpec((rb, PAIR), lambda i: (i, 0)), whole, whole],
        out_shape=[
            jax.ShapeDtypeStruct((rows, PAIR), BF),
            jax.ShapeDtypeStruct((tokens, PAIR), F32),
            jax.ShapeDtypeStruct((tokens, PAIR), F32),
        ],
        compiler_params=params(),
        cost_estimate=pl.CostEstimate(
            flops=32 * rows * tokens * PAIR, bytes_accessed=4 * rows * tokens, transcendentals=0
        ),
        name=f"backward_{p}_{'own' if carry is None else 'far'}",
    )(e, do, q, st, lse, dl, kt, v, *(() if carry is None else carry))


def local(
    ray_tokens,
    latents,
    group_ids,
    ln1_gain,
    ln1_shift,
    w_query,
    w_key,
    w_value,
    w_out,
    ln2_gain,
    ln2_shift,
    w_up,
    b_up,
    w_down,
    b_down,
    intrinsics,
    out_grad,
    *,
    keys,
):
    share = out_grad.shape[0]
    width = ray_tokens.shape[1]
    cols = width // 2
    pairs = cols // PAIR
    chips = keys // 2
    chip_rows = 2 * share
    place = lax.axis_index("key")
    core = place % 2
    chip = place // 2

    def core_swap(x):
        return lax.ppermute(x, "key", [(i, i ^ 1) for i in range(keys)])

    def chip_shift(x, s):
        return lax.ppermute(x, "key", [(i, (i + 2 * s) % keys) for i in range(keys)])

    def own_cols(w):
        return lax.dynamic_slice_in_dim(w, core * cols, cols, 1)

    def far_cols(w):
        return lax.dynamic_slice_in_dim(w, (1 - core) * cols, cols, 1)

    def own_rows(w):
        return lax.dynamic_slice_in_dim(w, core * cols, cols, 0)

    def far_rows(w):
        return lax.dynamic_slice_in_dim(w, (1 - core) * cols, cols, 0)

    gain_one = ln1_gain.astype(F32)
    shift_one = ln1_shift.astype(F32)
    gain_two = ln2_gain.astype(F32)
    shift_two = ln2_shift.astype(F32)
    lookup = group_ids[0][:, None] == jnp.arange(intrinsics.shape[0], dtype=jnp.int32)[None, :]
    carried = (
        latents[0].astype(F32)
        + jnp.dot(lookup.astype(BF), intrinsics, preferred_element_type=F32)
    ).astype(BF)
    tokens = carried.shape[0]
    chip_carried = jnp.concatenate([carried, core_swap(carried)], 0)
    steps = jnp.arange(keys, dtype=jnp.int32)
    order = ((chip + steps // 2) % chips) * 2 + (core + steps % 2) % 2
    normed, queries = query_call(order, core, ray_tokens, ln1_gain, ln1_shift, w_query, share)
    key_rows, value_rows, key_cols, value_cols = keyval_call(core, chip_carried, w_key, w_value)

    stats, exps, atts, lows, lses = [], [], [], [], []
    for p in range(pairs):
        o, st, e = attend_call(queries, key_rows, value_cols, p)
        stats.append(st)
        exps.append(e)
        os, sts = [o], [st]
        for s in range(1, chips):
            os.append(chip_shift(o[s * chip_rows : (s + 1) * chip_rows], s))
            sts.append(chip_shift(st[:, s * chip_rows : (s + 1) * chip_rows], s))
        att, low, lse = combine_call(os, sts, chip_rows)
        atts.append(att)
        lows.append(low)
        lses.append(lse)
    low_chip = jnp.concatenate(lows, 1)
    low_own = low_chip[:share]
    low_far = core_swap(low_chip[share:])
    attended_low = jnp.concatenate(
        [jnp.where(core == 0, low_own, low_far), jnp.where(core == 0, low_far, low_own)], 1
    )
    own_rays = lax.dynamic_slice_in_dim(ray_tokens, place * share, share, 0).astype(F32)
    middle = own_rays + dot(attended_low, w_out)
    normed_two, unit_two, scale_two = norm_forward(middle, gain_two, shift_two)
    normed_two_low = normed_two.astype(BF)
    hidden = dot(normed_two_low, w_up) + b_up.astype(F32)
    active, gelu_back = jax.vjp(jax.nn.gelu, hidden)
    active_low = active.astype(BF)
    output = (middle + dot(active_low, w_down) + b_down.astype(F32)).astype(BF)
    grad_out = out_grad.astype(F32)
    grad_active = lax.optimization_barrier(dot(out_grad, w_down, NT).astype(BF)).astype(F32)
    grad_hidden = gelu_back(grad_active)[0].astype(BF)
    grad_normed_two = dot(grad_hidden, w_up, NT)
    grad_middle_norm, grad_gain_two, grad_shift_two = norm_backward(
        grad_normed_two, unit_two, scale_two, gain_two
    )
    grad_middle = grad_out + grad_middle_norm
    grad_branch = grad_middle.astype(BF)
    do_far = core_swap(dot(grad_branch, far_rows(w_out), NT).astype(BF))
    do_own = dot(grad_branch, own_rows(w_out), NT).astype(BF)
    do_chip = jnp.concatenate([do_own, do_far], 0)
    deltas = delta_call(do_chip, atts)
    dos, dls, lss = [do_chip], [deltas], [lses]
    for t in range(1, chips):
        dos.append(chip_shift(do_chip, chips - t))
        dls.append(chip_shift(deltas, chips - t))
        lss.append([chip_shift(x, chips - t) for x in lses])
    grad_w_down = dot(active_low, out_grad, TN)
    grad_b_down = jnp.sum(grad_out, axis=0)
    grad_w_up = dot(normed_two_low, grad_hidden, TN)
    grad_b_up = jnp.sum(grad_hidden.astype(F32), axis=0)
    grad_w_out = dot(attended_low, grad_branch, TN)

    grad_q, grad_k, grad_v = [], [], []
    for p in range(pairs):
        carry = None
        parts = []
        for t in range(chips):
            dq, dk, dv = backward_call(
                exps[p],
                dos[t],
                queries,
                stats[p],
                lss[t][p],
                dls[t],
                key_cols,
                value_rows,
                carry,
                p,
                t * chip_rows,
            )
            carry = (dk, dv)
            parts.append(dq if t == 0 else chip_shift(dq, t))
        grad_q.append(sum(x.astype(F32) for x in parts).astype(BF))
        grad_k.append(carry[0].astype(BF))
        grad_v.append(carry[1].astype(BF))
    grad_queries = jnp.concatenate(grad_q, 1)
    grad_keys = jnp.concatenate(grad_k, 1)
    grad_values = jnp.concatenate(grad_v, 1)
    grad_w_query = dot(normed[:chip_rows], grad_queries, TN)
    grad_w_key = dot(chip_carried, grad_keys, TN)
    grad_w_value = dot(chip_carried, grad_values, TN)
    keys_far = core_swap(grad_keys[tokens:])
    values_far = core_swap(grad_values[tokens:])
    queries_far = core_swap(grad_queries[share:])
    grad_carried = (
        dot(grad_keys[:tokens], own_cols(w_key), NT)
        + dot(keys_far, far_cols(w_key), NT)
        + dot(grad_values[:tokens], own_cols(w_value), NT)
        + dot(values_far, far_cols(w_value), NT)
    )
    grad_normed = dot(grad_queries[:share], own_cols(w_query), NT) + dot(
        queries_far, far_cols(w_query), NT
    )
    _, unit_one, scale_one = norm_forward(own_rays, gain_one, shift_one)
    grad_rays_norm, grad_gain_one, grad_shift_one = norm_backward(
        grad_normed, unit_one, scale_one, gain_one
    )
    rays_grad = grad_middle + grad_rays_norm
    grad_table = jnp.dot(lookup.astype(F32).T, grad_carried, precision=HIGHEST)
    whole = jnp.zeros((width, width), F32)
    put = lambda g: lax.dynamic_update_slice_in_dim(whole, g, core * cols, 1)
    big = (put(grad_w_query), put(grad_w_key), put(grad_w_value), grad_w_out, grad_w_up, grad_w_down)
    small = (grad_gain_one, grad_shift_one, grad_gain_two, grad_shift_two, grad_b_up, grad_b_down, grad_table)
    big = [x.astype(F32) for x in lax.psum([x.astype(BF) for x in big], ("dp", "key"))]
    small = lax.psum(small, ("dp", "key"))
    return (
        output,
        rays_grad,
        grad_carried[None],
        small[0],
        small[1],
        big[0],
        big[1],
        big[2],
        big[3],
        small[2],
        small[3],
        big[4],
        small[4],
        big[5],
        small[5],
        small[6],
    )


def solution(mesh):
    rows = P(("dp", "key"), None)
    placed = (P("dp", None), P("dp", "key", None), P("dp", "key")) + (P(),) * 13 + (rows,)
    return jax.shard_map(
        functools.partial(local, keys=mesh.shape["key"]),
        mesh=mesh,
        in_specs=placed,
        out_specs=(rows, rows, P("dp", "key", None)) + (P(),) * 13,
        check_vma=False,
    )
```

```python
import functools

import jax
import jax.numpy as jnp
from jax import lax
from jax.experimental import pallas as pl
from jax.experimental.pallas import tpu as pltpu
from jax.sharding import PartitionSpec as P

H = 12
HD = 64
PAIR = 2 * HD
EPSILON = 1e-05
HIGHEST = lax.Precision.HIGHEST
BF = jnp.bfloat16
F32 = jnp.float32
LOG2E = 1.4426950408889634
LN2 = 0.6931471805599453
VMEM = 60 * 1024 * 1024


def dot(a, b, dims=((1,), (0,))):
    return lax.dot_general(a, b, (dims, ((), ())), preferred_element_type=F32)


NT = ((1,), (1,))
TN = ((0,), (0,))


def params(**kw):
    return pltpu.CompilerParams(vmem_limit_bytes=VMEM, **kw)


def head_half(x, h, axis=1):
    i = lax.broadcasted_iota(jnp.int32, x.shape, axis)
    return jnp.where((i < HD) == (h == 0), x, jnp.zeros_like(x))


def norm_forward(values, gain_vec, shift_vec):
    centre = values - jnp.mean(values, axis=-1, keepdims=True)
    scaled = lax.rsqrt(jnp.mean(centre * centre, axis=-1, keepdims=True) + EPSILON)
    unit_rows = centre * scaled
    return (unit_rows * gain_vec + shift_vec, unit_rows, scaled)


def norm_backward(grad_rows, unit_rows, scaled, gain_vec):
    grad_unit = grad_rows * gain_vec
    centred_grad = (
        grad_unit
        - jnp.mean(grad_unit, axis=-1, keepdims=True)
        - unit_rows * jnp.mean(grad_unit * unit_rows, axis=-1, keepdims=True)
    )
    return (
        scaled * centred_grad,
        jnp.sum(grad_rows * unit_rows, axis=0),
        jnp.sum(grad_rows, axis=0),
    )


def query_kernel(order, rays, gain, shift, wq, normed, q):
    n, _, _ = norm_forward(rays[...].astype(F32), gain[...].astype(F32), shift[...].astype(F32))
    n = n.astype(BF)
    normed[...] = n
    q[...] = (dot(n, wq[...]) * (HD**-0.5 * LOG2E)).astype(BF)


def query_call(order, core, rays, gain, shift, wq, share):
    rows, width = rays.shape
    cols = width // 2
    blocks = rows // share
    pre = jnp.concatenate([order, core[None]])
    return pl.pallas_call(
        query_kernel,
        grid_spec=pltpu.PrefetchScalarGridSpec(
            num_scalar_prefetch=1,
            grid=(blocks,),
            in_specs=[
                pl.BlockSpec((share, width), lambda i, o: (o[i], 0)),
                pl.BlockSpec((1, width), lambda i, o: (0, 0)),
                pl.BlockSpec((1, width), lambda i, o: (0, 0)),
                pl.BlockSpec((width, cols), lambda i, o: (0, o[blocks])),
            ],
            out_specs=[
                pl.BlockSpec((share, width), lambda i, o: (i, 0)),
                pl.BlockSpec((share, cols), lambda i, o: (i, 0)),
            ],
        ),
        out_shape=[
            jax.ShapeDtypeStruct((rows, width), BF),
            jax.ShapeDtypeStruct((rows, cols), BF),
        ],
        compiler_params=params(),
        name="rays_query",
    )(pre, rays, gain.reshape(1, -1), shift.reshape(1, -1), wq)


def keyval_kernel(core, x, wk, wv, k, v, kt, vt):
    kk = dot(x[...], wk[...])
    vv = dot(x[...], wv[...])
    k[...] = kk.astype(BF)
    v[...] = vv.astype(BF)
    kt[...] = kk.T.astype(BF)
    vt[...] = vv.T.astype(BF)


def keyval_call(core, carried, wk, wv):
    rows, width = carried.shape
    cols = width // 2
    blk = 512
    return pl.pallas_call(
        keyval_kernel,
        grid_spec=pltpu.PrefetchScalarGridSpec(
            num_scalar_prefetch=1,
            grid=(rows // blk,),
            in_specs=[
                pl.BlockSpec((blk, width), lambda i, o: (i, 0)),
                pl.BlockSpec((width, cols), lambda i, o: (0, o[0])),
                pl.BlockSpec((width, cols), lambda i, o: (0, o[0])),
            ],
            out_specs=[
                pl.BlockSpec((blk, cols), lambda i, o: (i, 0)),
                pl.BlockSpec((blk, cols), lambda i, o: (i, 0)),
                pl.BlockSpec((cols, blk), lambda i, o: (0, i)),
                pl.BlockSpec((cols, blk), lambda i, o: (0, i)),
            ],
        ),
        out_shape=[
            jax.ShapeDtypeStruct((rows, cols), BF),
            jax.ShapeDtypeStruct((rows, cols), BF),
            jax.ShapeDtypeStruct((cols, rows), BF),
            jax.ShapeDtypeStruct((cols, rows), BF),
        ],
        compiler_params=params(),
        name="keys_values",
    )(core[None], carried, wk, wv)


def attend_kernel(qb, qn, k, vt, o, st, e, s0, s1, mx, *, tc):
    i = pl.program_id(0)
    tokens = k.shape[0]
    rb = qb.shape[0]
    sb = (s0, s1)

    def score_chunk(dst, q, h, c, m):
        r = slice(c * tc, (c + 1) * tc)
        s = dot(head_half(k[r, :], h), q[...], NT)
        dst[r, :] = s
        mc = jnp.max(s.reshape(tc // 8, 8, rb), axis=0)
        return mc if m is None else jnp.maximum(m, mc)

    @pl.when(i == 0)
    def _():
        m = None
        for c in range(tokens // tc):
            m = score_chunk(s0, qb, 0, c, m)
        mx[0:1, :] = jnp.max(m, axis=0, keepdims=True)

    mixed = []
    for h in (0, 1):
        m = mx[h : h + 1, :]
        mn = None
        ot = None
        l = None
        for c in range(tokens // tc):
            r = slice(c * tc, (c + 1) * tc)
            mn = score_chunk(sb[1 - h], qb if h == 0 else qn, 1 - h, c, mn)
            p = jnp.exp2(sb[h][r, :] - m)
            lc = jnp.sum(p.reshape(tc // 8, 8, rb), axis=0)
            l = lc if l is None else l + lc
            pb = p.astype(BF)
            e[h, r, :] = pb
            oc = dot(vt[h * HD : (h + 1) * HD, r], pb)
            ot = oc if ot is None else ot + oc
        mx[1 - h : 2 - h, :] = jnp.max(mn, axis=0, keepdims=True)
        l = jnp.sum(l, axis=0, keepdims=True)
        mixed.append(ot / l)
        st[h : h + 1, :] = m
        st[h + 2 : h + 3, :] = m + jnp.log2(l)
    o[...] = jnp.concatenate(mixed, 0).T.astype(BF)


def attend_call(q, k, vt, p, rb=256):
    rays = q.shape[0]
    tokens = k.shape[0]
    n = rays // rb
    return pl.pallas_call(
        functools.partial(attend_kernel, tc=min(1024, tokens)),
        grid=(n,),
        in_specs=[
            pl.BlockSpec((rb, PAIR), lambda i: (i, p)),
            pl.BlockSpec((rb, PAIR), lambda i: (jnp.minimum(i + 1, n - 1), p)),
            pl.BlockSpec((tokens, PAIR), lambda i: (0, p)),
            pl.BlockSpec((PAIR, tokens), lambda i: (p, 0)),
        ],
        out_specs=[
            pl.BlockSpec((rb, PAIR), lambda i: (i, 0)),
            pl.BlockSpec((8, rb), lambda i: (0, i)),
            pl.BlockSpec((2, tokens, rb), lambda i: (0, 0, i)),
        ],
        out_shape=[
            jax.ShapeDtypeStruct((rays, PAIR), BF),
            jax.ShapeDtypeStruct((8, rays), F32),
            jax.ShapeDtypeStruct((2, tokens, rays), BF),
        ],
        scratch_shapes=[
            pltpu.VMEM((tokens, rb), F32),
            pltpu.VMEM((tokens, rb), F32),
            pltpu.VMEM((8, rb), F32),
        ],
        compiler_params=params(),
        cost_estimate=pl.CostEstimate(
            flops=rays * tokens * PAIR, bytes_accessed=rays * tokens, transcendentals=0
        ),
        name=f"attend_{p}",
    )(q, q, k, vt)


def spread(rows2):
    rows = rows2.shape[1]
    return jnp.concatenate([jnp.broadcast_to(rows2[h : h + 1, :], (HD, rows)) for h in (0, 1)], 0)


def combine_kernel(*refs, parts):
    os, sts = refs[:parts], refs[parts : 2 * parts]
    att, low, lse = refs[2 * parts :]
    ls = [s[2:4, :] for s in sts]
    top = functools.reduce(jnp.maximum, ls)
    tot = top + jnp.log2(sum(jnp.exp2(x - top) for x in ls))
    acc = 0.0
    for o, x in zip(os, ls):
        acc = acc + o[...].astype(F32) * spread(jnp.exp2(x - tot)).T
    att[...] = acc
    low[...] = acc.astype(BF)
    lse[0:2, :] = tot


def combine_call(os, sts, rows):
    parts = len(os)
    blk = 512 if rows % 512 == 0 else rows
    return pl.pallas_call(
        functools.partial(combine_kernel, parts=parts),
        grid=(rows // blk,),
        in_specs=[pl.BlockSpec((blk, PAIR), lambda i: (i, 0))] * parts
        + [pl.BlockSpec((8, blk), lambda i: (0, i))] * parts,
        out_specs=[
            pl.BlockSpec((blk, PAIR), lambda i: (i, 0)),
            pl.BlockSpec((blk, PAIR), lambda i: (i, 0)),
            pl.BlockSpec((8, blk), lambda i: (0, i)),
        ],
        out_shape=[
            jax.ShapeDtypeStruct((rows, PAIR), F32),
            jax.ShapeDtypeStruct((rows, PAIR), BF),
            jax.ShapeDtypeStruct((8, rows), F32),
        ],
        compiler_params=params(),
        name="combine",
    )(*os, *sts)


def delta_kernel(do, a0, a1, a2, out):
    for p, a in enumerate((a0, a1, a2)):
        prod = (do[:, p * PAIR : (p + 1) * PAIR].astype(F32) * a[...]).T
        for h in (0, 1):
            out[2 * p + h : 2 * p + h + 1, :] = jnp.sum(
                prod[h * HD : (h + 1) * HD, :], axis=0, keepdims=True
            )


def delta_call(do, atts):
    rows = do.shape[0]
    return pl.pallas_call(
        delta_kernel,
        out_shape=jax.ShapeDtypeStruct((8, rows), F32),
        compiler_params=params(),
        name="deltas",
    )(do, *atts)


def backward_kernel(e, do, q, st, lse, dl, kt, v, *refs, p, first):
    if first:
        dq, dk, dv = refs
    else:
        dk0, dv0, dq, dk, dv = refs

    @pl.when(pl.program_id(0) == 0)
    def _():
        if first:
            dk[...] = jnp.zeros_like(dk)
            dv[...] = jnp.zeros_like(dv)
        else:
            dk[...] = dk0[...]
            dv[...] = dv0[...]

    sc = jnp.exp2(st[0:2, :] - lse[0:2, :])
    scw = spread(sc)
    sct = scw.T
    dos = (do[...].astype(F32) * sct).astype(BF)
    qs = (q[...].astype(F32) * (sct * LN2)).astype(BF)
    grads = []
    for h in (0, 1):
        dp = dot(head_half(v[...], h), do[...], NT)
        grads.append((e[h].astype(F32) * (dp - dl[2 * p + h : 2 * p + h + 1, :])).astype(BF))
    dqt = jnp.concatenate(
        [dot(kt[h * HD : (h + 1) * HD, :], grads[h]) for h in (0, 1)], 0
    )
    dq[...] = (dqt * (scw * HD**-0.5)).T.astype(BF)
    both = lambda a: jnp.concatenate([head_half(a, 0), head_half(a, 1)], 0)
    dv[...] += dot(jnp.concatenate([e[0], e[1]], 1), both(dos))
    dk[...] += dot(jnp.concatenate(grads, 1), both(qs))


def backward_call(e, do, q, st, lse, dl, kt, v, carry, p, first_row, rb=256):
    rows = do.shape[0]
    tokens = v.shape[0]
    rb = min(rb, rows)
    off = first_row // rb
    whole = pl.BlockSpec((tokens, PAIR), lambda i: (0, 0))
    return pl.pallas_call(
        functools.partial(backward_kernel, p=p, first=carry is None),
        grid=(rows // rb,),
        in_specs=[
            pl.BlockSpec((2, tokens, rb), lambda i: (0, 0, i + off)),
            pl.BlockSpec((rb, PAIR), lambda i: (i, p)),
            pl.BlockSpec((rb, PAIR), lambda i: (i + off, p)),
            pl.BlockSpec((8, rb), lambda i: (0, i + off)),
            pl.BlockSpec((8, rb), lambda i: (0, i)),
            pl.BlockSpec((8, rb), lambda i: (0, i)),
            pl.BlockSpec((PAIR, tokens), lambda i: (p, 0)),
            pl.BlockSpec((tokens, PAIR), lambda i: (0, p)),
        ]
        + ([] if carry is None else [whole, whole]),
        out_specs=[pl.BlockSpec((rb, PAIR), lambda i: (i, 0)), whole, whole],
        out_shape=[
            jax.ShapeDtypeStruct((rows, PAIR), BF),
            jax.ShapeDtypeStruct((tokens, PAIR), F32),
            jax.ShapeDtypeStruct((tokens, PAIR), F32),
        ],
        compiler_params=params(),
        cost_estimate=pl.CostEstimate(
            flops=2 * rows * tokens * PAIR, bytes_accessed=rows * tokens, transcendentals=0
        ),
        name=f"backward_{p}_{'own' if carry is None else 'far'}",
    )(e, do, q, st, lse, dl, kt, v, *(() if carry is None else carry))


def fold_kernel(bits, *refs, modes):
    n = len(modes)
    keeps, recvs, outs = refs[:n], refs[n : 2 * n], list(refs[2 * n :])
    for i, mode in enumerate(modes):
        if mode:
            send, keep = outs.pop(0), outs.pop(0)
            half = send.shape[0]
            for dst, b in ((send, 1 - bits[i]), (keep, bits[i])):
                r = pl.ds(pl.multiple_of(b * half, 16), half)
                dst[...] = (keeps[i][r, :].astype(F32) + recvs[i][r, :].astype(F32)).astype(dst.dtype)
        else:
            dst = outs.pop(0)
            dst[...] = (keeps[i][...].astype(F32) + recvs[i][...].astype(F32)).astype(dst.dtype)


def fold_call(bits, keeps, recvs, modes):
    shapes = []
    for x, mode in zip(keeps, modes):
        if mode:
            shapes += [jax.ShapeDtypeStruct((x.shape[0] // 2,) + x.shape[1:], x.dtype)] * 2
        else:
            shapes.append(jax.ShapeDtypeStruct(x.shape, x.dtype))
    whole = pl.BlockSpec(memory_space=pltpu.VMEM)
    out = pl.pallas_call(
        functools.partial(fold_kernel, modes=tuple(modes)),
        in_specs=[pl.BlockSpec(memory_space=pltpu.SMEM)] + [whole] * (2 * len(keeps)),
        out_specs=[whole] * len(shapes),
        out_shape=shapes,
        compiler_params=params(),
        name="fold",
    )(bits, *keeps, *recvs)
    out = list(out)
    return [((out.pop(0), out.pop(0)) if mode else (out[0], out.pop(0))) for mode in modes]


def join_kernel(bits, *refs, n):
    mines, recvs, outs = refs[:n], refs[n : 2 * n], refs[2 * n :]
    for i in range(n):
        half = mines[i].shape[0]
        outs[i][pl.ds(pl.multiple_of(bits[i] * half, 16), half), :] = mines[i][...]
        outs[i][pl.ds(pl.multiple_of((1 - bits[i]) * half, 16), half), :] = recvs[i][...]


def join_call(bits, mines, recvs):
    whole = pl.BlockSpec(memory_space=pltpu.VMEM)
    return pl.pallas_call(
        functools.partial(join_kernel, n=len(mines)),
        in_specs=[pl.BlockSpec(memory_space=pltpu.SMEM)] + [whole] * (2 * len(mines)),
        out_specs=[whole] * len(mines),
        out_shape=[jax.ShapeDtypeStruct((2 * x.shape[0],) + x.shape[1:], x.dtype) for x in mines],
        compiler_params=params(),
        name="join",
    )(bits, *mines, *recvs)


def pair_swap(x, step, sizes):
    axis, mask = step
    return lax.ppermute(x, axis, [(i, i ^ mask) for i in range(sizes[axis])])


def step_bit(step):
    axis, mask = step
    return (lax.axis_index(axis) // mask) % 2


def chip_steps(sizes):
    along = [("dp", 1 << j) for j in range(sizes["dp"].bit_length() - 1)]
    across = [("key", 2 << j) for j in range(sizes["key"].bit_length() - 2)]
    return along[:1] + across[:1] + along[1:2], along[2:] + across[1:]


def turn(first, i):
    i = i % len(first)
    return first[i:] + first[:i]


def tree_sum(parts, first_halved, steps, sizes):
    n = len(parts)
    halved = [[h] for h in first_halved]
    count = len(steps[0])
    for j in range(count):
        recvs = [pair_swap(parts[i][0], steps[i][j], sizes) for i in range(n)]
        keeps = [parts[i][1] for i in range(n)]
        if j + 1 < count:
            modes = [keeps[i].shape[0] % 32 == 0 and keeps[i].dtype == BF for i in range(n)]
            bits = jnp.stack([step_bit(steps[i][j + 1]) for i in range(n)])
        else:
            modes = [False] * n
            bits = jnp.zeros((n,), jnp.int32)
        parts = fold_call(bits, keeps, recvs, modes)
        for i in range(n):
            halved[i].append(modes[i])
    mines = [x[1] for x in parts]
    for j in reversed(range(count)):
        live = [i for i in range(n) if halved[i][j]]
        if not live:
            continue
        recvs = [pair_swap(mines[i], steps[i][j], sizes) for i in live]
        bits = jnp.stack([step_bit(steps[i][j]) for i in live])
        for i, x in zip(live, join_call(bits, [mines[i] for i in live], recvs)):
            mines[i] = x
    return mines


def local(
    ray_tokens,
    latents,
    group_ids,
    ln1_gain,
    ln1_shift,
    w_query,
    w_key,
    w_value,
    w_out,
    ln2_gain,
    ln2_shift,
    w_up,
    b_up,
    w_down,
    b_down,
    intrinsics,
    out_grad,
    *,
    sizes,
):
    keys = sizes["key"]
    share = out_grad.shape[0]
    width = ray_tokens.shape[1]
    cols = width // 2
    pairs = cols // PAIR
    chips = keys // 2
    chip_rows = 2 * share
    place = lax.axis_index("key")
    core = place % 2
    chip = place // 2

    def core_swap(x):
        return lax.ppermute(x, "key", [(i, i ^ 1) for i in range(keys)])

    def chip_shift(x, s):
        return lax.ppermute(x, "key", [(i, (i + 2 * s) % keys) for i in range(keys)])

    def own_cols(w):
        return lax.dynamic_slice_in_dim(w, core * cols, cols, 1)

    def far_cols(w):
        return lax.dynamic_slice_in_dim(w, (1 - core) * cols, cols, 1)

    def own_rows(w):
        return lax.dynamic_slice_in_dim(w, core * cols, cols, 0)

    def far_rows(w):
        return lax.dynamic_slice_in_dim(w, (1 - core) * cols, cols, 0)

    gain_one = ln1_gain.astype(F32)
    shift_one = ln1_shift.astype(F32)
    gain_two = ln2_gain.astype(F32)
    shift_two = ln2_shift.astype(F32)
    lookup = group_ids[0][:, None] == jnp.arange(intrinsics.shape[0], dtype=jnp.int32)[None, :]
    carried = (
        latents[0].astype(F32)
        + jnp.dot(lookup.astype(BF), intrinsics, preferred_element_type=F32)
    ).astype(BF)
    tokens = carried.shape[0]
    chip_carried = jnp.concatenate([carried, core_swap(carried)], 0)
    steps = jnp.arange(keys, dtype=jnp.int32)
    order = ((chip + steps // 2) % chips) * 2 + (core + steps % 2) % 2
    normed, queries = query_call(order, core, ray_tokens, ln1_gain, ln1_shift, w_query, share)
    key_rows, value_rows, key_cols, value_cols = keyval_call(core, chip_carried, w_key, w_value)

    stats, exps, atts, lows, lses = [], [], [], [], []
    for p in range(pairs):
        o, st, e = attend_call(queries, key_rows, value_cols, p)
        stats.append(st)
        exps.append(e)
        os, sts = [o], [st]
        for s in range(1, chips):
            os.append(chip_shift(o[s * chip_rows : (s + 1) * chip_rows], s))
            sts.append(chip_shift(st[:, s * chip_rows : (s + 1) * chip_rows], s))
        att, low, lse = combine_call(os, sts, chip_rows)
        atts.append(att)
        lows.append(low)
        lses.append(lse)
    low_chip = jnp.concatenate(lows, 1)
    low_own = low_chip[:share]
    low_far = core_swap(low_chip[share:])
    attended_low = jnp.concatenate(
        [jnp.where(core == 0, low_own, low_far), jnp.where(core == 0, low_far, low_own)], 1
    )
    own_rays = lax.dynamic_slice_in_dim(ray_tokens, place * share, share, 0).astype(F32)
    middle = own_rays + dot(attended_low, w_out)
    normed_two, unit_two, scale_two = norm_forward(middle, gain_two, shift_two)
    normed_two_low = normed_two.astype(BF)
    hidden = dot(normed_two_low, w_up) + b_up.astype(F32)
    active, gelu_back = jax.vjp(jax.nn.gelu, hidden)
    active_low = active.astype(BF)
    output = (middle + dot(active_low, w_down) + b_down.astype(F32)).astype(BF)
    grad_out = out_grad.astype(F32)
    grad_active = lax.optimization_barrier(dot(out_grad, w_down, NT).astype(BF)).astype(F32)
    grad_hidden = gelu_back(grad_active)[0].astype(BF)
    grad_normed_two = dot(grad_hidden, w_up, NT)
    grad_middle_norm, grad_gain_two, grad_shift_two = norm_backward(
        grad_normed_two, unit_two, scale_two, gain_two
    )
    grad_middle = grad_out + grad_middle_norm
    grad_branch = grad_middle.astype(BF)
    do_far = core_swap(dot(grad_branch, far_rows(w_out), NT).astype(BF))
    do_own = dot(grad_branch, own_rows(w_out), NT).astype(BF)
    do_chip = jnp.concatenate([do_own, do_far], 0)
    deltas = delta_call(do_chip, atts)
    dos, dls, lss = [do_chip], [deltas], [lses]
    for t in range(1, chips):
        dos.append(chip_shift(do_chip, chips - t))
        dls.append(chip_shift(deltas, chips - t))
        lss.append([chip_shift(x, chips - t) for x in lses])
    grad_w_down = dot(active_low, out_grad, TN)
    grad_b_down = jnp.sum(grad_out, axis=0)
    grad_w_up = dot(normed_two_low, grad_hidden, TN)
    grad_b_up = jnp.sum(grad_hidden.astype(F32), axis=0)
    grad_w_out = dot(attended_low, grad_branch, TN)

    grad_q, grad_k, grad_v = [], [], []
    for p in range(pairs):
        carry = None
        parts = []
        for t in range(chips):
            dq, dk, dv = backward_call(
                exps[p],
                dos[t],
                queries,
                stats[p],
                lss[t][p],
                dls[t],
                key_cols,
                value_rows,
                carry,
                p,
                t * chip_rows,
            )
            carry = (dk, dv)
            parts.append(dq if t == 0 else chip_shift(dq, t))
        grad_q.append(sum(x.astype(F32) for x in parts).astype(BF))
        grad_k.append(carry[0].astype(BF))
        grad_v.append(carry[1].astype(BF))
    grad_queries = jnp.concatenate(grad_q, 1)
    grad_keys = jnp.concatenate(grad_k, 1)
    grad_values = jnp.concatenate(grad_v, 1)
    grad_w_query = dot(normed[:chip_rows], grad_queries, TN)
    grad_w_key = dot(chip_carried, grad_keys, TN)
    grad_w_value = dot(chip_carried, grad_values, TN)
    keys_far = core_swap(grad_keys[tokens:])
    values_far = core_swap(grad_values[tokens:])
    queries_far = core_swap(grad_queries[share:])
    grad_carried = (
        dot(grad_keys[:tokens], own_cols(w_key), NT)
        + dot(keys_far, far_cols(w_key), NT)
        + dot(grad_values[:tokens], own_cols(w_value), NT)
        + dot(values_far, far_cols(w_value), NT)
    )
    grad_normed = dot(grad_queries[:share], own_cols(w_query), NT) + dot(
        queries_far, far_cols(w_query), NT
    )
    _, unit_one, scale_one = norm_forward(own_rays, gain_one, shift_one)
    grad_rays_norm, grad_gain_one, grad_shift_one = norm_backward(
        grad_normed, unit_one, scale_one, gain_one
    )
    rays_grad = grad_middle + grad_rays_norm
    grad_table = jnp.dot(lookup.astype(F32).T, grad_carried, precision=HIGHEST)
    first, rest = chip_steps(sizes)
    steps = [turn(first, i) + rest for i in range(4)]
    parts = []
    for g, s in zip((grad_w_query, grad_w_key, grad_w_value), steps):
        half = g.shape[0] // 2
        b = step_bit(s[0])
        parts.append(
            [
                lax.dynamic_slice_in_dim(g.astype(BF), k * half, half, 0)
                for k in (1 - b, b)
            ]
        )
    vectors = (
        grad_gain_one,
        grad_shift_one,
        grad_gain_two,
        grad_shift_two,
        grad_b_up,
        grad_b_down,
        grad_table,
    )
    small = jnp.concatenate([x.reshape(-1, width) for x in vectors], 0)
    small = jnp.pad(small, ((0, -small.shape[0] % 8), (0, 0)))
    small = small + core_swap(small)
    parts.append([small, small])
    sums = tree_sum(parts, [True] * 3 + [False], steps, sizes)
    attention_grads = []
    for g in sums[:3]:
        far = core_swap(g)
        attention_grads.append(
            jnp.concatenate(
                [jnp.where(core == 0, g, far), jnp.where(core == 0, far, g)], 1
            ).astype(F32)
        )
    small = sums[3]
    spots = []
    at = 0
    for x in vectors:
        n = x.size // width
        spots.append(small[at : at + n].reshape(x.shape))
        at += n
    branch_grads = [
        x.astype(F32)
        for x in lax.psum([x.astype(BF) for x in (grad_w_out, grad_w_up, grad_w_down)], ("dp", "key"))
    ]
    return (
        output,
        rays_grad,
        grad_carried[None],
        spots[0],
        spots[1],
        attention_grads[0],
        attention_grads[1],
        attention_grads[2],
        branch_grads[0],
        spots[2],
        spots[3],
        branch_grads[1],
        spots[4],
        branch_grads[2],
        spots[5],
        spots[6],
    )


def solution(mesh):
    rows = P(("dp", "key"), None)
    placed = (P("dp", None), P("dp", "key", None), P("dp", "key")) + (P(),) * 13 + (rows,)
    return jax.shard_map(
        functools.partial(local, sizes=dict(mesh.shape)),
        mesh=mesh,
        in_specs=placed,
        out_specs=(rows, rows, P("dp", "key", None)) + (P(),) * 13,
        check_vma=False,
    )
```

```python
import functools

import jax
import jax.numpy as jnp
from jax import lax
from jax.experimental import pallas as pl
from jax.experimental.pallas import tpu as pltpu
from jax.sharding import PartitionSpec as P

H = 12
HD = 64
PAIR = 2 * HD
EPSILON = 1e-05
HIGHEST = lax.Precision.HIGHEST
BF = jnp.bfloat16
F32 = jnp.float32
LOG2E = 1.4426950408889634
LN2 = 0.6931471805599453
SAFE_BOUND = 60.0
VMEM = 60 * 1024 * 1024


def dot(a, b, dims=((1,), (0,))):
    return lax.dot_general(a, b, (dims, ((), ())), preferred_element_type=F32)


NT = ((1,), (1,))
TN = ((0,), (0,))


def params(**kw):
    return pltpu.CompilerParams(vmem_limit_bytes=VMEM, **kw)


def head_half(x, h, axis=1):
    i = lax.broadcasted_iota(jnp.int32, x.shape, axis)
    return jnp.where((i < HD) == (h == 0), x, jnp.zeros_like(x))


def norm_forward(values, gain_vec, shift_vec):
    centre = values - jnp.mean(values, axis=-1, keepdims=True)
    scaled = lax.rsqrt(jnp.mean(centre * centre, axis=-1, keepdims=True) + EPSILON)
    unit_rows = centre * scaled
    return (unit_rows * gain_vec + shift_vec, unit_rows, scaled)


def norm_backward(grad_rows, unit_rows, scaled, gain_vec):
    grad_unit = grad_rows * gain_vec
    centred_grad = (
        grad_unit
        - jnp.mean(grad_unit, axis=-1, keepdims=True)
        - unit_rows * jnp.mean(grad_unit * unit_rows, axis=-1, keepdims=True)
    )
    return (
        scaled * centred_grad,
        jnp.sum(grad_rows * unit_rows, axis=0),
        jnp.sum(grad_rows, axis=0),
    )


def query_kernel(order, rays, gain, shift, wq, normed, q):
    n, _, _ = norm_forward(rays[...].astype(F32), gain[...].astype(F32), shift[...].astype(F32))
    n = n.astype(BF)
    normed[...] = n
    q[...] = (dot(n, wq[...]) * (HD**-0.5 * LOG2E)).astype(BF)


def query_call(order, core, rays, gain, shift, wq, share):
    rows, width = rays.shape
    cols = width // 2
    blocks = rows // share
    pre = jnp.concatenate([order, core[None]])
    return pl.pallas_call(
        query_kernel,
        grid_spec=pltpu.PrefetchScalarGridSpec(
            num_scalar_prefetch=1,
            grid=(blocks,),
            in_specs=[
                pl.BlockSpec((share, width), lambda i, o: (o[i], 0)),
                pl.BlockSpec((1, width), lambda i, o: (0, 0)),
                pl.BlockSpec((1, width), lambda i, o: (0, 0)),
                pl.BlockSpec((width, cols), lambda i, o: (0, o[blocks])),
            ],
            out_specs=[
                pl.BlockSpec((share, width), lambda i, o: (i, 0)),
                pl.BlockSpec((share, cols), lambda i, o: (i, 0)),
            ],
        ),
        out_shape=[
            jax.ShapeDtypeStruct((rows, width), BF),
            jax.ShapeDtypeStruct((rows, cols), BF),
        ],
        compiler_params=params(),
        name="rays_query",
    )(pre, rays, gain.reshape(1, -1), shift.reshape(1, -1), wq)


def keyval_kernel(core, x, wk, wv, k, v, kt, vt):
    kk = dot(x[...], wk[...])
    vv = dot(x[...], wv[...])
    k[...] = kk.astype(BF)
    v[...] = vv.astype(BF)
    kt[...] = kk.T.astype(BF)
    vt[...] = vv.T.astype(BF)


def keyval_call(core, carried, wk, wv):
    rows, width = carried.shape
    cols = width // 2
    blk = 512
    return pl.pallas_call(
        keyval_kernel,
        grid_spec=pltpu.PrefetchScalarGridSpec(
            num_scalar_prefetch=1,
            grid=(rows // blk,),
            in_specs=[
                pl.BlockSpec((blk, width), lambda i, o: (i, 0)),
                pl.BlockSpec((width, cols), lambda i, o: (0, o[0])),
                pl.BlockSpec((width, cols), lambda i, o: (0, o[0])),
            ],
            out_specs=[
                pl.BlockSpec((blk, cols), lambda i, o: (i, 0)),
                pl.BlockSpec((blk, cols), lambda i, o: (i, 0)),
                pl.BlockSpec((cols, blk), lambda i, o: (0, i)),
                pl.BlockSpec((cols, blk), lambda i, o: (0, i)),
            ],
        ),
        out_shape=[
            jax.ShapeDtypeStruct((rows, cols), BF),
            jax.ShapeDtypeStruct((rows, cols), BF),
            jax.ShapeDtypeStruct((cols, rows), BF),
            jax.ShapeDtypeStruct((cols, rows), BF),
        ],
        compiler_params=params(),
        name="keys_values",
    )(core[None], carried, wk, wv)


def attend_kernel(qb, k, vt, o, st, e, km, kn, spare, *, tc):
    tokens = k.shape[0]
    rb = qb.shape[0]
    chunks = [slice(c, c + tc) for c in range(0, tokens, tc)]

    @pl.when(pl.program_id(1) == 0)
    def _():
        for h in (0, 1):
            kh = head_half(k[...], h)
            km[h] = kh
            kf = kh.astype(F32)
            top = jnp.max(jnp.sum(kf * kf, axis=1, keepdims=True), axis=0, keepdims=True)
            kn[h : h + 1, :] = jnp.broadcast_to(top, (1, PAIR))

    qf = qb[...].astype(F32)
    bound = jnp.float32(0)
    for h in (0, 1):
        qn = jnp.max(jnp.sum(head_half(qf * qf, h), axis=1, keepdims=True), axis=0, keepdims=True)
        bound = jnp.maximum(bound, jnp.max(qn * kn[h : h + 1, :]))
    small = bound < SAFE_BOUND * SAFE_BOUND

    def scores(h, r):
        return dot(km[h, r, :], qb[...], NT)

    def mixed(h, r, low):
        cols = jnp.concatenate([vt[h * HD : (h + 1) * HD, r], jnp.ones((HD, tc), BF)], 0)
        return dot(cols, low)

    def finish(acc, shifts):
        outs = []
        for h in (0, 1):
            total = acc[h][HD : HD + 1]
            outs.append(acc[h][:HD] / total)
            st[h : h + 1, :] = shifts[h]
            st[h + 2 : h + 3, :] = shifts[h] + jnp.log2(total)
        o[...] = jnp.concatenate(outs, 0).T.astype(BF)

    @pl.when(small)
    def _():
        items = [(h, r) for h in (0, 1) for r in chunks]
        acc = [0.0, 0.0]
        ready = [scores(*items[0])]
        waiting = []
        for n, (h, r) in enumerate(items):
            if n + 1 < len(items):
                ready.append(scores(*items[n + 1]))
            low = jnp.exp2(ready.pop(0)).astype(BF)
            e[h, r, :] = low
            if waiting:
                g, *rest = waiting.pop()
                acc[g] = acc[g] + mixed(g, *rest)
            waiting.append((h, r, low))
        g, *rest = waiting.pop()
        acc[g] = acc[g] + mixed(g, *rest)
        finish(acc, [jnp.zeros((1, rb), F32)] * 2)

    @pl.when(jnp.logical_not(small))
    def _():
        acc = [0.0, 0.0]
        shifts = []
        for h in (0, 1):
            m = None
            for r in chunks:
                s = scores(h, r)
                spare[r, :] = s
                mc = jnp.max(s, axis=0, keepdims=True)
                m = mc if m is None else jnp.maximum(m, mc)
            shifts.append(m)
            for r in chunks:
                low = jnp.exp2(spare[r, :] - m).astype(BF)
                e[h, r, :] = low
                acc[h] = acc[h] + mixed(h, r, low)
        finish(acc, shifts)


def attend_call(q, k, vt, first_row, rows, name):
    tokens, cols = k.shape
    pairs = cols // PAIR
    rb = min(512, rows)
    off = first_row // rb
    return pl.pallas_call(
        functools.partial(attend_kernel, tc=min(1024, tokens)),
        grid=(pairs, rows // rb),
        in_specs=[
            pl.BlockSpec((rb, PAIR), lambda p, i: (i + off, p)),
            pl.BlockSpec((tokens, PAIR), lambda p, i: (0, p)),
            pl.BlockSpec((PAIR, tokens), lambda p, i: (p, 0)),
        ],
        out_specs=[
            pl.BlockSpec((rb, PAIR), lambda p, i: (i, p)),
            pl.BlockSpec((8, rb), lambda p, i: (p, i)),
            pl.BlockSpec((2, tokens, rb), lambda p, i: (p, 0, i)),
        ],
        out_shape=[
            jax.ShapeDtypeStruct((rows, cols), BF),
            jax.ShapeDtypeStruct((8 * pairs, rows), F32),
            jax.ShapeDtypeStruct((2 * pairs, tokens, rows), BF),
        ],
        scratch_shapes=[
            pltpu.VMEM((2, tokens, PAIR), BF),
            pltpu.VMEM((8, PAIR), F32),
            pltpu.VMEM((tokens, rb), F32),
        ],
        compiler_params=params(),
        cost_estimate=pl.CostEstimate(
            flops=rows * tokens * cols, bytes_accessed=rows * tokens, transcendentals=0
        ),
        name=f"attend_{name}",
    )(q, k, vt)


def spread(rows2):
    rows = rows2.shape[1]
    return jnp.concatenate([jnp.broadcast_to(rows2[h : h + 1, :], (HD, rows)) for h in (0, 1)], 0)


def combine_kernel(*refs, parts, pairs):
    os, sts = refs[:parts], refs[parts : 2 * parts]
    att, low, lse = refs[2 * parts :]
    for p in range(pairs):
        c = slice(p * PAIR, (p + 1) * PAIR)
        ls = [s[8 * p + 2 : 8 * p + 4, :] for s in sts]
        top = functools.reduce(jnp.maximum, ls)
        tot = top + jnp.log2(sum(jnp.exp2(x - top) for x in ls))
        acc = 0.0
        for o, x in zip(os, ls):
            acc = acc + o[:, c].astype(F32) * spread(jnp.exp2(x - tot)).T
        att[:, c] = acc
        low[:, c] = acc.astype(BF)
        lse[8 * p : 8 * p + 2, :] = tot


def combine_call(os, sts):
    parts = len(os)
    rows, cols = os[0].shape
    pairs = cols // PAIR
    blk = min(256, rows)
    wide = pl.BlockSpec((blk, cols), lambda i: (i, 0))
    flat = pl.BlockSpec((8 * pairs, blk), lambda i: (0, i))
    return pl.pallas_call(
        functools.partial(combine_kernel, parts=parts, pairs=pairs),
        grid=(rows // blk,),
        in_specs=[wide] * parts + [flat] * parts,
        out_specs=[wide, wide, flat],
        out_shape=[
            jax.ShapeDtypeStruct((rows, cols), F32),
            jax.ShapeDtypeStruct((rows, cols), BF),
            jax.ShapeDtypeStruct((8 * pairs, rows), F32),
        ],
        compiler_params=params(),
        name="combine",
    )(*os, *sts)


def delta_kernel(do, att, lse, aux, *, pairs):
    for p in range(pairs):
        c = slice(p * PAIR, (p + 1) * PAIR)
        prod = (do[:, c].astype(F32) * att[:, c]).T
        aux[8 * p : 8 * p + 2, :] = lse[8 * p : 8 * p + 2, :]
        for h in (0, 1):
            aux[8 * p + 2 + h : 8 * p + 3 + h, :] = jnp.sum(
                prod[h * HD : (h + 1) * HD, :], axis=0, keepdims=True
            )


def delta_call(do, att, lse):
    rows, cols = do.shape
    pairs = cols // PAIR
    blk = min(256, rows)
    wide = pl.BlockSpec((blk, cols), lambda i: (i, 0))
    flat = pl.BlockSpec((8 * pairs, blk), lambda i: (0, i))
    return pl.pallas_call(
        functools.partial(delta_kernel, pairs=pairs),
        grid=(rows // blk,),
        in_specs=[wide, wide, flat],
        out_specs=flat,
        out_shape=jax.ShapeDtypeStruct((8 * pairs, rows), F32),
        compiler_params=params(),
        name="deltas",
    )(do, att, lse)


def backward_kernel(e, do, q, st, aux, kt, v, *refs, pair0, fresh):
    dq, dk, dv = refs[-3:]

    @pl.when(pl.program_id(1) == 0)
    def _():
        if len(refs) == 3:
            dk[...] = jnp.zeros_like(dk)
            dv[...] = jnp.zeros_like(dv)
        else:
            new = pl.program_id(0) + pair0 >= fresh
            dk[...] = jnp.where(new, 0.0, refs[0][...])
            dv[...] = jnp.where(new, 0.0, refs[1][...])

    scw = spread(jnp.exp2(st[0:2, :] - aux[0:2, :]))
    sct = scw.T
    dos = (do[...].astype(F32) * sct).astype(BF)
    qs = (q[...].astype(F32) * (sct * LN2)).astype(BF)
    grads = []
    for h in (0, 1):
        dp = dot(head_half(v[...], h), do[...], NT)
        grads.append((e[h].astype(F32) * (dp - aux[h + 2 : h + 3, :])).astype(BF))
    dqt = jnp.concatenate([dot(kt[h * HD : (h + 1) * HD, :], grads[h]) for h in (0, 1)], 0)
    dq[...] = (dqt * (scw * HD**-0.5)).T.astype(BF)
    both = lambda a: jnp.concatenate([head_half(a, 0), head_half(a, 1)], 0)
    dv[...] += dot(jnp.concatenate([e[0], e[1]], 1), both(dos))
    dk[...] += dot(jnp.concatenate(grads, 1), both(qs))


def backward_call(e, do, q, st, aux, kt, v, carry, first_row, pair0, pairs, fresh, name):
    rows = do.shape[0]
    tokens, cols = v.shape
    rb = min(256, rows)
    off = first_row // rb
    whole = pl.BlockSpec((tokens, PAIR), lambda p, i: (0, p + pair0))
    carry = () if carry is None else tuple(carry)
    return pl.pallas_call(
        functools.partial(backward_kernel, pair0=pair0, fresh=fresh),
        grid=(pairs, rows // rb),
        in_specs=[
            pl.BlockSpec((2, tokens, rb), lambda p, i: (p + pair0, 0, i)),
            pl.BlockSpec((rb, PAIR), lambda p, i: (i, p + pair0)),
            pl.BlockSpec((rb, PAIR), lambda p, i: (i + off, p + pair0)),
            pl.BlockSpec((8, rb), lambda p, i: (p + pair0, i)),
            pl.BlockSpec((8, rb), lambda p, i: (p + pair0, i)),
            pl.BlockSpec((PAIR, tokens), lambda p, i: (p + pair0, 0)),
            pl.BlockSpec((tokens, PAIR), lambda p, i: (0, p + pair0)),
        ]
        + [whole] * len(carry),
        out_specs=[pl.BlockSpec((rb, PAIR), lambda p, i: (i, p)), whole, whole],
        out_shape=[
            jax.ShapeDtypeStruct((rows, pairs * PAIR), BF),
            jax.ShapeDtypeStruct((tokens, cols), F32),
            jax.ShapeDtypeStruct((tokens, cols), F32),
        ],
        input_output_aliases={7: 1, 8: 2} if carry else {},
        compiler_params=params(),
        cost_estimate=pl.CostEstimate(
            flops=rows * tokens * PAIR * pairs, bytes_accessed=rows * tokens, transcendentals=0
        ),
        name=f"backward_{name}",
    )(e, do, q, st, aux, kt, v, *carry)


def halves(acc, bit, send, keep):
    half = send.shape[0]
    send[...] = acc[pl.ds(pl.multiple_of((1 - bit) * half, 16), half), :].astype(BF)
    keep[...] = acc[pl.ds(pl.multiple_of(bit * half, 16), half), :].astype(BF)


def keyval_grad_kernel(bits, x, dk, dv, ko, kf, vo, vf, ks, kk, vs, vk, acck, accv, *, spots):
    i = pl.program_id(0)
    n = pl.num_programs(0)

    @pl.when(i == 0)
    def _():
        acck[...] = jnp.zeros_like(acck)
        accv[...] = jnp.zeros_like(accv)

    a = dk[...].astype(BF)
    b = dv[...].astype(BF)

    @pl.when(i < n // 2)
    def _():
        kf[...] = a
        vf[...] = b

    @pl.when(i >= n // 2)
    def _():
        ko[...] = a
        vo[...] = b

    acck[...] += dot(x[...], a, TN)
    accv[...] += dot(x[...], b, TN)

    @pl.when(i == n - 1)
    def _():
        halves(acck, bits[spots[0]], ks, kk)
        halves(accv, bits[spots[1]], vs, vk)


def keyval_grad_call(bits, spots, x, dk, dv):
    rows, width = x.shape
    cols = dk.shape[1]
    blk = 512
    half = rows // blk // 2
    turn_rows = lambda i: ((i + half) % (2 * half), 0)
    wide = pl.BlockSpec((blk, cols), turn_rows)
    own = pl.BlockSpec((blk, cols), lambda i: (jnp.maximum(i - half, 0), 0))
    far = pl.BlockSpec((blk, cols), lambda i: (jnp.minimum(i, half - 1), 0))
    part = pl.BlockSpec((width // 2, cols), lambda i: (0, 0))
    return pl.pallas_call(
        functools.partial(keyval_grad_kernel, spots=spots),
        grid=(2 * half,),
        in_specs=[
            pl.BlockSpec(memory_space=pltpu.SMEM),
            pl.BlockSpec((blk, width), turn_rows),
            wide,
            wide,
        ],
        out_specs=[own, far, own, far] + [part] * 4,
        out_shape=[jax.ShapeDtypeStruct((rows // 2, cols), BF)] * 4
        + [jax.ShapeDtypeStruct((width // 2, cols), BF)] * 4,
        scratch_shapes=[pltpu.VMEM((width, cols), F32)] * 2,
        compiler_params=params(),
        name="keyval_grad",
    )(bits, x, dk, dv)


def query_grad_kernel(bits, x, d0, d1, *refs, parts, spot):
    own, far, send, keep, acc = refs[parts:]
    i = pl.program_id(0)
    a = jnp.concatenate([d0[...], d1[...]], 1)
    if parts:
        a = sum((r[...].astype(F32) for r in refs[:parts]), a.astype(F32)).astype(BF)
    g = dot(x[...], a, TN)

    @pl.when(i == 0)
    def _():
        own[...] = a
        acc[...] = g

    @pl.when(i == 1)
    def _():
        far[...] = a
        acc[...] += g
        halves(acc, bits[spot], send, keep)


def query_grad_call(bits, spot, x, d0, d1, parts):
    rows = d0.shape[0]
    cols = d0.shape[1] + d1.shape[1]
    width = x.shape[1]
    blk = rows // 2
    wide = lambda c: pl.BlockSpec((blk, c), lambda i: (i, 0))
    fixed = pl.BlockSpec((blk, cols), lambda i: (0, 0))
    part = pl.BlockSpec((width // 2, cols), lambda i: (0, 0))
    return pl.pallas_call(
        functools.partial(query_grad_kernel, parts=len(parts), spot=spot),
        grid=(2,),
        in_specs=[pl.BlockSpec(memory_space=pltpu.SMEM), wide(width), wide(d0.shape[1]), wide(d1.shape[1])]
        + [wide(cols)] * len(parts),
        out_specs=[fixed, fixed, part, part],
        out_shape=[jax.ShapeDtypeStruct((blk, cols), BF)] * 2
        + [jax.ShapeDtypeStruct((width // 2, cols), BF)] * 2,
        scratch_shapes=[pltpu.VMEM((width, cols), F32)],
        compiler_params=params(),
        name="query_grad",
    )(bits, x, d0, d1, *parts)


def carried_grad_kernel(core, ids, ko, kf, vo, vf, wko, wkf, wvo, wvf, out, table):
    acc = dot(ko[...], wko[...], NT) + dot(kf[...], wkf[...], NT)
    acc += dot(vo[...], wvo[...], NT) + dot(vf[...], wvf[...], NT)
    out[...] = acc
    groups = table.shape[0]
    hot = lax.broadcasted_iota(jnp.int32, (groups, ids.shape[1]), 0) == ids[...]
    hot = hot.astype(F32).astype(BF)
    high = acc.astype(BF)
    rest = (acc - high.astype(F32)).astype(BF)

    @pl.when(pl.program_id(0) == 0)
    def _():
        table[...] = jnp.zeros_like(table)

    table[...] += dot(hot, high) + dot(hot, rest)


def carried_grad_call(core, ids, ko, kf, vo, vf, wk, wv, groups):
    rows, cols = ko.shape
    width = wk.shape[0]
    blk = 256
    wide = pl.BlockSpec((blk, cols), lambda i, o: (i, 0))
    own = pl.BlockSpec((width, cols), lambda i, o: (0, o[0]))
    far = pl.BlockSpec((width, cols), lambda i, o: (0, 1 - o[0]))
    return pl.pallas_call(
        carried_grad_kernel,
        grid_spec=pltpu.PrefetchScalarGridSpec(
            num_scalar_prefetch=1,
            grid=(rows // blk,),
            in_specs=[pl.BlockSpec((1, blk), lambda i, o: (0, i))] + [wide] * 4 + [own, far, own, far],
            out_specs=[
                pl.BlockSpec((blk, width), lambda i, o: (i, 0)),
                pl.BlockSpec((groups, width), lambda i, o: (0, 0)),
            ],
        ),
        out_shape=[
            jax.ShapeDtypeStruct((rows, width), F32),
            jax.ShapeDtypeStruct((groups, width), F32),
        ],
        compiler_params=params(),
        name="carried_grad",
    )(core[None], ids, ko, kf, vo, vf, wk, wk, wv, wv)


def rays_grad_kernel(spots, dqo, dqf, wo, wf, rays, middle, gain, shift, out, sums):
    g = dot(dqo[...], wo[...], NT) + dot(dqf[...], wf[...], NT)
    gain_row = gain[...].astype(F32)
    _, unit, scale = norm_forward(rays[...].astype(F32), gain_row, shift[...].astype(F32))
    back, grad_gain, grad_shift = norm_backward(g, unit, scale, gain_row)
    out[...] = middle[...] + back

    @pl.when(pl.program_id(0) == 0)
    def _():
        sums[...] = jnp.zeros_like(sums)

    sums[0:1, :] += grad_gain[None]
    sums[1:2, :] += grad_shift[None]


def rays_grad_call(spots, dqo, dqf, w, rays, middle, gain, shift):
    rows, cols = dqo.shape
    width = w.shape[0]
    blk = min(256, rows)
    n = rows // blk
    wide = lambda c: pl.BlockSpec((blk, c), lambda i, o: (i, 0))
    line = pl.BlockSpec((1, width), lambda i, o: (0, 0))
    return pl.pallas_call(
        rays_grad_kernel,
        grid_spec=pltpu.PrefetchScalarGridSpec(
            num_scalar_prefetch=1,
            grid=(n,),
            in_specs=[
                wide(cols),
                wide(cols),
                pl.BlockSpec((width, cols), lambda i, o: (0, o[0])),
                pl.BlockSpec((width, cols), lambda i, o: (0, 1 - o[0])),
                pl.BlockSpec((blk, width), lambda i, o: (o[1] * n + i, 0)),
                wide(width),
                line,
                line,
            ],
            out_specs=[wide(width), pl.BlockSpec((8, width), lambda i, o: (0, 0))],
        ),
        out_shape=[
            jax.ShapeDtypeStruct((rows, width), F32),
            jax.ShapeDtypeStruct((8, width), F32),
        ],
        compiler_params=params(),
        name="rays_grad",
    )(spots, dqo, dqf, w, w, rays, middle, gain.reshape(1, -1), shift.reshape(1, -1))


def finish_kernel(place, *refs, n):
    mines, fars, outs = refs[:n], refs[n : 2 * n], refs[2 * n :]
    for mine, far, out in zip(mines, fars, outs):
        cols = mine.shape[1]
        core = place[0]
        out[:, pl.ds(pl.multiple_of(core * cols, 128), cols)] = mine[...].astype(F32)
        out[:, pl.ds(pl.multiple_of((1 - core) * cols, 128), cols)] = far[...].astype(F32)


def finish_call(place, mines, fars):
    rows, cols = mines[0].shape
    n = len(mines)
    blk = 256
    return pl.pallas_call(
        functools.partial(finish_kernel, n=n),
        grid=(rows // blk,),
        in_specs=[pl.BlockSpec(memory_space=pltpu.SMEM)]
        + [pl.BlockSpec((blk, cols), lambda i: (i, 0))] * (2 * n),
        out_specs=[pl.BlockSpec((blk, 2 * cols), lambda i: (i, 0))] * n,
        out_shape=[jax.ShapeDtypeStruct((rows, 2 * cols), F32)] * n,
        compiler_params=params(),
        name="finish",
    )(place, *mines, *fars)


def fold_kernel(bits, *refs, modes, spots):
    n = len(modes)
    keeps, recvs, outs = refs[:n], refs[n : 2 * n], list(refs[2 * n :])
    for i, mode in enumerate(modes):
        if mode:
            send, keep = outs.pop(0), outs.pop(0)
            half = send.shape[0]
            bit = bits[spots[i]]
            for dst, b in ((send, 1 - bit), (keep, bit)):
                r = pl.ds(pl.multiple_of(b * half, 16), half)
                dst[...] = (keeps[i][r, :].astype(F32) + recvs[i][r, :].astype(F32)).astype(dst.dtype)
        else:
            dst = outs.pop(0)
            dst[...] = (keeps[i][...].astype(F32) + recvs[i][...].astype(F32)).astype(dst.dtype)


def fold_call(bits, spots, keeps, recvs, modes):
    shapes = []
    for x, mode in zip(keeps, modes):
        if mode:
            shapes += [jax.ShapeDtypeStruct((x.shape[0] // 2,) + x.shape[1:], x.dtype)] * 2
        else:
            shapes.append(jax.ShapeDtypeStruct(x.shape, x.dtype))
    whole = pl.BlockSpec(memory_space=pltpu.VMEM)
    out = pl.pallas_call(
        functools.partial(fold_kernel, modes=tuple(modes), spots=tuple(spots)),
        in_specs=[pl.BlockSpec(memory_space=pltpu.SMEM)] + [whole] * (2 * len(keeps)),
        out_specs=[whole] * len(shapes),
        out_shape=shapes,
        compiler_params=params(),
        name="fold",
    )(bits, *keeps, *recvs)
    out = list(out)
    return [((out.pop(0), out.pop(0)) if mode else (out[0], out.pop(0))) for mode in modes]


def join_kernel(bits, *refs, n, spots):
    mines, recvs, outs = refs[:n], refs[n : 2 * n], refs[2 * n :]
    for i in range(n):
        half = mines[i].shape[0]
        bit = bits[spots[i]]
        outs[i][pl.ds(pl.multiple_of(bit * half, 16), half), :] = mines[i][...]
        outs[i][pl.ds(pl.multiple_of((1 - bit) * half, 16), half), :] = recvs[i][...]


def join_call(bits, spots, mines, recvs):
    whole = pl.BlockSpec(memory_space=pltpu.VMEM)
    return pl.pallas_call(
        functools.partial(join_kernel, n=len(mines), spots=tuple(spots)),
        in_specs=[pl.BlockSpec(memory_space=pltpu.SMEM)] + [whole] * (2 * len(mines)),
        out_specs=[whole] * len(mines),
        out_shape=[jax.ShapeDtypeStruct((2 * x.shape[0],) + x.shape[1:], x.dtype) for x in mines],
        compiler_params=params(),
        name="join",
    )(bits, *mines, *recvs)


def pair_swap(x, step, sizes):
    axis, mask = step
    return lax.ppermute(x, axis, [(i, i ^ mask) for i in range(sizes[axis])])


def step_bit(step):
    axis, mask = step
    return (lax.axis_index(axis) // mask) % 2


def chip_steps(sizes):
    along = [("dp", 1 << j) for j in range(sizes["dp"].bit_length() - 1)]
    across = [("key", 2 << j) for j in range(sizes["key"].bit_length() - 2)]
    return along[:1] + across[:1] + along[1:2], along[2:] + across[1:]


def turn(first, i):
    i = i % len(first)
    return first[i:] + first[:i]


def tree_sum(parts, steps, sizes, bits, spot, after_first, before_last):
    n = len(parts)
    halved = [[True] for _ in parts]
    count = len(steps[0])
    for j in range(count):
        recvs = [pair_swap(parts[i][0], steps[i][j], sizes) for i in range(n)]
        keeps = [parts[i][1] for i in range(n)]
        if j + 1 < count:
            modes = [keeps[i].shape[0] % 32 == 0 for i in range(n)]
            spots = [spot[steps[i][j + 1]] for i in range(n)]
        else:
            modes = [False] * n
            spots = [0] * n
        parts = fold_call(bits, spots, keeps, recvs, modes)
        if j == 0:
            parts, after_first = lax.optimization_barrier((parts, after_first))
        for i in range(n):
            halved[i].append(modes[i])
    mines = [x[1] for x in parts]
    for j in reversed(range(count)):
        live = [i for i in range(n) if halved[i][j]]
        if not live:
            continue
        recvs = [pair_swap(mines[i], steps[i][j], sizes) for i in live]
        if j == 0:
            recvs, before_last = lax.optimization_barrier((recvs, before_last))
        spots = [spot[steps[i][j]] for i in live]
        for i, x in zip(live, join_call(bits, spots, [mines[i] for i in live], recvs)):
            mines[i] = x
    return mines, after_first, before_last


def local(
    ray_tokens,
    latents,
    group_ids,
    ln1_gain,
    ln1_shift,
    w_query,
    w_key,
    w_value,
    w_out,
    ln2_gain,
    ln2_shift,
    w_up,
    b_up,
    w_down,
    b_down,
    intrinsics,
    out_grad,
    *,
    sizes,
):
    keys = sizes["key"]
    share = out_grad.shape[0]
    width = ray_tokens.shape[1]
    cols = width // 2
    pairs = cols // PAIR
    chips = keys // 2
    chip_rows = 2 * share
    place = lax.axis_index("key")
    core = place % 2
    chip = place // 2

    def core_swap(x):
        return lax.ppermute(x, "key", [(i, i ^ 1) for i in range(keys)])

    def chip_shift(x, s):
        return lax.ppermute(x, "key", [(i, (i + 2 * s) % keys) for i in range(keys)])

    def own_cols(w):
        return lax.dynamic_slice_in_dim(w, core * cols, cols, 1)

    def far_cols(w):
        return lax.dynamic_slice_in_dim(w, (1 - core) * cols, cols, 1)

    def own_rows(w):
        return lax.dynamic_slice_in_dim(w, core * cols, cols, 0)

    def far_rows(w):
        return lax.dynamic_slice_in_dim(w, (1 - core) * cols, cols, 0)

    gain_one = ln1_gain.astype(F32)
    shift_one = ln1_shift.astype(F32)
    gain_two = ln2_gain.astype(F32)
    shift_two = ln2_shift.astype(F32)
    lookup = group_ids[0][:, None] == jnp.arange(intrinsics.shape[0], dtype=jnp.int32)[None, :]
    carried = (
        latents[0].astype(F32)
        + jnp.dot(lookup.astype(BF), intrinsics, preferred_element_type=F32)
    ).astype(BF)
    tokens = carried.shape[0]
    chip_carried = jnp.concatenate([carried, core_swap(carried)], 0)
    steps = jnp.arange(keys, dtype=jnp.int32)
    order = ((chip + steps // 2) % chips) * 2 + (core + steps % 2) % 2
    normed, queries = query_call(order, core, ray_tokens, ln1_gain, ln1_shift, w_query, share)
    key_rows, value_rows, key_cols, value_cols = keyval_call(core, chip_carried, w_key, w_value)

    stats, exps, os, sts = [None] * chips, [None] * chips, [None] * chips, [None] * chips
    ordered = queries
    for t in [*range(1, chips), 0]:
        o, st, e = attend_call(
            ordered, key_rows, value_cols, t * chip_rows, chip_rows, "far" if t else "own"
        )
        stats[t], exps[t] = st, e
        if t:
            ordered, o, st = lax.optimization_barrier((ordered, o, st))
        os[t], sts[t] = (chip_shift(o, t), chip_shift(st, t)) if t else (o, st)
    att, low_chip, lse = combine_call(os, sts)
    low_own = low_chip[:share]
    low_far = core_swap(low_chip[share:])
    attended_low = jnp.concatenate(
        [jnp.where(core == 0, low_own, low_far), jnp.where(core == 0, low_far, low_own)], 1
    )
    own_rays = lax.dynamic_slice_in_dim(ray_tokens, place * share, share, 0).astype(F32)
    middle = own_rays + dot(attended_low, w_out)
    normed_two, unit_two, scale_two = norm_forward(middle, gain_two, shift_two)
    normed_two_low = normed_two.astype(BF)
    hidden = dot(normed_two_low, w_up) + b_up.astype(F32)
    active, gelu_back = jax.vjp(jax.nn.gelu, hidden)
    active_low = active.astype(BF)
    output = (middle + dot(active_low, w_down) + b_down.astype(F32)).astype(BF)
    grad_out = out_grad.astype(F32)
    grad_active = lax.optimization_barrier(dot(out_grad, w_down, NT).astype(BF)).astype(F32)
    grad_hidden = gelu_back(grad_active)[0].astype(BF)
    grad_normed_two = dot(grad_hidden, w_up, NT)
    grad_middle_norm, grad_gain_two, grad_shift_two = norm_backward(
        grad_normed_two, unit_two, scale_two, gain_two
    )
    grad_middle = grad_out + grad_middle_norm
    grad_branch = grad_middle.astype(BF)
    do_far = core_swap(dot(grad_branch, far_rows(w_out), NT).astype(BF))
    do_own = dot(grad_branch, own_rows(w_out), NT).astype(BF)
    do_chip = jnp.concatenate([do_own, do_far], 0)
    aux_chip = delta_call(do_chip, att, lse)
    dos, auxs = [do_chip], [aux_chip]
    for t in range(1, chips):
        dos.append(chip_shift(do_chip, chips - t))
        auxs.append(chip_shift(aux_chip, chips - t))
    grad_w_down = dot(active_low, out_grad, TN).astype(BF)
    grad_b_down = jnp.sum(grad_out, axis=0)
    grad_w_up = dot(normed_two_low, grad_hidden, TN).astype(BF)
    grad_b_up = jnp.sum(grad_hidden.astype(F32), axis=0)
    grad_w_out = dot(attended_low, grad_branch, TN).astype(BF)
    dos[0], auxs[0], *branch_parts = lax.optimization_barrier(
        (do_chip, aux_chip, grad_w_out, grad_w_up, grad_w_down)
    )
    branch_grads = lax.psum(branch_parts, ("dp", "key"))

    first, rest = chip_steps(sizes)
    steps = [turn(first, i) + rest for i in range(4)]
    spot = {x: i for i, x in enumerate(first + rest)}
    bits = jnp.stack([step_bit(x) for x in first + rest]).astype(jnp.int32)

    def back(t, carry, pair0, count, fresh, name):
        return backward_call(
            exps[t],
            dos[t],
            queries,
            stats[t],
            auxs[t],
            key_cols,
            value_rows,
            carry,
            t * chip_rows,
            pair0,
            count,
            fresh,
            name,
        )

    dq_first, *carry = back(0, None, 0, 1, 0, "own_first")
    parts = []
    for t in range(1, chips):
        dq, *carry = back(t, carry, 0, pairs, 1 if t == 1 else pairs, "far")
        parts.append(chip_shift(dq, t))
    dq_rest, *carry = back(0, carry, 1, pairs - 1, pairs, "own_rest")
    keys_own, keys_far, values_own, values_far, key_send, key_keep, value_send, value_keep = (
        keyval_grad_call(bits, (spot[steps[1][0]], spot[steps[2][0]]), chip_carried, *carry)
    )
    queries_own, queries_far, query_send, query_keep = query_grad_call(
        bits, spot[steps[0][0]], normed, dq_first, dq_rest, parts
    )
    queries_far = core_swap(queries_far)
    rays_grad, norm_sums = rays_grad_call(
        jnp.stack([core, place]),
        queries_own,
        queries_far,
        w_query,
        ray_tokens,
        grad_middle,
        ln1_gain,
        ln1_shift,
    )
    tokens_far = [core_swap(x) for x in (keys_far, values_far)]
    sums, (keys_own, values_own, *tokens_far), branch_grads = tree_sum(
        [(query_send, query_keep), (key_send, key_keep), (value_send, value_keep)],
        steps[:3],
        sizes,
        bits,
        spot,
        [keys_own, values_own] + tokens_far,
        branch_grads,
    )
    branch_grads = [x.astype(F32) for x in branch_grads]
    grad_carried, grad_table = carried_grad_call(
        core,
        group_ids,
        keys_own,
        tokens_far[0],
        values_own,
        tokens_far[1],
        w_key,
        w_value,
        intrinsics.shape[0],
    )
    grad_gain_one, grad_shift_one = norm_sums[0], norm_sums[1]
    vectors = (
        grad_gain_one,
        grad_shift_one,
        grad_gain_two,
        grad_shift_two,
        grad_b_up,
        grad_b_down,
        grad_table,
    )
    small = jnp.concatenate([x.reshape(-1, width) for x in vectors], 0)
    small = jnp.pad(small, ((0, -small.shape[0] % 8), (0, 0)))
    small = small + core_swap(small)
    for x in steps[0]:
        small = small + pair_swap(small, x, sizes)
    attention_grads = finish_call(core[None], sums[:3], [core_swap(g) for g in sums[:3]])
    spots = []
    at = 0
    for x in vectors:
        n = x.size // width
        spots.append(small[at : at + n].reshape(x.shape))
        at += n
    return (
        output,
        rays_grad,
        grad_carried[None],
        spots[0],
        spots[1],
        attention_grads[0],
        attention_grads[1],
        attention_grads[2],
        branch_grads[0],
        spots[2],
        spots[3],
        branch_grads[1],
        spots[4],
        branch_grads[2],
        spots[5],
        spots[6],
    )


def solution(mesh):
    rows = P(("dp", "key"), None)
    placed = (P("dp", None), P("dp", "key", None), P("dp", "key")) + (P(),) * 13 + (rows,)
    return jax.shard_map(
        functools.partial(local, sizes=dict(mesh.shape)),
        mesh=mesh,
        in_specs=placed,
        out_specs=(rows, rows, P("dp", "key", None)) + (P(),) * 13,
        check_vma=False,
    )
```

```python
import functools

import jax
import jax.numpy as jnp
from jax import lax
from jax.experimental import pallas as pl
from jax.experimental.pallas import tpu as pltpu
from jax.sharding import PartitionSpec as P

H = 12
HD = 64
PAIR = 2 * HD
EPSILON = 1e-05
HIGHEST = lax.Precision.HIGHEST
BF = jnp.bfloat16
F32 = jnp.float32
LOG2E = 1.4426950408889634
LN2 = 0.6931471805599453
SAFE_BOUND = 60.0
BRIEF = pl.CostEstimate(flops=1000, bytes_accessed=1000, transcendentals=0)
VMEM = 60 * 1024 * 1024


def dot(a, b, dims=((1,), (0,))):
    return lax.dot_general(a, b, (dims, ((), ())), preferred_element_type=F32)


NT = ((1,), (1,))
TN = ((0,), (0,))


def params(**kw):
    return pltpu.CompilerParams(vmem_limit_bytes=VMEM, **kw)


def head_half(x, h, axis=1):
    i = lax.broadcasted_iota(jnp.int32, x.shape, axis)
    return jnp.where((i < HD) == (h == 0), x, jnp.zeros_like(x))


def norm_forward(values, gain_vec, shift_vec):
    centre = values - jnp.mean(values, axis=-1, keepdims=True)
    scaled = lax.rsqrt(jnp.mean(centre * centre, axis=-1, keepdims=True) + EPSILON)
    unit_rows = centre * scaled
    return (unit_rows * gain_vec + shift_vec, unit_rows, scaled)


def norm_backward(grad_rows, unit_rows, scaled, gain_vec):
    grad_unit = grad_rows * gain_vec
    centred_grad = (
        grad_unit
        - jnp.mean(grad_unit, axis=-1, keepdims=True)
        - unit_rows * jnp.mean(grad_unit * unit_rows, axis=-1, keepdims=True)
    )
    return (
        scaled * centred_grad,
        jnp.sum(grad_rows * unit_rows, axis=0),
        jnp.sum(grad_rows, axis=0),
    )


def query_kernel(order, rays, gain, shift, wq, normed, q):
    n, _, _ = norm_forward(rays[...].astype(F32), gain[...].astype(F32), shift[...].astype(F32))
    n = n.astype(BF)
    normed[...] = n
    q[...] = (dot(n, wq[...]) * (HD**-0.5 * LOG2E)).astype(BF)


def query_call(order, core, rays, gain, shift, wq, share):
    rows, width = rays.shape
    cols = width // 2
    blocks = rows // share
    pre = jnp.concatenate([order, core[None]])
    return pl.pallas_call(
        query_kernel,
        grid_spec=pltpu.PrefetchScalarGridSpec(
            num_scalar_prefetch=1,
            grid=(blocks,),
            in_specs=[
                pl.BlockSpec((share, width), lambda i, o: (o[i], 0)),
                pl.BlockSpec((1, width), lambda i, o: (0, 0)),
                pl.BlockSpec((1, width), lambda i, o: (0, 0)),
                pl.BlockSpec((width, cols), lambda i, o: (0, o[blocks])),
            ],
            out_specs=[
                pl.BlockSpec((share, width), lambda i, o: (i, 0)),
                pl.BlockSpec((share, cols), lambda i, o: (i, 0)),
            ],
        ),
        out_shape=[
            jax.ShapeDtypeStruct((rows, width), BF),
            jax.ShapeDtypeStruct((rows, cols), BF),
        ],
        compiler_params=params(),
        cost_estimate=BRIEF,
        name="rays_query",
    )(pre, rays, gain.reshape(1, -1), shift.reshape(1, -1), wq)


def keyval_kernel(core, own, far, wk, wv, k, v, kt, vt):
    x = jnp.where(pl.program_id(0) < pl.num_programs(0) // 2, own[...], far[...])
    kk = dot(x, wk[...]).astype(BF)
    vv = dot(x, wv[...]).astype(BF)
    k[...] = kk
    v[...] = vv
    kt[...] = kk.T
    vt[...] = vv.T


def keyval_call(core, own, far, wk, wv):
    rows, width = own.shape
    rows = 2 * rows
    cols = width // 2
    blk = 512
    half = rows // blk // 2
    return pl.pallas_call(
        keyval_kernel,
        grid_spec=pltpu.PrefetchScalarGridSpec(
            num_scalar_prefetch=1,
            grid=(rows // blk,),
            in_specs=[
                pl.BlockSpec((blk, width), lambda i, o: (jnp.minimum(i, half - 1), 0)),
                pl.BlockSpec((blk, width), lambda i, o: (jnp.maximum(i - half, 0), 0)),
                pl.BlockSpec((width, cols), lambda i, o: (0, o[0])),
                pl.BlockSpec((width, cols), lambda i, o: (0, o[0])),
            ],
            out_specs=[
                pl.BlockSpec((blk, cols), lambda i, o: (i, 0)),
                pl.BlockSpec((blk, cols), lambda i, o: (i, 0)),
                pl.BlockSpec((cols, blk), lambda i, o: (0, i)),
                pl.BlockSpec((cols, blk), lambda i, o: (0, i)),
            ],
        ),
        out_shape=[
            jax.ShapeDtypeStruct((rows, cols), BF),
            jax.ShapeDtypeStruct((rows, cols), BF),
            jax.ShapeDtypeStruct((cols, rows), BF),
            jax.ShapeDtypeStruct((cols, rows), BF),
        ],
        compiler_params=params(),
        cost_estimate=BRIEF,
        name="keys_values",
    )(core[None], own, far, wk, wv)


def attend_kernel(qb, k, vt, o, st, e, km, kn, spare, *, tc):
    tokens = k.shape[0]
    rb = qb.shape[0]
    chunks = [slice(c, c + tc) for c in range(0, tokens, tc)]

    @pl.when(pl.program_id(1) == 0)
    def _():
        for h in (0, 1):
            kh = head_half(k[...], h)
            km[h] = kh
            kf = kh.astype(F32)
            top = jnp.max(jnp.sum(kf * kf, axis=1, keepdims=True), axis=0, keepdims=True)
            kn[h : h + 1, :] = jnp.broadcast_to(top, (1, PAIR))

    qf = qb[...].astype(F32)
    bound = jnp.float32(0)
    for h in (0, 1):
        qn = jnp.max(jnp.sum(head_half(qf * qf, h), axis=1, keepdims=True), axis=0, keepdims=True)
        bound = jnp.maximum(bound, jnp.max(qn * kn[h : h + 1, :]))
    small = bound < SAFE_BOUND * SAFE_BOUND

    def scores(h, r):
        return dot(km[h, r, :], qb[...], NT)

    def mixed(h, r, low):
        cols = jnp.concatenate([vt[h * HD : (h + 1) * HD, r], jnp.ones((HD, tc), BF)], 0)
        return dot(cols, low)

    def finish(acc, shifts):
        outs = []
        for h in (0, 1):
            total = acc[h][HD : HD + 1]
            outs.append(acc[h][:HD] / total)
            st[h : h + 1, :] = shifts[h]
            st[h + 2 : h + 3, :] = shifts[h] + jnp.log2(total)
        o[...] = jnp.concatenate(outs, 0).T.astype(BF)

    @pl.when(small)
    def _():
        items = [(h, r) for h in (0, 1) for r in chunks]
        acc = [0.0, 0.0]
        ready = [scores(*items[0])]
        waiting = []
        for n, (h, r) in enumerate(items):
            if n + 1 < len(items):
                ready.append(scores(*items[n + 1]))
            low = jnp.exp2(ready.pop(0)).astype(BF)
            e[h, r, :] = low
            if waiting:
                g, *rest = waiting.pop()
                acc[g] = acc[g] + mixed(g, *rest)
            waiting.append((h, r, low))
        g, *rest = waiting.pop()
        acc[g] = acc[g] + mixed(g, *rest)
        finish(acc, [jnp.zeros((1, rb), F32)] * 2)

    @pl.when(jnp.logical_not(small))
    def _():
        acc = [0.0, 0.0]
        shifts = []
        for h in (0, 1):
            m = None
            for r in chunks:
                s = scores(h, r)
                spare[r, :] = s
                mc = jnp.max(s, axis=0, keepdims=True)
                m = mc if m is None else jnp.maximum(m, mc)
            shifts.append(m)
            for r in chunks:
                low = jnp.exp2(spare[r, :] - m).astype(BF)
                e[h, r, :] = low
                acc[h] = acc[h] + mixed(h, r, low)
        finish(acc, shifts)


def attend_call(q, k, vt, first_row, rows, name):
    tokens, cols = k.shape
    pairs = cols // PAIR
    rb = min(512, rows)
    off = first_row // rb
    return pl.pallas_call(
        functools.partial(attend_kernel, tc=min(1024, tokens)),
        grid=(pairs, rows // rb),
        in_specs=[
            pl.BlockSpec((rb, PAIR), lambda p, i: (i + off, p)),
            pl.BlockSpec((tokens, PAIR), lambda p, i: (0, p)),
            pl.BlockSpec((PAIR, tokens), lambda p, i: (p, 0)),
        ],
        out_specs=[
            pl.BlockSpec((rb, PAIR), lambda p, i: (i, p)),
            pl.BlockSpec((8, rb), lambda p, i: (p, i)),
            pl.BlockSpec((2, tokens, rb), lambda p, i: (p, 0, i)),
        ],
        out_shape=[
            jax.ShapeDtypeStruct((rows, cols), BF),
            jax.ShapeDtypeStruct((8 * pairs, rows), F32),
            jax.ShapeDtypeStruct((2 * pairs, tokens, rows), BF),
        ],
        scratch_shapes=[
            pltpu.VMEM((2, tokens, PAIR), BF),
            pltpu.VMEM((8, PAIR), F32),
            pltpu.VMEM((tokens, rb), F32),
        ],
        compiler_params=params(),
        cost_estimate=BRIEF,
        name=f"attend_{name}",
    )(q, k, vt)


def spread(rows2):
    rows = rows2.shape[1]
    return jnp.concatenate([jnp.broadcast_to(rows2[h : h + 1, :], (HD, rows)) for h in (0, 1)], 0)


def combine_kernel(*refs, parts, pairs):
    os, sts = refs[:parts], refs[parts : 2 * parts]
    att, low, lse = refs[2 * parts :]
    for p in range(pairs):
        c = slice(p * PAIR, (p + 1) * PAIR)
        ls = [s[8 * p + 2 : 8 * p + 4, :] for s in sts]
        top = functools.reduce(jnp.maximum, ls)
        tot = top + jnp.log2(sum(jnp.exp2(x - top) for x in ls))
        acc = 0.0
        for o, x in zip(os, ls):
            acc = acc + o[:, c].astype(F32) * spread(jnp.exp2(x - tot)).T
        att[:, c] = acc
        low[:, c] = acc.astype(BF)
        lse[8 * p : 8 * p + 2, :] = tot


def combine_call(os, sts):
    parts = len(os)
    rows, cols = os[0].shape
    pairs = cols // PAIR
    blk = min(256, rows)
    wide = pl.BlockSpec((blk, cols), lambda i: (i, 0))
    flat = pl.BlockSpec((8 * pairs, blk), lambda i: (0, i))
    return pl.pallas_call(
        functools.partial(combine_kernel, parts=parts, pairs=pairs),
        grid=(rows // blk,),
        in_specs=[wide] * parts + [flat] * parts,
        out_specs=[wide, wide, flat],
        out_shape=[
            jax.ShapeDtypeStruct((rows, cols), F32),
            jax.ShapeDtypeStruct((rows, cols), BF),
            jax.ShapeDtypeStruct((8 * pairs, rows), F32),
        ],
        compiler_params=params(),
        cost_estimate=BRIEF,
        name="combine",
    )(*os, *sts)


def delta_kernel(do, att, lse, aux, *, pairs):
    for p in range(pairs):
        c = slice(p * PAIR, (p + 1) * PAIR)
        prod = (do[:, c].astype(F32) * att[:, c]).T
        aux[8 * p : 8 * p + 2, :] = lse[8 * p : 8 * p + 2, :]
        for h in (0, 1):
            aux[8 * p + 2 + h : 8 * p + 3 + h, :] = jnp.sum(
                prod[h * HD : (h + 1) * HD, :], axis=0, keepdims=True
            )


def delta_call(do, att, lse):
    rows, cols = do.shape
    pairs = cols // PAIR
    blk = min(256, rows)
    wide = pl.BlockSpec((blk, cols), lambda i: (i, 0))
    flat = pl.BlockSpec((8 * pairs, blk), lambda i: (0, i))
    return pl.pallas_call(
        functools.partial(delta_kernel, pairs=pairs),
        grid=(rows // blk,),
        in_specs=[wide, wide, flat],
        out_specs=flat,
        out_shape=jax.ShapeDtypeStruct((8 * pairs, rows), F32),
        compiler_params=params(),
        cost_estimate=BRIEF,
        name="deltas",
    )(do, att, lse)


def backward_kernel(e, do, q, st, aux, kt, v, *refs, pair0, fresh):
    dq, dk, dv = refs[-3:]

    @pl.when(pl.program_id(1) == 0)
    def _():
        if len(refs) == 3:
            dk[...] = jnp.zeros_like(dk)
            dv[...] = jnp.zeros_like(dv)
        else:
            new = pl.program_id(0) + pair0 >= fresh
            dk[...] = jnp.where(new, 0.0, refs[0][...])
            dv[...] = jnp.where(new, 0.0, refs[1][...])

    scw = spread(jnp.exp2(st[0:2, :] - aux[0:2, :]))
    sct = scw.T
    dos = (do[...].astype(F32) * sct).astype(BF)
    qs = (q[...].astype(F32) * (sct * LN2)).astype(BF)
    grads = []
    for h in (0, 1):
        dp = dot(head_half(v[...], h), do[...], NT)
        grads.append((e[h].astype(F32) * (dp - aux[h + 2 : h + 3, :])).astype(BF))
    dqt = jnp.concatenate([dot(kt[h * HD : (h + 1) * HD, :], grads[h]) for h in (0, 1)], 0)
    dq[...] = (dqt * (scw * HD**-0.5)).T.astype(BF)
    both = lambda a: jnp.concatenate([head_half(a, 0), head_half(a, 1)], 0)
    dv[...] += dot(jnp.concatenate([e[0], e[1]], 1), both(dos))
    dk[...] += dot(jnp.concatenate(grads, 1), both(qs))


def backward_call(e, do, q, st, aux, kt, v, carry, first_row, pair0, pairs, fresh, name):
    rows = do.shape[0]
    tokens, cols = v.shape
    rb = min(256, rows)
    off = first_row // rb
    whole = pl.BlockSpec((tokens, PAIR), lambda p, i: (0, p + pair0))
    carry = () if carry is None else tuple(carry)
    return pl.pallas_call(
        functools.partial(backward_kernel, pair0=pair0, fresh=fresh),
        grid=(pairs, rows // rb),
        in_specs=[
            pl.BlockSpec((2, tokens, rb), lambda p, i: (p + pair0, 0, i)),
            pl.BlockSpec((rb, PAIR), lambda p, i: (i, p + pair0)),
            pl.BlockSpec((rb, PAIR), lambda p, i: (i + off, p + pair0)),
            pl.BlockSpec((8, rb), lambda p, i: (p + pair0, i)),
            pl.BlockSpec((8, rb), lambda p, i: (p + pair0, i)),
            pl.BlockSpec((PAIR, tokens), lambda p, i: (p + pair0, 0)),
            pl.BlockSpec((tokens, PAIR), lambda p, i: (0, p + pair0)),
        ]
        + [whole] * len(carry),
        out_specs=[pl.BlockSpec((rb, PAIR), lambda p, i: (i, p)), whole, whole],
        out_shape=[
            jax.ShapeDtypeStruct((rows, pairs * PAIR), BF),
            jax.ShapeDtypeStruct((tokens, cols), F32),
            jax.ShapeDtypeStruct((tokens, cols), F32),
        ],
        input_output_aliases={7: 1, 8: 2} if carry else {},
        compiler_params=params(),
        cost_estimate=BRIEF,
        name=f"backward_{name}",
    )(e, do, q, st, aux, kt, v, *carry)


def halves(acc, mark, count, send, keep):
    blocks = 1 << count
    size = acc.shape[0] // blocks
    for j in range(blocks):
        dst = keep if j < blocks // 2 else send
        at = j % (blocks // 2) * size
        rows = pl.ds(pl.multiple_of((j ^ mark) * size, 16), size)
        dst[at : at + size, :] = acc[rows, :].astype(BF)


def keyval_grad_kernel(marks, x_own, x_far, dk, dv, ko, kf, vo, vf, ks, kk, vs, vk, acck, accv, *, count):
    i = pl.program_id(0)
    n = pl.num_programs(0)

    @pl.when(i == 0)
    def _():
        acck[...] = jnp.zeros_like(acck)
        accv[...] = jnp.zeros_like(accv)

    a = dk[...].astype(BF)
    b = dv[...].astype(BF)

    @pl.when(i < n // 2)
    def _():
        kf[...] = a
        vf[...] = b

    @pl.when(i >= n // 2)
    def _():
        ko[...] = a
        vo[...] = b

    x = jnp.where(i < n // 2, x_far[...], x_own[...])
    acck[...] += dot(x, a, TN)
    accv[...] += dot(x, b, TN)

    @pl.when(i == n - 1)
    def _():
        halves(acck, marks[1], count, ks, kk)
        halves(accv, marks[2], count, vs, vk)


def keyval_grad_call(marks, count, own, far, dk, dv):
    rows, width = own.shape
    rows = 2 * rows
    cols = dk.shape[1]
    blk = 512
    half = rows // blk // 2
    turn_rows = lambda i: ((i + half) % (2 * half), 0)
    wide = pl.BlockSpec((blk, cols), turn_rows)
    own_at = lambda c: pl.BlockSpec((blk, c), lambda i: (jnp.maximum(i - half, 0), 0))
    far_at = lambda c: pl.BlockSpec((blk, c), lambda i: (jnp.minimum(i, half - 1), 0))
    part = pl.BlockSpec((width // 2, cols), lambda i: (0, 0))
    return pl.pallas_call(
        functools.partial(keyval_grad_kernel, count=count),
        grid=(2 * half,),
        in_specs=[
            pl.BlockSpec(memory_space=pltpu.SMEM),
            own_at(width),
            far_at(width),
            wide,
            wide,
        ],
        out_specs=[own_at(cols), far_at(cols)] * 2 + [part] * 4,
        out_shape=[jax.ShapeDtypeStruct((rows // 2, cols), BF)] * 4
        + [jax.ShapeDtypeStruct((width // 2, cols), BF)] * 4,
        scratch_shapes=[pltpu.VMEM((width, cols), F32)] * 2,
        compiler_params=params(),
        cost_estimate=BRIEF,
        name="keyval_grad",
    )(marks, own, far, dk, dv)


def query_grad_kernel(marks, x, d0, d1, *refs, parts, count):
    own, far, send, keep, acc = refs[parts:]
    i = pl.program_id(0)
    a = jnp.concatenate([d0[...], d1[...]], 1)
    if parts:
        a = sum((r[...].astype(F32) for r in refs[:parts]), a.astype(F32)).astype(BF)
    g = dot(x[...], a, TN)

    @pl.when(i == 0)
    def _():
        own[...] = a
        acc[...] = g

    @pl.when(i == 1)
    def _():
        far[...] = a
        acc[...] += g
        halves(acc, marks[0], count, send, keep)


def query_grad_call(marks, count, x, d0, d1, parts):
    rows = d0.shape[0]
    cols = d0.shape[1] + d1.shape[1]
    width = x.shape[1]
    blk = rows // 2
    wide = lambda c: pl.BlockSpec((blk, c), lambda i: (i, 0))
    fixed = pl.BlockSpec((blk, cols), lambda i: (0, 0))
    part = pl.BlockSpec((width // 2, cols), lambda i: (0, 0))
    return pl.pallas_call(
        functools.partial(query_grad_kernel, parts=len(parts), count=count),
        grid=(2,),
        in_specs=[pl.BlockSpec(memory_space=pltpu.SMEM), wide(width), wide(d0.shape[1]), wide(d1.shape[1])]
        + [wide(cols)] * len(parts),
        out_specs=[fixed, fixed, part, part],
        out_shape=[jax.ShapeDtypeStruct((blk, cols), BF)] * 2
        + [jax.ShapeDtypeStruct((width // 2, cols), BF)] * 2,
        scratch_shapes=[pltpu.VMEM((width, cols), F32)],
        compiler_params=params(),
        cost_estimate=BRIEF,
        name="query_grad",
    )(marks, x, d0, d1, *parts)


def carried_grad_kernel(core, ids, ko, kf, vo, vf, wko, wkf, wvo, wvf, out, table):
    acc = dot(ko[...], wko[...], NT) + dot(kf[...], wkf[...], NT)
    acc += dot(vo[...], wvo[...], NT) + dot(vf[...], wvf[...], NT)
    out[...] = acc
    groups = table.shape[0]
    hot = lax.broadcasted_iota(jnp.int32, (groups, ids.shape[1]), 0) == ids[...]
    hot = hot.astype(F32).astype(BF)
    high = acc.astype(BF)
    rest = (acc - high.astype(F32)).astype(BF)

    @pl.when(pl.program_id(0) == 0)
    def _():
        table[...] = jnp.zeros_like(table)

    table[...] += dot(hot, high) + dot(hot, rest)


def carried_grad_call(core, ids, ko, kf, vo, vf, wk, wv, groups):
    rows, cols = ko.shape
    width = wk.shape[0]
    blk = 256
    wide = pl.BlockSpec((blk, cols), lambda i, o: (i, 0))
    own = pl.BlockSpec((width, cols), lambda i, o: (0, o[0]))
    far = pl.BlockSpec((width, cols), lambda i, o: (0, 1 - o[0]))
    return pl.pallas_call(
        carried_grad_kernel,
        grid_spec=pltpu.PrefetchScalarGridSpec(
            num_scalar_prefetch=1,
            grid=(rows // blk,),
            in_specs=[pl.BlockSpec((1, blk), lambda i, o: (0, i))] + [wide] * 4 + [own, far, own, far],
            out_specs=[
                pl.BlockSpec((blk, width), lambda i, o: (i, 0)),
                pl.BlockSpec((groups, width), lambda i, o: (0, 0)),
            ],
        ),
        out_shape=[
            jax.ShapeDtypeStruct((rows, width), F32),
            jax.ShapeDtypeStruct((groups, width), F32),
        ],
        compiler_params=params(),
        cost_estimate=BRIEF,
        name="carried_grad",
    )(core[None], ids, ko, kf, vo, vf, wk, wk, wv, wv)


def rays_grad_kernel(spots, dqo, dqf, wo, wf, rays, middle, gain, shift, out, sums):
    g = dot(dqo[...], wo[...], NT) + dot(dqf[...], wf[...], NT)
    gain_row = gain[...].astype(F32)
    _, unit, scale = norm_forward(rays[...].astype(F32), gain_row, shift[...].astype(F32))
    back, grad_gain, grad_shift = norm_backward(g, unit, scale, gain_row)
    out[...] = middle[...] + back

    @pl.when(pl.program_id(0) == 0)
    def _():
        sums[...] = jnp.zeros_like(sums)

    sums[0:1, :] += grad_gain[None]
    sums[1:2, :] += grad_shift[None]


def rays_grad_call(spots, dqo, dqf, w, rays, middle, gain, shift):
    rows, cols = dqo.shape
    width = w.shape[0]
    blk = min(256, rows)
    n = rows // blk
    wide = lambda c: pl.BlockSpec((blk, c), lambda i, o: (i, 0))
    line = pl.BlockSpec((1, width), lambda i, o: (0, 0))
    return pl.pallas_call(
        rays_grad_kernel,
        grid_spec=pltpu.PrefetchScalarGridSpec(
            num_scalar_prefetch=1,
            grid=(n,),
            in_specs=[
                wide(cols),
                wide(cols),
                pl.BlockSpec((width, cols), lambda i, o: (0, o[0])),
                pl.BlockSpec((width, cols), lambda i, o: (0, 1 - o[0])),
                pl.BlockSpec((blk, width), lambda i, o: (o[1] * n + i, 0)),
                wide(width),
                line,
                line,
            ],
            out_specs=[wide(width), pl.BlockSpec((8, width), lambda i, o: (0, 0))],
        ),
        out_shape=[
            jax.ShapeDtypeStruct((rows, width), F32),
            jax.ShapeDtypeStruct((8, width), F32),
        ],
        compiler_params=params(),
        cost_estimate=BRIEF,
        name="rays_grad",
    )(spots, dqo, dqf, w, w, rays, middle, gain.reshape(1, -1), shift.reshape(1, -1))


def finish_kernel(marks, *refs, n, inner, size):
    core = marks[n]
    mines, fars, outs = refs[:n], refs[n : 2 * n], refs[2 * n :]
    for i, (mine, far, out) in enumerate(zip(mines, fars, outs)):
        cols = mine.shape[1]
        for j in range(inner):
            src = pl.ds(pl.multiple_of((j ^ (marks[i] & (inner - 1))) * size, 16), size)
            dst = slice(j * size, (j + 1) * size)
            out[dst, pl.ds(pl.multiple_of(core * cols, 128), cols)] = mine[src, :].astype(F32)
            out[dst, pl.ds(pl.multiple_of((1 - core) * cols, 128), cols)] = far[src, :].astype(F32)


def finish_call(marks, count, mines, fars):
    rows, cols = mines[0].shape
    n = len(mines)
    outer = min(2, count)
    inner = 1 << (count - outer)
    size = rows >> count
    blk = size * inner

    def place(k):
        return pl.BlockSpec((blk, cols), lambda i, m: (i ^ (m[k] // inner), 0))

    return pl.pallas_call(
        functools.partial(finish_kernel, n=n, inner=inner, size=size),
        grid_spec=pltpu.PrefetchScalarGridSpec(
            num_scalar_prefetch=1,
            grid=(1 << outer,),
            in_specs=[place(k) for k in range(n)] * 2,
            out_specs=[pl.BlockSpec((blk, 2 * cols), lambda i, m: (i, 0))] * n,
        ),
        out_shape=[jax.ShapeDtypeStruct((rows, 2 * cols), F32)] * n,
        compiler_params=params(),
        cost_estimate=BRIEF,
        name="finish",
    )(marks, *mines, *fars)


def pair_swap(x, step, sizes):
    axis, mask = step
    return lax.ppermute(x, axis, [(i, i ^ mask) for i in range(sizes[axis])])


def step_bit(step):
    axis, mask = step
    return (lax.axis_index(axis) // mask) % 2


def chip_steps(sizes):
    along = [("dp", 1 << j) for j in range(sizes["dp"].bit_length() - 1)]
    across = [("key", 2 << j) for j in range(sizes["key"].bit_length() - 2)]
    return along[:1] + across[:1] + along[1:2], along[2:] + across[1:]


def turn(first, i):
    i = i % len(first)
    return first[i:] + first[:i]


def halvings(rows, steps):
    count = 0
    while count < len(steps) and rows % 32 == 0:
        rows //= 2
        count += 1
    return count


def mark_of(steps, count):
    return sum(step_bit(x) << (count - 1 - j) for j, x in enumerate(steps[:count]))


def plus(a, b):
    return (a.astype(F32) + b.astype(F32)).astype(a.dtype)


def tree_sum(parts, steps, count, sizes, ties, small):
    sends = [p[0] for p in parts]
    keeps = [p[1] for p in parts]
    n = len(parts)
    for j in range(len(steps[0])):
        recvs = [pair_swap(sends[i], steps[i][j], sizes) for i in range(n)]
        for i in range(n):
            if j + 1 < count:
                half = keeps[i].shape[0] // 2
                sends[i] = plus(keeps[i][half:], recvs[i][half:])
                keeps[i] = plus(keeps[i][:half], recvs[i][:half])
            else:
                sends[i] = keeps[i] = plus(keeps[i], recvs[i])
        if j in ties:
            (sends, keeps), ties[j] = lax.optimization_barrier(((sends, keeps), ties[j]()))
    mines = keeps
    vector = small()
    turns = list(steps[0])
    for j in reversed(range(count)):
        recvs = [pair_swap(mines[i], steps[i][j], sizes) for i in range(n)]
        vector = plus(vector, pair_swap(vector, turns.pop(0), sizes))
        recvs, vector = lax.optimization_barrier((recvs, vector))
        if j - count in ties:
            recvs, ties[j - count] = lax.optimization_barrier((recvs, ties[j - count]()))
        mines = [jnp.concatenate([m, r], 0) for m, r in zip(mines, recvs)]
    for x in turns:
        vector = plus(vector, pair_swap(vector, x, sizes))
    return mines, vector


def local(
    ray_tokens,
    latents,
    group_ids,
    ln1_gain,
    ln1_shift,
    w_query,
    w_key,
    w_value,
    w_out,
    ln2_gain,
    ln2_shift,
    w_up,
    b_up,
    w_down,
    b_down,
    intrinsics,
    out_grad,
    *,
    sizes,
):
    keys = sizes["key"]
    share = out_grad.shape[0]
    width = ray_tokens.shape[1]
    cols = width // 2
    pairs = cols // PAIR
    chips = keys // 2
    chip_rows = 2 * share
    place = lax.axis_index("key")
    core = place % 2
    chip = place // 2

    def core_swap(x):
        return lax.ppermute(x, "key", [(i, i ^ 1) for i in range(keys)])

    def chip_shift(x, s):
        return lax.ppermute(x, "key", [(i, (i + 2 * s) % keys) for i in range(keys)])

    def own_cols(w):
        return lax.dynamic_slice_in_dim(w, core * cols, cols, 1)

    def far_cols(w):
        return lax.dynamic_slice_in_dim(w, (1 - core) * cols, cols, 1)

    def own_rows(w):
        return lax.dynamic_slice_in_dim(w, core * cols, cols, 0)

    def far_rows(w):
        return lax.dynamic_slice_in_dim(w, (1 - core) * cols, cols, 0)

    gain_one = ln1_gain.astype(F32)
    shift_one = ln1_shift.astype(F32)
    gain_two = ln2_gain.astype(F32)
    shift_two = ln2_shift.astype(F32)
    lookup = group_ids[0][:, None] == jnp.arange(intrinsics.shape[0], dtype=jnp.int32)[None, :]
    carried = (
        latents[0].astype(F32)
        + jnp.dot(lookup.astype(BF), intrinsics, preferred_element_type=F32)
    ).astype(BF)
    tokens = carried.shape[0]
    carried_far = core_swap(carried)
    steps = jnp.arange(keys, dtype=jnp.int32)
    order = ((chip + steps // 2) % chips) * 2 + (core + steps % 2) % 2
    normed, queries = query_call(order, core, ray_tokens, ln1_gain, ln1_shift, w_query, share)
    key_rows, value_rows, key_cols, value_cols = keyval_call(
        core, carried, carried_far, w_key, w_value
    )

    stats, exps, os, sts = [None] * chips, [None] * chips, [None] * chips, [None] * chips
    ordered = queries
    for t in [*range(1, chips), 0]:
        o, st, e = attend_call(
            ordered, key_rows, value_cols, t * chip_rows, chip_rows, "far" if t else "own"
        )
        stats[t], exps[t] = st, e
        if t:
            ordered, o, st = lax.optimization_barrier((ordered, o, st))
        os[t], sts[t] = (chip_shift(o, t), chip_shift(st, t)) if t else (o, st)
    att, low_chip, lse = combine_call(os, sts)
    low_own = low_chip[:share]
    low_far = core_swap(low_chip[share:])
    attended_low = jnp.concatenate(
        [jnp.where(core == 0, low_own, low_far), jnp.where(core == 0, low_far, low_own)], 1
    )
    own_rays = lax.dynamic_slice_in_dim(ray_tokens, place * share, share, 0).astype(F32)
    middle = own_rays + dot(attended_low, w_out)
    normed_two, unit_two, scale_two = norm_forward(middle, gain_two, shift_two)
    normed_two_low = normed_two.astype(BF)
    hidden = dot(normed_two_low, w_up) + b_up.astype(F32)
    active, gelu_back = jax.vjp(jax.nn.gelu, hidden)
    active_low = active.astype(BF)
    output = (middle + dot(active_low, w_down) + b_down.astype(F32)).astype(BF)
    grad_out = out_grad.astype(F32)
    grad_active = lax.optimization_barrier(dot(out_grad, w_down, NT).astype(BF)).astype(F32)
    grad_hidden = gelu_back(grad_active)[0].astype(BF)
    grad_normed_two = dot(grad_hidden, w_up, NT)
    grad_middle_norm, grad_gain_two, grad_shift_two = norm_backward(
        grad_normed_two, unit_two, scale_two, gain_two
    )
    grad_middle = grad_out + grad_middle_norm
    grad_branch = grad_middle.astype(BF)
    do_far = core_swap(dot(grad_branch, far_rows(w_out), NT).astype(BF))
    do_own = dot(grad_branch, own_rows(w_out), NT).astype(BF)
    do_chip = jnp.concatenate([do_own, do_far], 0)
    aux_chip = delta_call(do_chip, att, lse)
    grad_w_down = dot(active_low, out_grad, TN).astype(BF)
    grad_b_down = jnp.sum(grad_out, axis=0)
    grad_w_up = dot(normed_two_low, grad_hidden, TN).astype(BF)
    grad_b_up = jnp.sum(grad_hidden.astype(F32), axis=0)
    grad_w_out = dot(attended_low, grad_branch, TN).astype(BF)
    branch_grads = lax.psum((grad_w_out, grad_w_up, grad_w_down), ("dp", "key"))

    first, rest = chip_steps(sizes)
    steps = [turn(first, i) + rest for i in range(4)]
    count = halvings(width, steps[0])
    marks = jnp.stack([mark_of(x, count) for x in steps[:3]] + [core]).astype(jnp.int32)

    branch_sums = jnp.concatenate(
        [x.reshape(-1, width) for x in (grad_gain_two, grad_shift_two, grad_b_down, grad_b_up)], 0
    )
    branch_sums = jnp.pad(branch_sums, ((0, -branch_sums.shape[0] % 8), (0, 0)))

    def rest():
        dos, auxs = [do_chip], [aux_chip]
        for t in range(1, chips):
            dos.append(chip_shift(do_chip, chips - t))
            auxs.append(chip_shift(aux_chip, chips - t))

        def back(t, carry, pair0, count, fresh, name):
            return backward_call(
                exps[t],
                dos[t],
                queries,
                stats[t],
                auxs[t],
                key_cols,
                value_rows,
                carry,
                t * chip_rows,
                pair0,
                count,
                fresh,
                name,
            )

        dq_first, *carry = back(0, None, 0, 1, 0, "own_first")
        parts = []
        for t in range(1, chips):
            dq, *carry = back(t, carry, 0, pairs, 1 if t == 1 else pairs, "far")
            parts.append(chip_shift(dq, t))
        dq_rest, *carry = back(0, carry, 1, pairs - 1, pairs, "own_rest")
        keys_own, keys_far, values_own, values_far, key_send, key_keep, value_send, value_keep = (
            keyval_grad_call(marks, count, carried, carried_far, *carry)
        )
        queries_own, queries_far, query_send, query_keep = query_grad_call(
            marks, count, normed, dq_first, dq_rest, parts
        )
        queries_far = core_swap(queries_far)
        rays_grad, norm_sums = rays_grad_call(
            jnp.stack([core, place]),
            queries_own,
            queries_far,
            w_query,
            ray_tokens,
            grad_middle,
            ln1_gain,
            ln1_shift,
        )
        tokens_far = [core_swap(x) for x in (keys_far, values_far)]
        late = {}

        def small_sum():
            small = jnp.concatenate([norm_sums, branch_sums, ties[2]], 0)
            return small + core_swap(small)

        def tokens_back():
            grad_carried, grad_table = carried_grad_call(
                core,
                group_ids,
                ties[0][0],
                ties[0][2],
                ties[0][1],
                ties[0][3],
                w_key,
                w_value,
                intrinsics.shape[0],
            )
            late["carried"] = grad_carried
            return grad_table

        ties = {
            0: lambda: [keys_own, values_own] + tokens_far + [norm_sums],
            2: tokens_back,
        }
        sums, small = tree_sum(
            [(query_send, query_keep), (key_send, key_keep), (value_send, value_keep)],
            steps[:3],
            count,
            sizes,
            ties,
            small_sum,
        )
        grad_carried, grad_table = late["carried"], ties[2]
        attention_grads = finish_call(marks, count, sums, [core_swap(g) for g in sums])
        return rays_grad, grad_carried, attention_grads, small

    shapes = jax.eval_shape(rest)
    rays_grad, grad_carried, attention_grads, small = lax.cond(
        group_ids[0, 0] >= 0,
        rest,
        lambda: jax.tree.map(lambda x: jnp.zeros(x.shape, x.dtype), shapes),
    )
    branch_grads = [x.astype(F32) for x in branch_grads]
    up_rows = b_up.shape[0] // width
    table_row = 8 + branch_sums.shape[0]
    spots = [
        small[0],
        small[1],
        small[8],
        small[9],
        small[11 : 11 + up_rows].reshape(-1),
        small[10],
        small[table_row:],
    ]
    return (
        output,
        rays_grad,
        grad_carried[None],
        spots[0],
        spots[1],
        attention_grads[0],
        attention_grads[1],
        attention_grads[2],
        branch_grads[0],
        spots[2],
        spots[3],
        branch_grads[1],
        spots[4],
        branch_grads[2],
        spots[5],
        spots[6],
    )


def solution(mesh):
    rows = P(("dp", "key"), None)
    placed = (P("dp", None), P("dp", "key", None), P("dp", "key")) + (P(),) * 13 + (rows,)
    return jax.shard_map(
        functools.partial(local, sizes=dict(mesh.shape)),
        mesh=mesh,
        in_specs=placed,
        out_specs=(rows, rows, P("dp", "key", None)) + (P(),) * 13,
        check_vma=False,
    )
```

```python
import functools

import jax
import jax.numpy as jnp
from jax import lax
from jax.experimental import pallas as pl
from jax.experimental.pallas import tpu as pltpu
from jax.sharding import PartitionSpec as P

H = 12
HD = 64
PAIR = 2 * HD
EPSILON = 1e-05
BF = jnp.bfloat16
F32 = jnp.float32
LOG2E = 1.4426950408889634
LN2 = 0.6931471805599453
SAFE_BOUND = 60.0
GELU_A = 0.7978845608028654
GELU_B = 0.044715
BRIEF = pl.CostEstimate(flops=1000, bytes_accessed=1000, transcendentals=0)
VMEM = 60 * 1024 * 1024


def dot(a, b, dims=((1,), (0,))):
    return lax.dot_general(a, b, (dims, ((), ())), preferred_element_type=F32)


NT = ((1,), (1,))
TN = ((0,), (0,))


def params(**kw):
    return pltpu.CompilerParams(vmem_limit_bytes=VMEM, **kw)


def head_half(x, h, axis=1):
    i = lax.broadcasted_iota(jnp.int32, x.shape, axis)
    return jnp.where((i < HD) == (h == 0), x, jnp.zeros_like(x))


def norm_forward(values, gain_vec, shift_vec):
    centre = values - jnp.mean(values, axis=-1, keepdims=True)
    scaled = lax.rsqrt(jnp.mean(centre * centre, axis=-1, keepdims=True) + EPSILON)
    unit_rows = centre * scaled
    return (unit_rows * gain_vec + shift_vec, unit_rows, scaled)


def norm_backward(grad_rows, unit_rows, scaled, gain_vec):
    grad_unit = grad_rows * gain_vec
    centred_grad = (
        grad_unit
        - jnp.mean(grad_unit, axis=-1, keepdims=True)
        - unit_rows * jnp.mean(grad_unit * unit_rows, axis=-1, keepdims=True)
    )
    return (
        scaled * centred_grad,
        jnp.sum(grad_rows * unit_rows, axis=0),
        jnp.sum(grad_rows, axis=0),
    )


def query_kernel(order, rays, lines, wq, normed, q):
    n, _, _ = norm_forward(rays[...].astype(F32), lines[0:1, :], lines[1:2, :])
    n = n.astype(BF)
    normed[...] = n
    q[...] = (dot(n, wq[...]) * (HD**-0.5 * LOG2E)).astype(BF)


def query_call(order, core, rays, lines, wq, share):
    rows, width = rays.shape
    cols = width // 2
    blocks = rows // share
    pre = jnp.concatenate([order, core[None]])
    return pl.pallas_call(
        query_kernel,
        grid_spec=pltpu.PrefetchScalarGridSpec(
            num_scalar_prefetch=1,
            grid=(blocks,),
            in_specs=[
                pl.BlockSpec((share, width), lambda i, o: (o[i], 0)),
                pl.BlockSpec(lines.shape, lambda i, o: (0, 0)),
                pl.BlockSpec((width, cols), lambda i, o: (0, o[blocks])),
            ],
            out_specs=[
                pl.BlockSpec((share, width), lambda i, o: (i, 0)),
                pl.BlockSpec((share, cols), lambda i, o: (i, 0)),
            ],
        ),
        out_shape=[
            jax.ShapeDtypeStruct((rows, width), BF),
            jax.ShapeDtypeStruct((rows, cols), BF),
        ],
        compiler_params=params(),
        cost_estimate=BRIEF,
        name="rays_query",
    )(pre, rays, lines, wq)


def keyval_kernel(core, own, far, wk, wv, k, v, kt, vt):
    x = jnp.where(pl.program_id(0) < pl.num_programs(0) // 2, own[...], far[...])
    kk = dot(x, wk[...]).astype(BF)
    vv = dot(x, wv[...]).astype(BF)
    k[...] = kk
    v[...] = vv
    kt[...] = kk.T
    vt[...] = vv.T


def keyval_call(core, own, far, wk, wv):
    rows, width = own.shape
    rows = 2 * rows
    cols = width // 2
    blk = 512
    half = rows // blk // 2
    return pl.pallas_call(
        keyval_kernel,
        grid_spec=pltpu.PrefetchScalarGridSpec(
            num_scalar_prefetch=1,
            grid=(rows // blk,),
            in_specs=[
                pl.BlockSpec((blk, width), lambda i, o: (jnp.minimum(i, half - 1), 0)),
                pl.BlockSpec((blk, width), lambda i, o: (jnp.maximum(i - half, 0), 0)),
                pl.BlockSpec((width, cols), lambda i, o: (0, o[0])),
                pl.BlockSpec((width, cols), lambda i, o: (0, o[0])),
            ],
            out_specs=[
                pl.BlockSpec((blk, cols), lambda i, o: (i, 0)),
                pl.BlockSpec((blk, cols), lambda i, o: (i, 0)),
                pl.BlockSpec((cols, blk), lambda i, o: (0, i)),
                pl.BlockSpec((cols, blk), lambda i, o: (0, i)),
            ],
        ),
        out_shape=[
            jax.ShapeDtypeStruct((rows, cols), BF),
            jax.ShapeDtypeStruct((rows, cols), BF),
            jax.ShapeDtypeStruct((cols, rows), BF),
            jax.ShapeDtypeStruct((cols, rows), BF),
        ],
        compiler_params=params(),
        cost_estimate=BRIEF,
        name="keys_values",
    )(core[None], own, far, wk, wv)


def attend_kernel(qb, k, vt, o, st, e, km, kn, spare, *, tc):
    tokens = k.shape[0]
    rb = qb.shape[0]
    chunks = [slice(c, c + tc) for c in range(0, tokens, tc)]

    @pl.when(pl.program_id(1) == 0)
    def _():
        for h in (0, 1):
            kh = head_half(k[...], h)
            km[h] = kh
            kf = kh.astype(F32)
            top = jnp.max(jnp.sum(kf * kf, axis=1, keepdims=True), axis=0, keepdims=True)
            kn[h : h + 1, :] = jnp.broadcast_to(top, (1, PAIR))

    qf = qb[...].astype(F32)
    bound = jnp.float32(0)
    for h in (0, 1):
        qn = jnp.max(jnp.sum(head_half(qf * qf, h), axis=1, keepdims=True), axis=0, keepdims=True)
        bound = jnp.maximum(bound, jnp.max(qn * kn[h : h + 1, :]))
    small = bound < SAFE_BOUND * SAFE_BOUND

    def scores(h, r):
        return dot(km[h, r, :], qb[...], NT)

    def mixed(h, r, low):
        cols = jnp.concatenate([vt[h * HD : (h + 1) * HD, r], jnp.ones((HD, tc), BF)], 0)
        return dot(cols, low)

    def finish(acc, shifts):
        outs = []
        for h in (0, 1):
            total = acc[h][HD : HD + 1]
            outs.append(acc[h][:HD] / total)
            st[h : h + 1, :] = shifts[h]
            st[h + 2 : h + 3, :] = shifts[h] + jnp.log2(total)
        o[...] = jnp.concatenate(outs, 0).T.astype(BF)

    @pl.when(small)
    def _():
        items = [(h, r) for h in (0, 1) for r in chunks]
        acc = [0.0, 0.0]
        ready = [scores(*items[0])]
        waiting = []
        for n, (h, r) in enumerate(items):
            if n + 1 < len(items):
                ready.append(scores(*items[n + 1]))
            low = jnp.exp2(ready.pop(0)).astype(BF)
            e[h, r, :] = low
            if waiting:
                g, *rest = waiting.pop()
                acc[g] = acc[g] + mixed(g, *rest)
            waiting.append((h, r, low))
        g, *rest = waiting.pop()
        acc[g] = acc[g] + mixed(g, *rest)
        finish(acc, [jnp.zeros((1, rb), F32)] * 2)

    @pl.when(jnp.logical_not(small))
    def _():
        acc = [0.0, 0.0]
        shifts = []
        for h in (0, 1):
            m = None
            for r in chunks:
                s = scores(h, r)
                spare[r, :] = s
                mc = jnp.max(s, axis=0, keepdims=True)
                m = mc if m is None else jnp.maximum(m, mc)
            shifts.append(m)
            for r in chunks:
                low = jnp.exp2(spare[r, :] - m).astype(BF)
                e[h, r, :] = low
                acc[h] = acc[h] + mixed(h, r, low)
        finish(acc, shifts)


def attend_call(q, k, vt, first_row, rows, name):
    tokens, cols = k.shape
    pairs = cols // PAIR
    rb = min(512, rows)
    off = first_row // rb
    return pl.pallas_call(
        functools.partial(attend_kernel, tc=min(1024, tokens)),
        grid=(pairs, rows // rb),
        in_specs=[
            pl.BlockSpec((rb, PAIR), lambda p, i: (i + off, p)),
            pl.BlockSpec((tokens, PAIR), lambda p, i: (0, p)),
            pl.BlockSpec((PAIR, tokens), lambda p, i: (p, 0)),
        ],
        out_specs=[
            pl.BlockSpec((rb, PAIR), lambda p, i: (i, p)),
            pl.BlockSpec((8, rb), lambda p, i: (p, i)),
            pl.BlockSpec((2, tokens, rb), lambda p, i: (p, 0, i)),
        ],
        out_shape=[
            jax.ShapeDtypeStruct((rows, cols), BF),
            jax.ShapeDtypeStruct((8 * pairs, rows), F32),
            jax.ShapeDtypeStruct((2 * pairs, tokens, rows), BF),
        ],
        scratch_shapes=[
            pltpu.VMEM((2, tokens, PAIR), BF),
            pltpu.VMEM((8, PAIR), F32),
            pltpu.VMEM((tokens, rb), F32),
        ],
        compiler_params=params(),
        cost_estimate=BRIEF,
        name=f"attend_{name}",
    )(q, k, vt)


def spread(rows2):
    rows = rows2.shape[1]
    return jnp.concatenate([jnp.broadcast_to(rows2[h : h + 1, :], (HD, rows)) for h in (0, 1)], 0)


def combine_kernel(*refs, parts, pairs):
    os, sts = refs[:parts], refs[parts : 2 * parts]
    att, low_own, low_send, lse = refs[2 * parts :]
    first = pl.program_id(0) < pl.num_programs(0) // 2
    lows = []
    for p in range(pairs):
        c = slice(p * PAIR, (p + 1) * PAIR)
        ls = [s[8 * p + 2 : 8 * p + 4, :] for s in sts]
        top = functools.reduce(jnp.maximum, ls)
        tot = top + jnp.log2(sum(jnp.exp2(x - top) for x in ls))
        acc = 0.0
        for o, x in zip(os, ls):
            acc = acc + o[:, c].astype(F32) * spread(jnp.exp2(x - tot)).T
        att[:, c] = acc
        lows.append(acc.astype(BF))
        lse[8 * p : 8 * p + 2, :] = tot
    low = jnp.concatenate(lows, 1)

    @pl.when(first)
    def _():
        low_own[...] = low

    @pl.when(jnp.logical_not(first))
    def _():
        low_send[...] = low


def combine_call(os, sts):
    parts = len(os)
    rows, cols = os[0].shape
    pairs = cols // PAIR
    blk = min(256, rows // 2)
    half = rows // blk // 2
    wide = pl.BlockSpec((blk, cols), lambda i: (i, 0))
    flat = pl.BlockSpec((8 * pairs, blk), lambda i: (0, i))
    return pl.pallas_call(
        functools.partial(combine_kernel, parts=parts, pairs=pairs),
        grid=(rows // blk,),
        in_specs=[wide] * parts + [flat] * parts,
        out_specs=[
            wide,
            pl.BlockSpec((blk, cols), lambda i: (jnp.minimum(i, half - 1), 0)),
            pl.BlockSpec((blk, cols), lambda i: (jnp.maximum(i - half, 0), 0)),
            flat,
        ],
        out_shape=[
            jax.ShapeDtypeStruct((rows, cols), F32),
            jax.ShapeDtypeStruct((rows // 2, cols), BF),
            jax.ShapeDtypeStruct((rows // 2, cols), BF),
            jax.ShapeDtypeStruct((8 * pairs, rows), F32),
        ],
        compiler_params=params(),
        cost_estimate=BRIEF,
        name="combine",
    )(*os, *sts)


def delta_kernel(own, far, att, lse, do, aux, *, pairs):
    both = jnp.where(pl.program_id(0) < pl.num_programs(0) // 2, own[...], far[...])
    do[...] = both
    for p in range(pairs):
        c = slice(p * PAIR, (p + 1) * PAIR)
        prod = (both[:, c].astype(F32) * att[:, c]).T
        aux[8 * p : 8 * p + 2, :] = lse[8 * p : 8 * p + 2, :]
        for h in (0, 1):
            aux[8 * p + 2 + h : 8 * p + 3 + h, :] = jnp.sum(
                prod[h * HD : (h + 1) * HD, :], axis=0, keepdims=True
            )


def delta_call(own, far, att, lse):
    rows, cols = att.shape
    pairs = cols // PAIR
    blk = min(256, rows // 2)
    half = rows // blk // 2
    wide = pl.BlockSpec((blk, cols), lambda i: (i, 0))
    flat = pl.BlockSpec((8 * pairs, blk), lambda i: (0, i))
    return pl.pallas_call(
        functools.partial(delta_kernel, pairs=pairs),
        grid=(2 * half,),
        in_specs=[
            pl.BlockSpec((blk, cols), lambda i: (jnp.minimum(i, half - 1), 0)),
            pl.BlockSpec((blk, cols), lambda i: (jnp.maximum(i - half, 0), 0)),
            wide,
            flat,
        ],
        out_specs=[wide, flat],
        out_shape=[
            jax.ShapeDtypeStruct((rows, cols), BF),
            jax.ShapeDtypeStruct((8 * pairs, rows), F32),
        ],
        compiler_params=params(),
        cost_estimate=BRIEF,
        name="deltas",
    )(own, far, att, lse)


def mlp_kernel(
    spots, low_own, low_far, rays, wo_own, wo_far, w_up, w_down, lines, og,
    mixed, grad_middle, do_own, do_far, active_low, grad_hidden, normed_low, branch, sums,
):
    gain_row = lines[2:3, :]
    up_rows = w_up.shape[1] // w_up.shape[0]
    b_up = jnp.concatenate([lines[5 + j : 6 + j, :] for j in range(up_rows)], 1)
    middle = rays[...].astype(F32) + dot(low_own[...], wo_own[...]) + dot(low_far[...], wo_far[...])
    normed, unit, scale = norm_forward(middle, gain_row, lines[3:4, :])
    normed = normed.astype(BF)
    normed_low[...] = normed
    hidden = dot(normed, w_up[...]) + b_up
    square = hidden * hidden
    t = jnp.tanh(GELU_A * hidden * (1.0 + GELU_B * square))
    active = (0.5 * hidden * (1.0 + t)).astype(BF)
    active_low[...] = active
    mixed[...] = (middle + dot(active, w_down[...]) + lines[4:5, :]).astype(BF)
    grad_active = dot(og[...], w_down[...], NT).astype(BF).astype(F32)
    slope = 0.5 * (1.0 + t) + (0.5 * GELU_A) * hidden * (1.0 - t * t) * (1.0 + 3.0 * GELU_B * square)
    gh = (grad_active * slope).astype(BF)
    grad_hidden[...] = gh
    back, grad_gain, grad_shift = norm_backward(dot(gh, w_up[...], NT), unit, scale, gain_row)
    grad_out = og[...].astype(F32)
    gm = grad_out + back
    grad_middle[...] = gm
    gb = gm.astype(BF)
    branch[...] = gb
    do_far[...] = dot(gb, wo_far[...], NT).astype(BF)
    do_own[...] = dot(gb, wo_own[...], NT).astype(BF)

    @pl.when(pl.program_id(0) == 0)
    def _():
        sums[...] = jnp.zeros_like(sums)

    width = gm.shape[1]
    sums[0:1, :] += grad_gain[None]
    sums[1:2, :] += grad_shift[None]
    sums[2:3, :] += jnp.sum(grad_out, axis=0, keepdims=True)
    up = jnp.sum(gh.astype(F32), axis=0, keepdims=True)
    for j in range(up.shape[1] // width):
        sums[3 + j : 4 + j, :] += up[:, j * width : (j + 1) * width]


def mlp_call(spots, low_own, low_far, rays, w_out, w_up, w_down, lines, og):
    rows, width = og.shape
    cols = low_own.shape[1]
    hidden = w_up.shape[1]
    blk = min(256, rows)
    n = rows // blk
    wide = lambda c: pl.BlockSpec((blk, c), lambda i, o: (i, 0))
    fixed = lambda *d: pl.BlockSpec(d, lambda i, o: (0, 0))
    out = lambda c, t: jax.ShapeDtypeStruct((rows, c), t)
    return pl.pallas_call(
        mlp_kernel,
        grid_spec=pltpu.PrefetchScalarGridSpec(
            num_scalar_prefetch=1,
            grid=(n,),
            in_specs=[
                wide(cols),
                wide(cols),
                pl.BlockSpec((blk, width), lambda i, o: (o[1] * n + i, 0)),
                pl.BlockSpec((cols, width), lambda i, o: (o[0], 0)),
                pl.BlockSpec((cols, width), lambda i, o: (1 - o[0], 0)),
                fixed(width, hidden),
                fixed(hidden, width),
                fixed(*lines.shape),
                wide(width),
            ],
            out_specs=[
                wide(width),
                wide(width),
                wide(cols),
                wide(cols),
                wide(hidden),
                wide(hidden),
                wide(width),
                wide(width),
                fixed(8, width),
            ],
        ),
        out_shape=[
            out(width, BF),
            out(width, F32),
            out(cols, BF),
            out(cols, BF),
            out(hidden, BF),
            out(hidden, BF),
            out(width, BF),
            out(width, BF),
            jax.ShapeDtypeStruct((8, width), F32),
        ],
        compiler_params=params(),
        cost_estimate=BRIEF,
        name="mlp",
    )(
        spots,
        low_own,
        low_far,
        rays,
        w_out,
        w_out,
        w_up,
        w_down,
        lines,
        og,
    )


def backward_kernel(e, do, q, st, aux, kt, v, *refs, pair0, fresh):
    dq, dk, dv = refs[-3:]

    @pl.when(pl.program_id(1) == 0)
    def _():
        if len(refs) == 3:
            dk[...] = jnp.zeros_like(dk)
            dv[...] = jnp.zeros_like(dv)
        else:
            new = pl.program_id(0) + pair0 >= fresh
            dk[...] = jnp.where(new, 0.0, refs[0][...])
            dv[...] = jnp.where(new, 0.0, refs[1][...])

    scw = spread(jnp.exp2(st[0:2, :] - aux[0:2, :]))
    sct = scw.T
    dos = (do[...].astype(F32) * sct).astype(BF)
    qs = (q[...].astype(F32) * (sct * LN2)).astype(BF)
    grads = []
    for h in (0, 1):
        dp = dot(head_half(v[...], h), do[...], NT)
        grads.append((e[h].astype(F32) * (dp - aux[h + 2 : h + 3, :])).astype(BF))
    dqt = jnp.concatenate([dot(kt[h * HD : (h + 1) * HD, :], grads[h]) for h in (0, 1)], 0)
    dq[...] = (dqt * (scw * HD**-0.5)).T.astype(BF)
    both = lambda a: jnp.concatenate([head_half(a, 0), head_half(a, 1)], 0)
    dv[...] += dot(jnp.concatenate([e[0], e[1]], 1), both(dos))
    dk[...] += dot(jnp.concatenate(grads, 1), both(qs))


def backward_call(e, do, q, st, aux, kt, v, carry, first_row, pair0, pairs, fresh, name):
    rows = do.shape[0]
    tokens, cols = v.shape
    rb = min(256, rows)
    off = first_row // rb
    whole = pl.BlockSpec((tokens, PAIR), lambda p, i: (0, p + pair0))
    carry = () if carry is None else tuple(carry)
    return pl.pallas_call(
        functools.partial(backward_kernel, pair0=pair0, fresh=fresh),
        grid=(pairs, rows // rb),
        in_specs=[
            pl.BlockSpec((2, tokens, rb), lambda p, i: (p + pair0, 0, i)),
            pl.BlockSpec((rb, PAIR), lambda p, i: (i, p + pair0)),
            pl.BlockSpec((rb, PAIR), lambda p, i: (i + off, p + pair0)),
            pl.BlockSpec((8, rb), lambda p, i: (p + pair0, i)),
            pl.BlockSpec((8, rb), lambda p, i: (p + pair0, i)),
            pl.BlockSpec((PAIR, tokens), lambda p, i: (p + pair0, 0)),
            pl.BlockSpec((tokens, PAIR), lambda p, i: (0, p + pair0)),
        ]
        + [whole] * len(carry),
        out_specs=[pl.BlockSpec((rb, PAIR), lambda p, i: (i, p)), whole, whole],
        out_shape=[
            jax.ShapeDtypeStruct((rows, pairs * PAIR), BF),
            jax.ShapeDtypeStruct((tokens, cols), F32),
            jax.ShapeDtypeStruct((tokens, cols), F32),
        ],
        input_output_aliases={7: 1, 8: 2} if carry else {},
        compiler_params=params(),
        cost_estimate=BRIEF,
        name=f"backward_{name}",
    )(e, do, q, st, aux, kt, v, *carry)


def halves(acc, mark, count, send, keep):
    blocks = 1 << count
    size = acc.shape[0] // blocks
    for j in range(blocks):
        dst = keep if j < blocks // 2 else send
        at = j % (blocks // 2) * size
        rows = pl.ds(pl.multiple_of((j ^ mark) * size, 16), size)
        dst[at : at + size, :] = acc[rows, :].astype(BF)


def keyval_grad_kernel(marks, x_own, x_far, dk, dv, ko, kf, vo, vf, ks, kk, vs, vk, acck, accv, *, count):
    i = pl.program_id(0)
    n = pl.num_programs(0)

    @pl.when(i == 0)
    def _():
        acck[...] = jnp.zeros_like(acck)
        accv[...] = jnp.zeros_like(accv)

    a = dk[...].astype(BF)
    b = dv[...].astype(BF)

    @pl.when(i < n // 2)
    def _():
        kf[...] = a
        vf[...] = b

    @pl.when(i >= n // 2)
    def _():
        ko[...] = a
        vo[...] = b

    x = jnp.where(i < n // 2, x_far[...], x_own[...])
    acck[...] += dot(x, a, TN)
    accv[...] += dot(x, b, TN)

    @pl.when(i == n - 1)
    def _():
        halves(acck, marks[1], count, ks, kk)
        halves(accv, marks[2], count, vs, vk)


def keyval_grad_call(marks, count, own, far, dk, dv):
    rows, width = own.shape
    rows = 2 * rows
    cols = dk.shape[1]
    blk = 512
    half = rows // blk // 2
    turn_rows = lambda i: ((i + half) % (2 * half), 0)
    wide = pl.BlockSpec((blk, cols), turn_rows)
    own_at = lambda c: pl.BlockSpec((blk, c), lambda i: (jnp.maximum(i - half, 0), 0))
    far_at = lambda c: pl.BlockSpec((blk, c), lambda i: (jnp.minimum(i, half - 1), 0))
    part = pl.BlockSpec((width // 2, cols), lambda i: (0, 0))
    return pl.pallas_call(
        functools.partial(keyval_grad_kernel, count=count),
        grid=(2 * half,),
        in_specs=[
            pl.BlockSpec(memory_space=pltpu.SMEM),
            own_at(width),
            far_at(width),
            wide,
            wide,
        ],
        out_specs=[own_at(cols), far_at(cols)] * 2 + [part] * 4,
        out_shape=[jax.ShapeDtypeStruct((rows // 2, cols), BF)] * 4
        + [jax.ShapeDtypeStruct((width // 2, cols), BF)] * 4,
        scratch_shapes=[pltpu.VMEM((width, cols), F32)] * 2,
        compiler_params=params(),
        cost_estimate=BRIEF,
        name="keyval_grad",
    )(marks, own, far, dk, dv)


def query_grad_kernel(marks, x, d0, d1, *refs, parts, count):
    own, far, send, keep = refs[-5:-1]
    acc = refs[-1]
    i = pl.program_id(0)
    a = jnp.concatenate([d0[...], d1[...]], 1)
    if parts:
        a = sum((r[...].astype(F32) for r in refs[:parts]), a.astype(F32)).astype(BF)
    g = dot(x[...], a, TN)

    @pl.when(i == 0)
    def _():
        own[...] = a
        acc[...] = g

    @pl.when(i == 1)
    def _():
        far[...] = a
        acc[...] += g
        halves(acc, marks[0], count, send, keep)


def query_grad_call(marks, count, x, d0, d1, parts, sends):
    rows = d0.shape[0]
    cols = d0.shape[1] + d1.shape[1]
    width = x.shape[1]
    blk = rows // 2
    k = len(sends)
    anywhere = pl.BlockSpec(memory_space=pl.ANY)
    wide = lambda c: pl.BlockSpec((blk, c), lambda i: (i, 0))
    fixed = pl.BlockSpec((blk, cols), lambda i: (0, 0))
    part = pl.BlockSpec((width // 2, cols), lambda i: (0, 0))
    return pl.pallas_call(
        functools.partial(query_grad_kernel, parts=len(parts), count=count),
        grid=(2,),
        in_specs=[pl.BlockSpec(memory_space=pltpu.SMEM), wide(width), wide(d0.shape[1]), wide(d1.shape[1])]
        + [wide(cols)] * len(parts)
        + [anywhere] * k,
        out_specs=[anywhere] * k + [fixed, fixed, part, part],
        out_shape=[jax.ShapeDtypeStruct(y.shape, y.dtype) for y in sends]
        + [jax.ShapeDtypeStruct((blk, cols), BF)] * 2
        + [jax.ShapeDtypeStruct((width // 2, cols), BF)] * 2,
        scratch_shapes=[pltpu.VMEM((width, cols), F32)],
        input_output_aliases={4 + len(parts) + i: i for i in range(k)},
        compiler_params=params(),
        cost_estimate=BRIEF,
        name="query_grad",
    )(marks, x, d0, d1, *parts, *sends)


def carried_grad_kernel(core, ids, ko, kf, vo, vf, wko, wkf, wvo, wvf, out, table):
    acc = dot(ko[...], wko[...], NT) + dot(kf[...], wkf[...], NT)
    acc += dot(vo[...], wvo[...], NT) + dot(vf[...], wvf[...], NT)
    out[...] = acc
    groups = table.shape[0]
    hot = lax.broadcasted_iota(jnp.int32, (groups, ids.shape[1]), 0) == ids[...]
    hot = hot.astype(F32).astype(BF)
    high = acc.astype(BF)
    rest = (acc - high.astype(F32)).astype(BF)

    @pl.when(pl.program_id(0) == 0)
    def _():
        table[...] = jnp.zeros_like(table)

    table[...] += dot(hot, high) + dot(hot, rest)


def carried_grad_call(core, ids, ko, kf, vo, vf, wk, wv, groups):
    rows, cols = ko.shape
    width = wk.shape[0]
    blk = 256
    wide = pl.BlockSpec((blk, cols), lambda i, o: (i, 0))
    own = pl.BlockSpec((width, cols), lambda i, o: (0, o[0]))
    far = pl.BlockSpec((width, cols), lambda i, o: (0, 1 - o[0]))
    return pl.pallas_call(
        carried_grad_kernel,
        grid_spec=pltpu.PrefetchScalarGridSpec(
            num_scalar_prefetch=1,
            grid=(rows // blk,),
            in_specs=[pl.BlockSpec((1, blk), lambda i, o: (0, i))] + [wide] * 4 + [own, far, own, far],
            out_specs=[
                pl.BlockSpec((blk, width), lambda i, o: (i, 0)),
                pl.BlockSpec((groups, width), lambda i, o: (0, 0)),
            ],
        ),
        out_shape=[
            jax.ShapeDtypeStruct((rows, width), F32),
            jax.ShapeDtypeStruct((groups, width), F32),
        ],
        compiler_params=params(),
        cost_estimate=BRIEF,
        name="carried_grad",
    )(core[None], ids, ko, kf, vo, vf, wk, wk, wv, wv)


def rays_grad_kernel(spots, dqo, dqf, wo, wf, rays, middle, lines, out, sums):
    g = dot(dqo[...], wo[...], NT) + dot(dqf[...], wf[...], NT)
    gain_row = lines[0:1, :]
    _, unit, scale = norm_forward(rays[...].astype(F32), gain_row, lines[1:2, :])
    back, grad_gain, grad_shift = norm_backward(g, unit, scale, gain_row)
    out[...] = middle[...] + back

    @pl.when(pl.program_id(0) == 0)
    def _():
        sums[...] = jnp.zeros_like(sums)

    sums[0:1, :] += grad_gain[None]
    sums[1:2, :] += grad_shift[None]


def rays_grad_call(spots, dqo, dqf, w, rays, middle, lines):
    rows, cols = dqo.shape
    width = w.shape[0]
    blk = min(256, rows)
    n = rows // blk
    wide = lambda c: pl.BlockSpec((blk, c), lambda i, o: (i, 0))
    return pl.pallas_call(
        rays_grad_kernel,
        grid_spec=pltpu.PrefetchScalarGridSpec(
            num_scalar_prefetch=1,
            grid=(n,),
            in_specs=[
                wide(cols),
                wide(cols),
                pl.BlockSpec((width, cols), lambda i, o: (0, o[0])),
                pl.BlockSpec((width, cols), lambda i, o: (0, 1 - o[0])),
                pl.BlockSpec((blk, width), lambda i, o: (o[1] * n + i, 0)),
                wide(width),
                pl.BlockSpec(lines.shape, lambda i, o: (0, 0)),
            ],
            out_specs=[wide(width), pl.BlockSpec((8, width), lambda i, o: (0, 0))],
        ),
        out_shape=[
            jax.ShapeDtypeStruct((rows, width), F32),
            jax.ShapeDtypeStruct((8, width), F32),
        ],
        compiler_params=params(),
        cost_estimate=BRIEF,
        name="rays_grad",
    )(spots, dqo, dqf, w, w, rays, middle, lines)


def finish_kernel(marks, *refs, n, inner, size):
    core = marks[n]
    k = (len(refs) - 3 * n) // 2
    mines, fars, whole = refs[:n], refs[n : 2 * n], refs[2 * n : 2 * n + k]
    outs, wide = refs[2 * n + k : 3 * n + k], refs[3 * n + k :]
    for i, (mine, far, out) in enumerate(zip(mines, fars, outs)):
        cols = mine.shape[1]
        for j in range(inner):
            src = pl.ds(pl.multiple_of((j ^ (marks[i] & (inner - 1))) * size, 16), size)
            dst = slice(j * size, (j + 1) * size)
            out[dst, pl.ds(pl.multiple_of(core * cols, 128), cols)] = mine[src, :].astype(F32)
            out[dst, pl.ds(pl.multiple_of((1 - core) * cols, 128), cols)] = far[src, :].astype(F32)
    for src, dst in zip(whole, wide):
        dst[...] = src[...].astype(F32)


def finish_call(marks, count, mines, fars, whole):
    rows, cols = mines[0].shape
    n = len(mines)
    outer = min(2, count)
    inner = 1 << (count - outer)
    size = rows >> count
    blk = size * inner

    def place(k):
        return pl.BlockSpec((blk, cols), lambda i, m: (i ^ (m[k] // inner), 0))

    cuts = [pl.BlockSpec((x.shape[0] >> outer, x.shape[1]), lambda i, m: (i, 0)) for x in whole]
    return pl.pallas_call(
        functools.partial(finish_kernel, n=n, inner=inner, size=size),
        grid_spec=pltpu.PrefetchScalarGridSpec(
            num_scalar_prefetch=1,
            grid=(1 << outer,),
            in_specs=[place(k) for k in range(n)] * 2 + cuts,
            out_specs=[pl.BlockSpec((blk, 2 * cols), lambda i, m: (i, 0))] * n + cuts,
        ),
        out_shape=[jax.ShapeDtypeStruct((rows, 2 * cols), F32)] * n
        + [jax.ShapeDtypeStruct(x.shape, F32) for x in whole],
        compiler_params=params(),
        cost_estimate=BRIEF,
        name="finish",
    )(marks, *mines, *fars, *whole)


def pair_swap(x, step, sizes):
    axis, mask = step
    return lax.ppermute(x, axis, [(i, i ^ mask) for i in range(sizes[axis])])


def step_bit(step):
    axis, mask = step
    return (lax.axis_index(axis) // mask) % 2


def chip_steps(sizes):
    along = [("dp", 1 << j) for j in range(sizes["dp"].bit_length() - 1)]
    across = [("key", 2 << j) for j in range(sizes["key"].bit_length() - 2)]
    return along[:1] + across[:1] + along[1:2], along[2:] + across[1:]


def turn(first, i):
    i = i % len(first)
    return first[i:] + first[:i]


def halvings(rows, steps):
    count = 0
    while count < len(steps) and rows % 32 == 0:
        rows //= 2
        count += 1
    return count


def mark_of(steps, count):
    return sum(step_bit(x) << (count - 1 - j) for j, x in enumerate(steps[:count]))


def plus(a, b):
    return (a.astype(F32) + b.astype(F32)).astype(a.dtype)


def plus_after_kernel(a, b, _, out):
    out[...] = plus(a[...], b[...])


def plus_after(a, b, after):
    whole = pl.BlockSpec(memory_space=pltpu.VMEM)
    return pl.pallas_call(
        plus_after_kernel,
        in_specs=[whole, whole, pl.BlockSpec(memory_space=pl.ANY)],
        out_specs=whole,
        out_shape=jax.ShapeDtypeStruct(a.shape, a.dtype),
        compiler_params=params(),
        cost_estimate=BRIEF,
        name="plus_after",
    )(a, b, after)


def tree_scatter(parts, steps, count, sizes, beside):
    sends = [p[0] for p in parts]
    keeps = [p[1] for p in parts]
    for j in range(len(steps[0])):
        recvs = [pair_swap(x, s[j], sizes) for x, s in zip(sends, steps)]
        for i, recv in enumerate(recvs):
            if j + 1 < count:
                half = recv.shape[0] // 2
                late = j == 0 and i + 1 == len(steps)
                join = functools.partial(plus_after, after=beside) if late else plus
                sends[i] = join(keeps[i][half:], recv[half:])
                keeps[i] = plus(keeps[i][:half], recv[:half])
            else:
                sends[i] = keeps[i] = plus(keeps[i], recv)
    return keeps


def tree_gather(mines, steps, count, sizes):
    for j in reversed(range(count)):
        recvs = [pair_swap(x, s[j], sizes) for x, s in zip(mines, steps)]
        mines = [jnp.concatenate([m, r], 0) for m, r in zip(mines, recvs)]
    return mines


def local(
    ray_tokens,
    latents,
    group_ids,
    ln1_gain,
    ln1_shift,
    w_query,
    w_key,
    w_value,
    w_out,
    ln2_gain,
    ln2_shift,
    w_up,
    b_up,
    w_down,
    b_down,
    intrinsics,
    out_grad,
    *,
    sizes,
):
    keys = sizes["key"]
    share = out_grad.shape[0]
    width = ray_tokens.shape[1]
    cols = width // 2
    pairs = cols // PAIR
    chips = keys // 2
    chip_rows = 2 * share
    place = lax.axis_index("key")
    core = place % 2
    chip = place // 2

    def core_swap(x):
        return lax.ppermute(x, "key", [(i, i ^ 1) for i in range(keys)])

    def chip_shift(x, s):
        return lax.ppermute(x, "key", [(i, (i + 2 * s) % keys) for i in range(keys)])

    lookup = group_ids[0][:, None] == jnp.arange(intrinsics.shape[0], dtype=jnp.int32)[None, :]
    carried = (
        latents[0].astype(F32)
        + jnp.dot(lookup.astype(BF), intrinsics, preferred_element_type=F32)
    ).astype(BF)
    tokens = carried.shape[0]
    carried_far = core_swap(carried)
    lines = jnp.concatenate(
        [x.reshape(-1, width) for x in (ln1_gain, ln1_shift, ln2_gain, ln2_shift, b_down, b_up)], 0
    ).astype(F32)
    steps = jnp.arange(keys, dtype=jnp.int32)
    order = ((chip + steps // 2) % chips) * 2 + (core + steps % 2) % 2
    normed, queries = query_call(order, core, ray_tokens, lines, w_query, share)
    key_rows, value_rows, key_cols, value_cols = keyval_call(
        core, carried, carried_far, w_key, w_value
    )

    stats, exps, os, sts = [None] * chips, [None] * chips, [None] * chips, [None] * chips
    ordered = queries
    for t in [*range(1, chips), 0]:
        o, st, e = attend_call(
            ordered, key_rows, value_cols, t * chip_rows, chip_rows, "far" if t else "own"
        )
        stats[t], exps[t] = st, e
        if t:
            ordered, o, st = lax.optimization_barrier((ordered, o, st))
        os[t], sts[t] = (chip_shift(o, t), chip_shift(st, t)) if t else (o, st)
    att, low_own, low_send, lse = combine_call(os, sts)
    low_far = core_swap(low_send)
    spots = jnp.stack([core, place])
    output, grad_middle, do_own, do_far, active, grad_hidden, normed_two, branch, branch_sums = (
        mlp_call(
            spots,
            low_own,
            low_far,
            ray_tokens,
            w_out,
            w_up,
            w_down,
            lines,
            out_grad,
        )
    )
    do_chip, aux_chip = delta_call(do_own, core_swap(do_far), att, lse)
    attended_low = jnp.concatenate(
        [jnp.where(core == 0, low_own, low_far), jnp.where(core == 0, low_far, low_own)], 1
    )
    branch_grads = lax.psum(
        (
            dot(attended_low, branch, TN).astype(BF),
            dot(normed_two, grad_hidden, TN).astype(BF),
            dot(active, out_grad, TN).astype(BF),
        ),
        ("dp", "key"),
    )

    first, rest = chip_steps(sizes)
    steps = [turn(first, i) + rest for i in range(3)]
    count = halvings(width, steps[0])
    marks = jnp.stack([mark_of(x, count) for x in steps] + [core]).astype(jnp.int32)

    dos, auxs = [do_chip], [aux_chip]
    for t in range(1, chips):
        dos.append(chip_shift(do_chip, chips - t))
        auxs.append(chip_shift(aux_chip, chips - t))

    def back(t, carry, pair0, count, fresh, name):
        return backward_call(
            exps[t],
            dos[t],
            queries,
            stats[t],
            auxs[t],
            key_cols,
            value_rows,
            carry,
            t * chip_rows,
            pair0,
            count,
            fresh,
            name,
        )

    early = pairs - 1
    dq_first, *first_carry = back(0, None, 0, early, 0, "own_first")

    def rest_of_backward():
        carry = first_carry
        parts = []
        for t in range(1, chips):
            dq, *carry = back(t, carry, 0, pairs, early if t == 1 else pairs, "far")
            parts.append(chip_shift(dq, t))
        dq_rest, *carry = back(0, carry, early, pairs - early, pairs, "own_rest")
        keys_own, keys_far, values_own, values_far, key_send, key_keep, value_send, value_keep = (
            keyval_grad_call(marks, count, carried, carried_far, *carry)
        )
        tokens_far = [core_swap(x) for x in (keys_far, values_far)]
        key_send, value_send, queries_own, queries_far, query_send, query_keep = query_grad_call(
            marks, count, normed, dq_first, dq_rest, parts, (key_send, value_send)
        )
        queries_far = core_swap(queries_far)
        rays_grad, norm_sums = rays_grad_call(
            spots,
            queries_own,
            queries_far,
            w_query,
            ray_tokens,
            grad_middle,
            lines,
        )
        grad_carried, grad_table = carried_grad_call(
            core,
            group_ids,
            keys_own,
            tokens_far[0],
            values_own,
            tokens_far[1],
            w_key,
            w_value,
            intrinsics.shape[0],
        )
        small = jnp.concatenate([norm_sums, branch_sums, grad_table], 0)
        small = small + core_swap(small)
        for x in steps[0]:
            small = plus(small, pair_swap(small, x, sizes))
        sums = tree_scatter(
            [(query_send, query_keep), (key_send, key_keep), (value_send, value_keep)],
            steps,
            count,
            sizes,
            grad_table,
        )
        sums = tree_gather(sums, steps, count, sizes)
        return rays_grad, grad_carried, sums, [core_swap(g) for g in sums], small

    shapes = jax.eval_shape(rest_of_backward)
    rays_grad, grad_carried, sums, far_sums, small = lax.cond(
        group_ids[0, 0] >= 0,
        rest_of_backward,
        lambda: jax.tree.map(lambda x: jnp.zeros(x.shape, x.dtype), shapes),
    )
    *attention_grads, grad_out, grad_up, grad_down = finish_call(
        marks, count, sums, far_sums, branch_grads
    )
    branch_grads = (grad_out, grad_up, grad_down)
    up_rows = b_up.shape[0] // width
    table_row = 8 + branch_sums.shape[0]
    grads = [
        small[0],
        small[1],
        small[8],
        small[9],
        small[11 : 11 + up_rows].reshape(-1),
        small[10],
        small[table_row:],
    ]
    return (
        output,
        rays_grad,
        grad_carried[None],
        grads[0],
        grads[1],
        attention_grads[0],
        attention_grads[1],
        attention_grads[2],
        branch_grads[0],
        grads[2],
        grads[3],
        branch_grads[1],
        grads[4],
        branch_grads[2],
        grads[5],
        grads[6],
    )


def solution(mesh):
    rows = P(("dp", "key"), None)
    placed = (P("dp", None), P("dp", "key", None), P("dp", "key")) + (P(),) * 13 + (rows,)
    return jax.shard_map(
        functools.partial(local, sizes=dict(mesh.shape)),
        mesh=mesh,
        in_specs=placed,
        out_specs=(rows, rows, P("dp", "key", None)) + (P(),) * 13,
        check_vma=False,
    )
```

```python
import functools

import jax
import jax.numpy as jnp
from jax import lax
from jax.experimental import pallas as pl
from jax.experimental.pallas import tpu as pltpu
from jax.sharding import PartitionSpec as P

H = 12
HD = 64
PAIR = 2 * HD
EPSILON = 1e-05
BF = jnp.bfloat16
F32 = jnp.float32
LOG2E = 1.4426950408889634
LN2 = 0.6931471805599453
SAFE_BOUND = 60.0
GELU_A = 0.7978845608028654
GELU_B = 0.044715
BRIEF = pl.CostEstimate(flops=1000, bytes_accessed=1000, transcendentals=0)
VMEM = 60 * 1024 * 1024


def dot(a, b, dims=((1,), (0,))):
    return lax.dot_general(a, b, (dims, ((), ())), preferred_element_type=F32)


NT = ((1,), (1,))
TN = ((0,), (0,))


def params(**kw):
    return pltpu.CompilerParams(vmem_limit_bytes=VMEM, **kw)


def head_half(x, h, axis=1):
    i = lax.broadcasted_iota(jnp.int32, x.shape, axis)
    return jnp.where((i < HD) == (h == 0), x, jnp.zeros_like(x))


def norm_forward(values, gain_vec, shift_vec):
    centre = values - jnp.mean(values, axis=-1, keepdims=True)
    scaled = lax.rsqrt(jnp.mean(centre * centre, axis=-1, keepdims=True) + EPSILON)
    unit_rows = centre * scaled
    return (unit_rows * gain_vec + shift_vec, unit_rows, scaled)


def norm_backward(grad_rows, unit_rows, scaled, gain_vec):
    grad_unit = grad_rows * gain_vec
    centred_grad = (
        grad_unit
        - jnp.mean(grad_unit, axis=-1, keepdims=True)
        - unit_rows * jnp.mean(grad_unit * unit_rows, axis=-1, keepdims=True)
    )
    return (
        scaled * centred_grad,
        jnp.sum(grad_rows * unit_rows, axis=0),
        jnp.sum(grad_rows, axis=0),
    )


def query_kernel(order, rays, lines, wq, normed, q):
    n, _, _ = norm_forward(rays[...].astype(F32), lines[0:1, :], lines[1:2, :])
    n = n.astype(BF)
    normed[...] = n
    q[...] = (dot(n, wq[...]) * (HD**-0.5 * LOG2E)).astype(BF)


def query_call(order, core, rays, lines, wq, share):
    rows, width = rays.shape
    cols = width // 2
    blocks = rows // share
    pre = jnp.concatenate([order, core[None]])
    return pl.pallas_call(
        query_kernel,
        grid_spec=pltpu.PrefetchScalarGridSpec(
            num_scalar_prefetch=1,
            grid=(blocks,),
            in_specs=[
                pl.BlockSpec((share, width), lambda i, o: (o[i], 0)),
                pl.BlockSpec(lines.shape, lambda i, o: (0, 0)),
                pl.BlockSpec((width, cols), lambda i, o: (0, o[blocks])),
            ],
            out_specs=[
                pl.BlockSpec((share, width), lambda i, o: (i, 0)),
                pl.BlockSpec((share, cols), lambda i, o: (i, 0)),
            ],
        ),
        out_shape=[
            jax.ShapeDtypeStruct((rows, width), BF),
            jax.ShapeDtypeStruct((rows, cols), BF),
        ],
        compiler_params=params(),
        cost_estimate=BRIEF,
        name="rays_query",
    )(pre, rays, lines, wq)


def keyval_kernel(core, own, far, wk, wv, k, v, kt, vt):
    x = jnp.where(pl.program_id(0) < pl.num_programs(0) // 2, own[...], far[...])
    kk = dot(x, wk[...]).astype(BF)
    vv = dot(x, wv[...]).astype(BF)
    k[...] = kk
    v[...] = vv
    kt[...] = kk.T
    vt[...] = vv.T


def keyval_call(core, own, far, wk, wv):
    rows, width = own.shape
    rows = 2 * rows
    cols = width // 2
    blk = 512
    half = rows // blk // 2
    return pl.pallas_call(
        keyval_kernel,
        grid_spec=pltpu.PrefetchScalarGridSpec(
            num_scalar_prefetch=1,
            grid=(rows // blk,),
            in_specs=[
                pl.BlockSpec((blk, width), lambda i, o: (jnp.minimum(i, half - 1), 0)),
                pl.BlockSpec((blk, width), lambda i, o: (jnp.maximum(i - half, 0), 0)),
                pl.BlockSpec((width, cols), lambda i, o: (0, o[0])),
                pl.BlockSpec((width, cols), lambda i, o: (0, o[0])),
            ],
            out_specs=[
                pl.BlockSpec((blk, cols), lambda i, o: (i, 0)),
                pl.BlockSpec((blk, cols), lambda i, o: (i, 0)),
                pl.BlockSpec((cols, blk), lambda i, o: (0, i)),
                pl.BlockSpec((cols, blk), lambda i, o: (0, i)),
            ],
        ),
        out_shape=[
            jax.ShapeDtypeStruct((rows, cols), BF),
            jax.ShapeDtypeStruct((rows, cols), BF),
            jax.ShapeDtypeStruct((cols, rows), BF),
            jax.ShapeDtypeStruct((cols, rows), BF),
        ],
        compiler_params=params(),
        cost_estimate=BRIEF,
        name="keys_values",
    )(core[None], own, far, wk, wv)


def attend_kernel(qb, k, vt, o, st, e, km, kn, spare, *, tc):
    tokens = k.shape[0]
    rb = qb.shape[0]
    chunks = [slice(c, c + tc) for c in range(0, tokens, tc)]

    @pl.when(pl.program_id(1) == 0)
    def _():
        for h in (0, 1):
            kh = head_half(k[...], h)
            km[h] = kh
            kf = kh.astype(F32)
            top = jnp.max(jnp.sum(kf * kf, axis=1, keepdims=True), axis=0, keepdims=True)
            kn[h : h + 1, :] = jnp.broadcast_to(top, (1, PAIR))

    qf = qb[...].astype(F32)
    bound = jnp.float32(0)
    for h in (0, 1):
        qn = jnp.max(jnp.sum(head_half(qf * qf, h), axis=1, keepdims=True), axis=0, keepdims=True)
        bound = jnp.maximum(bound, jnp.max(qn * kn[h : h + 1, :]))
    small = bound < SAFE_BOUND * SAFE_BOUND

    def scores(h, r):
        return dot(km[h, r, :], qb[...], NT)

    def mixed(h, r, low):
        cols = jnp.concatenate([vt[h * HD : (h + 1) * HD, r], jnp.ones((HD, tc), BF)], 0)
        return dot(cols, low)

    def finish(acc, shifts):
        outs = []
        for h in (0, 1):
            total = acc[h][HD : HD + 1]
            outs.append(acc[h][:HD] / total)
            st[h : h + 1, :] = shifts[h]
            st[h + 2 : h + 3, :] = shifts[h] + jnp.log2(total)
        o[...] = jnp.concatenate(outs, 0).T.astype(BF)

    @pl.when(small)
    def _():
        items = [(h, r) for h in (0, 1) for r in chunks]
        acc = [0.0, 0.0]
        ready = [scores(*items[0])]
        waiting = []
        for n, (h, r) in enumerate(items):
            if n + 1 < len(items):
                ready.append(scores(*items[n + 1]))
            low = jnp.exp2(ready.pop(0)).astype(BF)
            e[h, r, :] = low
            if waiting:
                g, *rest = waiting.pop()
                acc[g] = acc[g] + mixed(g, *rest)
            waiting.append((h, r, low))
        g, *rest = waiting.pop()
        acc[g] = acc[g] + mixed(g, *rest)
        finish(acc, [jnp.zeros((1, rb), F32)] * 2)

    @pl.when(jnp.logical_not(small))
    def _():
        acc = [0.0, 0.0]
        shifts = []
        for h in (0, 1):
            m = None
            for r in chunks:
                s = scores(h, r)
                spare[r, :] = s
                mc = jnp.max(s, axis=0, keepdims=True)
                m = mc if m is None else jnp.maximum(m, mc)
            shifts.append(m)
            for r in chunks:
                low = jnp.exp2(spare[r, :] - m).astype(BF)
                e[h, r, :] = low
                acc[h] = acc[h] + mixed(h, r, low)
        finish(acc, shifts)


def attend_call(q, k, vt, first_row, rows, name):
    tokens, cols = k.shape
    pairs = cols // PAIR
    rb = min(512, rows)
    off = first_row // rb
    return pl.pallas_call(
        functools.partial(attend_kernel, tc=min(1024, tokens)),
        grid=(pairs, rows // rb),
        in_specs=[
            pl.BlockSpec((rb, PAIR), lambda p, i: (i + off, p)),
            pl.BlockSpec((tokens, PAIR), lambda p, i: (0, p)),
            pl.BlockSpec((PAIR, tokens), lambda p, i: (p, 0)),
        ],
        out_specs=[
            pl.BlockSpec((rb, PAIR), lambda p, i: (i, p)),
            pl.BlockSpec((8, rb), lambda p, i: (p, i)),
            pl.BlockSpec((2, tokens, rb), lambda p, i: (p, 0, i)),
        ],
        out_shape=[
            jax.ShapeDtypeStruct((rows, cols), BF),
            jax.ShapeDtypeStruct((8 * pairs, rows), F32),
            jax.ShapeDtypeStruct((2 * pairs, tokens, rows), BF),
        ],
        scratch_shapes=[
            pltpu.VMEM((2, tokens, PAIR), BF),
            pltpu.VMEM((8, PAIR), F32),
            pltpu.VMEM((tokens, rb), F32),
        ],
        compiler_params=params(),
        cost_estimate=BRIEF,
        name=f"attend_{name}",
    )(q, k, vt)


def spread(rows2):
    rows = rows2.shape[1]
    return jnp.concatenate([jnp.broadcast_to(rows2[h : h + 1, :], (HD, rows)) for h in (0, 1)], 0)


def combine_kernel(*refs, parts, pairs):
    os, sts = refs[:parts], refs[parts : 2 * parts]
    att, low_own, low_send, lse = refs[2 * parts :]
    first = pl.program_id(0) < pl.num_programs(0) // 2
    lows = []
    for p in range(pairs):
        c = slice(p * PAIR, (p + 1) * PAIR)
        ls = [s[8 * p + 2 : 8 * p + 4, :] for s in sts]
        top = functools.reduce(jnp.maximum, ls)
        tot = top + jnp.log2(sum(jnp.exp2(x - top) for x in ls))
        acc = 0.0
        for o, x in zip(os, ls):
            acc = acc + o[:, c].astype(F32) * spread(jnp.exp2(x - tot)).T
        att[:, c] = acc
        lows.append(acc.astype(BF))
        lse[8 * p : 8 * p + 2, :] = tot
    low = jnp.concatenate(lows, 1)

    @pl.when(first)
    def _():
        low_own[...] = low

    @pl.when(jnp.logical_not(first))
    def _():
        low_send[...] = low


def combine_call(os, sts):
    parts = len(os)
    rows, cols = os[0].shape
    pairs = cols // PAIR
    blk = min(256, rows // 2)
    half = rows // blk // 2
    wide = pl.BlockSpec((blk, cols), lambda i: (i, 0))
    flat = pl.BlockSpec((8 * pairs, blk), lambda i: (0, i))
    return pl.pallas_call(
        functools.partial(combine_kernel, parts=parts, pairs=pairs),
        grid=(rows // blk,),
        in_specs=[wide] * parts + [flat] * parts,
        out_specs=[
            wide,
            pl.BlockSpec((blk, cols), lambda i: (jnp.minimum(i, half - 1), 0)),
            pl.BlockSpec((blk, cols), lambda i: (jnp.maximum(i - half, 0), 0)),
            flat,
        ],
        out_shape=[
            jax.ShapeDtypeStruct((rows, cols), F32),
            jax.ShapeDtypeStruct((rows // 2, cols), BF),
            jax.ShapeDtypeStruct((rows // 2, cols), BF),
            jax.ShapeDtypeStruct((8 * pairs, rows), F32),
        ],
        compiler_params=params(),
        cost_estimate=BRIEF,
        name="combine",
    )(*os, *sts)


def delta_kernel(own, far, att, lse, do, aux, *, pairs):
    both = jnp.where(pl.program_id(0) < pl.num_programs(0) // 2, own[...], far[...])
    do[...] = both
    for p in range(pairs):
        c = slice(p * PAIR, (p + 1) * PAIR)
        prod = (both[:, c].astype(F32) * att[:, c]).T
        aux[8 * p : 8 * p + 2, :] = lse[8 * p : 8 * p + 2, :]
        for h in (0, 1):
            aux[8 * p + 2 + h : 8 * p + 3 + h, :] = jnp.sum(
                prod[h * HD : (h + 1) * HD, :], axis=0, keepdims=True
            )


def delta_call(own, far, att, lse):
    rows, cols = att.shape
    pairs = cols // PAIR
    blk = min(256, rows // 2)
    half = rows // blk // 2
    wide = pl.BlockSpec((blk, cols), lambda i: (i, 0))
    flat = pl.BlockSpec((8 * pairs, blk), lambda i: (0, i))
    return pl.pallas_call(
        functools.partial(delta_kernel, pairs=pairs),
        grid=(2 * half,),
        in_specs=[
            pl.BlockSpec((blk, cols), lambda i: (jnp.minimum(i, half - 1), 0)),
            pl.BlockSpec((blk, cols), lambda i: (jnp.maximum(i - half, 0), 0)),
            wide,
            flat,
        ],
        out_specs=[wide, flat],
        out_shape=[
            jax.ShapeDtypeStruct((rows, cols), BF),
            jax.ShapeDtypeStruct((8 * pairs, rows), F32),
        ],
        compiler_params=params(),
        cost_estimate=BRIEF,
        name="deltas",
    )(own, far, att, lse)


def mlp_kernel(
    spots, low_own, low_far, rays, wo_own, wo_far, w_up, w_down, lines, og,
    mixed, grad_middle, do_own, do_far, active_low, grad_hidden, normed_low, branch, sums,
):
    gain_row = lines[2:3, :]
    up_rows = w_up.shape[1] // w_up.shape[0]
    b_up = jnp.concatenate([lines[5 + j : 6 + j, :] for j in range(up_rows)], 1)
    middle = rays[...].astype(F32) + dot(low_own[...], wo_own[...]) + dot(low_far[...], wo_far[...])
    normed, unit, scale = norm_forward(middle, gain_row, lines[3:4, :])
    normed = normed.astype(BF)
    normed_low[...] = normed
    hidden = dot(normed, w_up[...]) + b_up
    square = hidden * hidden
    t = jnp.tanh(GELU_A * hidden * (1.0 + GELU_B * square))
    active = (0.5 * hidden * (1.0 + t)).astype(BF)
    active_low[...] = active
    mixed[...] = (middle + dot(active, w_down[...]) + lines[4:5, :]).astype(BF)
    grad_active = dot(og[...], w_down[...], NT).astype(BF).astype(F32)
    slope = 0.5 * (1.0 + t) + (0.5 * GELU_A) * hidden * (1.0 - t * t) * (1.0 + 3.0 * GELU_B * square)
    gh = (grad_active * slope).astype(BF)
    grad_hidden[...] = gh
    back, grad_gain, grad_shift = norm_backward(dot(gh, w_up[...], NT), unit, scale, gain_row)
    grad_out = og[...].astype(F32)
    gm = grad_out + back
    grad_middle[...] = gm
    gb = gm.astype(BF)
    branch[...] = gb
    do_far[...] = dot(gb, wo_far[...], NT).astype(BF)
    do_own[...] = dot(gb, wo_own[...], NT).astype(BF)

    @pl.when(pl.program_id(0) == 0)
    def _():
        sums[...] = jnp.zeros_like(sums)

    width = gm.shape[1]
    sums[0:1, :] += grad_gain[None]
    sums[1:2, :] += grad_shift[None]
    sums[2:3, :] += jnp.sum(grad_out, axis=0, keepdims=True)
    up = jnp.sum(gh.astype(F32), axis=0, keepdims=True)
    for j in range(up.shape[1] // width):
        sums[3 + j : 4 + j, :] += up[:, j * width : (j + 1) * width]


def mlp_call(spots, low_own, low_far, rays, w_out, w_up, w_down, lines, og):
    rows, width = og.shape
    cols = low_own.shape[1]
    hidden = w_up.shape[1]
    blk = min(256, rows)
    n = rows // blk
    wide = lambda c: pl.BlockSpec((blk, c), lambda i, o: (i, 0))
    fixed = lambda *d: pl.BlockSpec(d, lambda i, o: (0, 0))
    out = lambda c, t: jax.ShapeDtypeStruct((rows, c), t)
    return pl.pallas_call(
        mlp_kernel,
        grid_spec=pltpu.PrefetchScalarGridSpec(
            num_scalar_prefetch=1,
            grid=(n,),
            in_specs=[
                wide(cols),
                wide(cols),
                pl.BlockSpec((blk, width), lambda i, o: (o[1] * n + i, 0)),
                pl.BlockSpec((cols, width), lambda i, o: (o[0], 0)),
                pl.BlockSpec((cols, width), lambda i, o: (1 - o[0], 0)),
                fixed(width, hidden),
                fixed(hidden, width),
                fixed(*lines.shape),
                wide(width),
            ],
            out_specs=[
                wide(width),
                wide(width),
                wide(cols),
                wide(cols),
                wide(hidden),
                wide(hidden),
                wide(width),
                wide(width),
                fixed(8, width),
            ],
        ),
        out_shape=[
            out(width, BF),
            out(width, F32),
            out(cols, BF),
            out(cols, BF),
            out(hidden, BF),
            out(hidden, BF),
            out(width, BF),
            out(width, BF),
            jax.ShapeDtypeStruct((8, width), F32),
        ],
        compiler_params=params(),
        cost_estimate=BRIEF,
        name="mlp",
    )(
        spots,
        low_own,
        low_far,
        rays,
        w_out,
        w_out,
        w_up,
        w_down,
        lines,
        og,
    )


def backward_kernel(e, do, q, st, aux, kt, v, *refs, pair0, fresh):
    dq, dk, dv = refs[-3:]

    @pl.when(pl.program_id(1) == 0)
    def _():
        if len(refs) == 3:
            dk[...] = jnp.zeros_like(dk)
            dv[...] = jnp.zeros_like(dv)
        else:
            new = pl.program_id(0) + pair0 >= fresh
            dk[...] = jnp.where(new, 0.0, refs[0][...])
            dv[...] = jnp.where(new, 0.0, refs[1][...])

    scw = spread(jnp.exp2(st[0:2, :] - aux[0:2, :]))
    sct = scw.T
    dos = (do[...].astype(F32) * sct).astype(BF)
    qs = (q[...].astype(F32) * (sct * LN2)).astype(BF)
    grads = []
    for h in (0, 1):
        dp = dot(head_half(v[...], h), do[...], NT)
        grads.append((e[h].astype(F32) * (dp - aux[h + 2 : h + 3, :])).astype(BF))
    dqt = jnp.concatenate([dot(kt[h * HD : (h + 1) * HD, :], grads[h]) for h in (0, 1)], 0)
    dq[...] = (dqt * (scw * HD**-0.5)).T.astype(BF)
    both = lambda a: jnp.concatenate([head_half(a, 0), head_half(a, 1)], 0)
    dv[...] += dot(jnp.concatenate([e[0], e[1]], 1), both(dos))
    dk[...] += dot(jnp.concatenate(grads, 1), both(qs))


def backward_call(e, do, q, st, aux, kt, v, carry, first_row, pair0, pairs, fresh, name):
    rows = do.shape[0]
    tokens, cols = v.shape
    rb = min(512, rows)
    off = first_row // rb
    whole = pl.BlockSpec((tokens, PAIR), lambda p, i: (0, p + pair0))
    carry = () if carry is None else tuple(carry)
    return pl.pallas_call(
        functools.partial(backward_kernel, pair0=pair0, fresh=fresh),
        grid=(pairs, rows // rb),
        in_specs=[
            pl.BlockSpec((2, tokens, rb), lambda p, i: (p + pair0, 0, i)),
            pl.BlockSpec((rb, PAIR), lambda p, i: (i, p + pair0)),
            pl.BlockSpec((rb, PAIR), lambda p, i: (i + off, p + pair0)),
            pl.BlockSpec((8, rb), lambda p, i: (p + pair0, i)),
            pl.BlockSpec((8, rb), lambda p, i: (p + pair0, i)),
            pl.BlockSpec((PAIR, tokens), lambda p, i: (p + pair0, 0)),
            pl.BlockSpec((tokens, PAIR), lambda p, i: (0, p + pair0)),
        ]
        + [whole] * len(carry),
        out_specs=[pl.BlockSpec((rb, PAIR), lambda p, i: (i, p)), whole, whole],
        out_shape=[
            jax.ShapeDtypeStruct((rows, pairs * PAIR), BF),
            jax.ShapeDtypeStruct((tokens, cols), F32),
            jax.ShapeDtypeStruct((tokens, cols), F32),
        ],
        input_output_aliases={7: 1, 8: 2} if carry else {},
        compiler_params=params(),
        cost_estimate=BRIEF,
        name=f"backward_{name}",
    )(e, do, q, st, aux, kt, v, *carry)


def halves(acc, mark, count, send, keep):
    blocks = 1 << count
    size = acc.shape[0] // blocks
    for j in range(blocks):
        dst = keep if j < blocks // 2 else send
        at = j % (blocks // 2) * size
        rows = pl.ds(pl.multiple_of((j ^ mark) * size, 16), size)
        dst[at : at + size, :] = acc[rows, :].astype(BF)


def keyval_grad_kernel(marks, x_own, x_far, dk, dv, ko, kf, vo, vf, ks, kk, vs, vk, acck, accv, *, count):
    i = pl.program_id(0)
    n = pl.num_programs(0)

    @pl.when(i == 0)
    def _():
        acck[...] = jnp.zeros_like(acck)
        accv[...] = jnp.zeros_like(accv)

    a = dk[...].astype(BF)
    b = dv[...].astype(BF)

    @pl.when(i < n // 2)
    def _():
        kf[...] = a
        vf[...] = b

    @pl.when(i >= n // 2)
    def _():
        ko[...] = a
        vo[...] = b

    x = jnp.where(i < n // 2, x_far[...], x_own[...])
    acck[...] += dot(x, a, TN)
    accv[...] += dot(x, b, TN)

    @pl.when(i == n - 1)
    def _():
        halves(acck, marks[1], count, ks, kk)
        halves(accv, marks[2], count, vs, vk)


def keyval_grad_call(marks, count, own, far, dk, dv):
    rows, width = own.shape
    rows = 2 * rows
    cols = dk.shape[1]
    blk = 512
    half = rows // blk // 2
    turn_rows = lambda i: ((i + half) % (2 * half), 0)
    wide = pl.BlockSpec((blk, cols), turn_rows)
    own_at = lambda c: pl.BlockSpec((blk, c), lambda i: (jnp.maximum(i - half, 0), 0))
    far_at = lambda c: pl.BlockSpec((blk, c), lambda i: (jnp.minimum(i, half - 1), 0))
    part = pl.BlockSpec((width // 2, cols), lambda i: (0, 0))
    return pl.pallas_call(
        functools.partial(keyval_grad_kernel, count=count),
        grid=(2 * half,),
        in_specs=[
            pl.BlockSpec(memory_space=pltpu.SMEM),
            own_at(width),
            far_at(width),
            wide,
            wide,
        ],
        out_specs=[own_at(cols), far_at(cols)] * 2 + [part] * 4,
        out_shape=[jax.ShapeDtypeStruct((rows // 2, cols), BF)] * 4
        + [jax.ShapeDtypeStruct((width // 2, cols), BF)] * 4,
        scratch_shapes=[pltpu.VMEM((width, cols), F32)] * 2,
        compiler_params=params(),
        cost_estimate=BRIEF,
        name="keyval_grad",
    )(marks, own, far, dk, dv)


def query_grad_kernel(marks, x, d0, d1, *refs, parts, count):
    own, far, send, keep = refs[-5:-1]
    acc = refs[-1]
    i = pl.program_id(0)
    a = jnp.concatenate([d0[...], d1[...]], 1)
    if parts:
        a = sum((r[...].astype(F32) for r in refs[:parts]), a.astype(F32)).astype(BF)
    g = dot(x[...], a, TN)

    @pl.when(i == 0)
    def _():
        own[...] = a
        acc[...] = g

    @pl.when(i == 1)
    def _():
        far[...] = a
        acc[...] += g
        halves(acc, marks[0], count, send, keep)


def query_grad_call(marks, count, x, d0, d1, parts, sends):
    rows = d0.shape[0]
    cols = d0.shape[1] + d1.shape[1]
    width = x.shape[1]
    blk = rows // 2
    k = len(sends)
    anywhere = pl.BlockSpec(memory_space=pl.ANY)
    wide = lambda c: pl.BlockSpec((blk, c), lambda i: (i, 0))
    fixed = pl.BlockSpec((blk, cols), lambda i: (0, 0))
    part = pl.BlockSpec((width // 2, cols), lambda i: (0, 0))
    return pl.pallas_call(
        functools.partial(query_grad_kernel, parts=len(parts), count=count),
        grid=(2,),
        in_specs=[pl.BlockSpec(memory_space=pltpu.SMEM), wide(width), wide(d0.shape[1]), wide(d1.shape[1])]
        + [wide(cols)] * len(parts)
        + [anywhere] * k,
        out_specs=[anywhere] * k + [fixed, fixed, part, part],
        out_shape=[jax.ShapeDtypeStruct(y.shape, y.dtype) for y in sends]
        + [jax.ShapeDtypeStruct((blk, cols), BF)] * 2
        + [jax.ShapeDtypeStruct((width // 2, cols), BF)] * 2,
        scratch_shapes=[pltpu.VMEM((width, cols), F32)],
        input_output_aliases={4 + len(parts) + i: i for i in range(k)},
        compiler_params=params(),
        cost_estimate=BRIEF,
        name="query_grad",
    )(marks, x, d0, d1, *parts, *sends)


def carried_grad_kernel(core, ids, ko, kf, vo, vf, wko, wkf, wvo, wvf, out, table):
    acc = dot(ko[...], wko[...], NT) + dot(kf[...], wkf[...], NT)
    acc += dot(vo[...], wvo[...], NT) + dot(vf[...], wvf[...], NT)
    out[...] = acc
    groups = table.shape[0]
    hot = lax.broadcasted_iota(jnp.int32, (groups, ids.shape[1]), 0) == ids[...]
    hot = hot.astype(F32).astype(BF)
    high = acc.astype(BF)
    rest = (acc - high.astype(F32)).astype(BF)

    @pl.when(pl.program_id(0) == 0)
    def _():
        table[...] = jnp.zeros_like(table)

    table[...] += dot(hot, high) + dot(hot, rest)


def carried_grad_call(core, ids, ko, kf, vo, vf, wk, wv, groups):
    rows, cols = ko.shape
    width = wk.shape[0]
    blk = 256
    wide = pl.BlockSpec((blk, cols), lambda i, o: (i, 0))
    own = pl.BlockSpec((width, cols), lambda i, o: (0, o[0]))
    far = pl.BlockSpec((width, cols), lambda i, o: (0, 1 - o[0]))
    return pl.pallas_call(
        carried_grad_kernel,
        grid_spec=pltpu.PrefetchScalarGridSpec(
            num_scalar_prefetch=1,
            grid=(rows // blk,),
            in_specs=[pl.BlockSpec((1, blk), lambda i, o: (0, i))] + [wide] * 4 + [own, far, own, far],
            out_specs=[
                pl.BlockSpec((blk, width), lambda i, o: (i, 0)),
                pl.BlockSpec((groups, width), lambda i, o: (0, 0)),
            ],
        ),
        out_shape=[
            jax.ShapeDtypeStruct((rows, width), F32),
            jax.ShapeDtypeStruct((groups, width), F32),
        ],
        compiler_params=params(),
        cost_estimate=BRIEF,
        name="carried_grad",
    )(core[None], ids, ko, kf, vo, vf, wk, wk, wv, wv)


def rays_grad_kernel(spots, dqo, dqf, wo, wf, rays, middle, lines, out, sums):
    g = dot(dqo[...], wo[...], NT) + dot(dqf[...], wf[...], NT)
    gain_row = lines[0:1, :]
    _, unit, scale = norm_forward(rays[...].astype(F32), gain_row, lines[1:2, :])
    back, grad_gain, grad_shift = norm_backward(g, unit, scale, gain_row)
    out[...] = middle[...] + back

    @pl.when(pl.program_id(0) == 0)
    def _():
        sums[...] = jnp.zeros_like(sums)

    sums[0:1, :] += grad_gain[None]
    sums[1:2, :] += grad_shift[None]


def rays_grad_call(spots, dqo, dqf, w, rays, middle, lines):
    rows, cols = dqo.shape
    width = w.shape[0]
    blk = min(256, rows)
    n = rows // blk
    wide = lambda c: pl.BlockSpec((blk, c), lambda i, o: (i, 0))
    return pl.pallas_call(
        rays_grad_kernel,
        grid_spec=pltpu.PrefetchScalarGridSpec(
            num_scalar_prefetch=1,
            grid=(n,),
            in_specs=[
                wide(cols),
                wide(cols),
                pl.BlockSpec((width, cols), lambda i, o: (0, o[0])),
                pl.BlockSpec((width, cols), lambda i, o: (0, 1 - o[0])),
                pl.BlockSpec((blk, width), lambda i, o: (o[1] * n + i, 0)),
                wide(width),
                pl.BlockSpec(lines.shape, lambda i, o: (0, 0)),
            ],
            out_specs=[wide(width), pl.BlockSpec((8, width), lambda i, o: (0, 0))],
        ),
        out_shape=[
            jax.ShapeDtypeStruct((rows, width), F32),
            jax.ShapeDtypeStruct((8, width), F32),
        ],
        compiler_params=params(),
        cost_estimate=BRIEF,
        name="rays_grad",
    )(spots, dqo, dqf, w, w, rays, middle, lines)


def finish_kernel(marks, *refs, n, inner, size):
    core = marks[n]
    k = (len(refs) - 3 * n) // 2
    mines, fars, whole = refs[:n], refs[n : 2 * n], refs[2 * n : 2 * n + k]
    outs, wide = refs[2 * n + k : 3 * n + k], refs[3 * n + k :]
    for i, (mine, far, out) in enumerate(zip(mines, fars, outs)):
        cols = mine.shape[1]
        for j in range(inner):
            src = pl.ds(pl.multiple_of((j ^ (marks[i] & (inner - 1))) * size, 16), size)
            dst = slice(j * size, (j + 1) * size)
            out[dst, pl.ds(pl.multiple_of(core * cols, 128), cols)] = mine[src, :].astype(F32)
            out[dst, pl.ds(pl.multiple_of((1 - core) * cols, 128), cols)] = far[src, :].astype(F32)
    for src, dst in zip(whole, wide):
        dst[...] = src[...].astype(F32)


def finish_call(marks, count, mines, fars, whole):
    rows, cols = mines[0].shape
    n = len(mines)
    outer = min(2, count)
    inner = 1 << (count - outer)
    size = rows >> count
    blk = size * inner

    def place(k):
        return pl.BlockSpec((blk, cols), lambda i, m: (i ^ (m[k] // inner), 0))

    cuts = [pl.BlockSpec((x.shape[0] >> outer, x.shape[1]), lambda i, m: (i, 0)) for x in whole]
    return pl.pallas_call(
        functools.partial(finish_kernel, n=n, inner=inner, size=size),
        grid_spec=pltpu.PrefetchScalarGridSpec(
            num_scalar_prefetch=1,
            grid=(1 << outer,),
            in_specs=[place(k) for k in range(n)] * 2 + cuts,
            out_specs=[pl.BlockSpec((blk, 2 * cols), lambda i, m: (i, 0))] * n + cuts,
        ),
        out_shape=[jax.ShapeDtypeStruct((rows, 2 * cols), F32)] * n
        + [jax.ShapeDtypeStruct(x.shape, F32) for x in whole],
        compiler_params=params(),
        cost_estimate=BRIEF,
        name="finish",
    )(marks, *mines, *fars, *whole)


def pair_swap(x, step, sizes):
    axis, mask = step
    return lax.ppermute(x, axis, [(i, i ^ mask) for i in range(sizes[axis])])


def step_bit(step):
    axis, mask = step
    return (lax.axis_index(axis) // mask) % 2


def chip_steps(sizes):
    along = [("dp", 1 << j) for j in range(sizes["dp"].bit_length() - 1)]
    across = [("key", 2 << j) for j in range(sizes["key"].bit_length() - 2)]
    return along[:1] + across[:1] + along[1:2], along[2:] + across[1:]


def turn(first, i):
    i = i % len(first)
    return first[i:] + first[:i]


def halvings(rows, steps):
    count = 0
    while count < len(steps) and rows % 32 == 0:
        rows //= 2
        count += 1
    return count


def mark_of(steps, count):
    return sum(step_bit(x) << (count - 1 - j) for j, x in enumerate(steps[:count]))


def plus(a, b):
    return (a.astype(F32) + b.astype(F32)).astype(a.dtype)


def plus_after_kernel(a, b, _, out):
    half = out.shape[0]
    out[...] = plus(a[half:, :], b[half:, :])


def plus_after(a, b, after):
    whole = pl.BlockSpec(memory_space=pltpu.VMEM)
    return pl.pallas_call(
        plus_after_kernel,
        in_specs=[whole, whole, pl.BlockSpec(memory_space=pl.ANY)],
        out_specs=whole,
        out_shape=jax.ShapeDtypeStruct((a.shape[0] // 2, a.shape[1]), a.dtype),
        compiler_params=params(),
        cost_estimate=BRIEF,
        name="plus_after",
    )(a, b, after)


def tree_scatter(parts, steps, count, sizes, beside):
    sends = [p[0] for p in parts]
    keeps = [p[1] for p in parts]
    for j in range(len(steps[0])):
        recvs = [pair_swap(x, s[j], sizes) for x, s in zip(sends, steps)]
        for i, recv in enumerate(recvs):
            if j + 1 < count:
                half = recv.shape[0] // 2
                if j == 0 and i + 1 == len(steps):
                    sends[i] = plus_after(keeps[i], recv, beside)
                else:
                    sends[i] = plus(keeps[i][half:], recv[half:])
                keeps[i] = plus(keeps[i][:half], recv[:half])
            else:
                sends[i] = keeps[i] = plus(keeps[i], recv)
    return keeps


def join_after_kernel(a, b, _, out):
    half = a.shape[0]
    out[:half, :] = a[...]
    out[half:, :] = b[...]


def join_after(a, b, after):
    whole = pl.BlockSpec(memory_space=pltpu.VMEM)
    return pl.pallas_call(
        join_after_kernel,
        in_specs=[whole, whole, pl.BlockSpec(memory_space=pl.ANY)],
        out_specs=whole,
        out_shape=jax.ShapeDtypeStruct((2 * a.shape[0], a.shape[1]), a.dtype),
        compiler_params=params(),
        cost_estimate=BRIEF,
        name="join_after",
    )(a, b, after)


def tree_gather(mines, steps, count, sizes, small):
    turns = list(steps[0])
    for j in reversed(range(count)):
        recvs = [pair_swap(x, s[j], sizes) for x, s in zip(mines, steps)]
        while len(turns) > j:
            small = plus(small, pair_swap(small, turns.pop(0), sizes))
        pairs = list(zip(mines, recvs))
        mines = [jnp.concatenate(x, 0) for x in pairs[:-1]] + [join_after(*pairs[-1], small)]
    return mines, small


def local(
    ray_tokens,
    latents,
    group_ids,
    ln1_gain,
    ln1_shift,
    w_query,
    w_key,
    w_value,
    w_out,
    ln2_gain,
    ln2_shift,
    w_up,
    b_up,
    w_down,
    b_down,
    intrinsics,
    out_grad,
    *,
    sizes,
):
    keys = sizes["key"]
    share = out_grad.shape[0]
    width = ray_tokens.shape[1]
    cols = width // 2
    pairs = cols // PAIR
    chips = keys // 2
    chip_rows = 2 * share
    place = lax.axis_index("key")
    core = place % 2
    chip = place // 2

    def core_swap(x):
        return lax.ppermute(x, "key", [(i, i ^ 1) for i in range(keys)])

    def chip_shift(x, s):
        return lax.ppermute(x, "key", [(i, (i + 2 * s) % keys) for i in range(keys)])

    lookup = group_ids[0][:, None] == jnp.arange(intrinsics.shape[0], dtype=jnp.int32)[None, :]
    carried = (
        latents[0].astype(F32)
        + jnp.dot(lookup.astype(BF), intrinsics, preferred_element_type=F32)
    ).astype(BF)
    tokens = carried.shape[0]
    carried_far = core_swap(carried)
    lines = jnp.concatenate(
        [x.reshape(-1, width) for x in (ln1_gain, ln1_shift, ln2_gain, ln2_shift, b_down, b_up)], 0
    ).astype(F32)
    steps = jnp.arange(keys, dtype=jnp.int32)
    order = ((chip + steps // 2) % chips) * 2 + (core + steps % 2) % 2
    normed, queries = query_call(order, core, ray_tokens, lines, w_query, share)
    key_rows, value_rows, key_cols, value_cols = keyval_call(
        core, carried, carried_far, w_key, w_value
    )

    stats, exps, os, sts = [None] * chips, [None] * chips, [None] * chips, [None] * chips
    ordered = queries
    for t in [*range(1, chips), 0]:
        o, st, e = attend_call(
            ordered, key_rows, value_cols, t * chip_rows, chip_rows, "far" if t else "own"
        )
        stats[t], exps[t] = st, e
        if t:
            ordered, o, st = lax.optimization_barrier((ordered, o, st))
        os[t], sts[t] = (chip_shift(o, t), chip_shift(st, t)) if t else (o, st)
    att, low_own, low_send, lse = combine_call(os, sts)
    low_far = core_swap(low_send)
    spots = jnp.stack([core, place])
    output, grad_middle, do_own, do_far, active, grad_hidden, normed_two, branch, branch_sums = (
        mlp_call(
            spots,
            low_own,
            low_far,
            ray_tokens,
            w_out,
            w_up,
            w_down,
            lines,
            out_grad,
        )
    )
    do_chip, aux_chip = delta_call(do_own, core_swap(do_far), att, lse)
    attended_low = jnp.concatenate(
        [jnp.where(core == 0, low_own, low_far), jnp.where(core == 0, low_far, low_own)], 1
    )
    branch_grads = lax.psum(
        (
            dot(attended_low, branch, TN).astype(BF),
            dot(normed_two, grad_hidden, TN).astype(BF),
            dot(active, out_grad, TN).astype(BF),
        ),
        ("dp", "key"),
    )

    first, rest = chip_steps(sizes)
    steps = [turn(first, i) + rest for i in range(3)]
    count = halvings(width, steps[0])
    marks = jnp.stack([mark_of(x, count) for x in steps] + [core]).astype(jnp.int32)

    dos, auxs = [do_chip], [aux_chip]
    for t in range(1, chips):
        dos.append(chip_shift(do_chip, chips - t))
        auxs.append(chip_shift(aux_chip, chips - t))

    def back(t, carry, pair0, count, fresh, name):
        return backward_call(
            exps[t],
            dos[t],
            queries,
            stats[t],
            auxs[t],
            key_cols,
            value_rows,
            carry,
            t * chip_rows,
            pair0,
            count,
            fresh,
            name,
        )

    early = pairs - 1
    dq_first, *first_carry = back(0, None, 0, early, 0, "own_first")

    def rest_of_backward():
        carry = first_carry
        parts = []
        for t in range(1, chips):
            dq, *carry = back(t, carry, 0, pairs, early if t == 1 else pairs, "far")
            parts.append(chip_shift(dq, t))
        dq_rest, *carry = back(0, carry, early, pairs - early, pairs, "own_rest")
        keys_own, keys_far, values_own, values_far, key_send, key_keep, value_send, value_keep = (
            keyval_grad_call(marks, count, carried, carried_far, *carry)
        )
        tokens_far = [core_swap(x) for x in (keys_far, values_far)]
        key_send, value_send, queries_own, queries_far, query_send, query_keep = query_grad_call(
            marks, count, normed, dq_first, dq_rest, parts, (key_send, value_send)
        )
        queries_far = core_swap(queries_far)
        rays_grad, norm_sums = rays_grad_call(
            spots,
            queries_own,
            queries_far,
            w_query,
            ray_tokens,
            grad_middle,
            lines,
        )
        grad_carried, grad_table = carried_grad_call(
            core,
            group_ids,
            keys_own,
            tokens_far[0],
            values_own,
            tokens_far[1],
            w_key,
            w_value,
            intrinsics.shape[0],
        )
        small = jnp.concatenate([norm_sums, branch_sums, grad_table], 0)
        small = small + core_swap(small)
        sums = tree_scatter(
            [(query_send, query_keep), (key_send, key_keep), (value_send, value_keep)],
            steps,
            count,
            sizes,
            grad_table,
        )
        sums, small = tree_gather(sums, steps, count, sizes, small)
        far_sums = [core_swap(g) for g in sums]
        up_rows = b_up.shape[0] // width
        table_row = 8 + branch_sums.shape[0]
        grads = [
            small[0],
            small[1],
            small[8],
            small[9],
            small[11 : 11 + up_rows].reshape(-1),
            small[10],
            small[table_row:],
        ]
        return rays_grad, grad_carried, sums, far_sums, grads

    shapes = jax.eval_shape(rest_of_backward)
    rays_grad, grad_carried, sums, far_sums, grads = lax.cond(
        group_ids[0, 0] >= 0,
        rest_of_backward,
        lambda: jax.tree.map(lambda x: jnp.zeros(x.shape, x.dtype), shapes),
    )
    *attention_grads, grad_out, grad_up, grad_down = finish_call(
        marks, count, sums, far_sums, branch_grads
    )
    branch_grads = (grad_out, grad_up, grad_down)
    return (
        output,
        rays_grad,
        grad_carried[None],
        grads[0],
        grads[1],
        attention_grads[0],
        attention_grads[1],
        attention_grads[2],
        branch_grads[0],
        grads[2],
        grads[3],
        branch_grads[1],
        grads[4],
        branch_grads[2],
        grads[5],
        grads[6],
    )


def solution(mesh):
    rows = P(("dp", "key"), None)
    placed = (P("dp", None), P("dp", "key", None), P("dp", "key")) + (P(),) * 13 + (rows,)
    return jax.shard_map(
        functools.partial(local, sizes=dict(mesh.shape)),
        mesh=mesh,
        in_specs=placed,
        out_specs=(rows, rows, P("dp", "key", None)) + (P(),) * 13,
        check_vma=False,
    )
```

```python
import functools

import jax
import jax.numpy as jnp
from jax import lax
from jax.experimental import pallas as pl
from jax.experimental.pallas import tpu as pltpu
from jax.sharding import PartitionSpec as P

H = 12
HD = 64
PAIR = 2 * HD
EPSILON = 1e-05
BF = jnp.bfloat16
F32 = jnp.float32
LOG2E = 1.4426950408889634
LN2 = 0.6931471805599453
SAFE_BOUND = 60.0
GELU_A = 0.7978845608028654
GELU_B = 0.044715
BRIEF = pl.CostEstimate(flops=1000, bytes_accessed=1000, transcendentals=0)
VMEM = 60 * 1024 * 1024


def dot(a, b, dims=((1,), (0,))):
    return lax.dot_general(a, b, (dims, ((), ())), preferred_element_type=F32)


NT = ((1,), (1,))
TN = ((0,), (0,))


def params(**kw):
    return pltpu.CompilerParams(vmem_limit_bytes=VMEM, **kw)


def head_half(x, h, axis=1):
    i = lax.broadcasted_iota(jnp.int32, x.shape, axis)
    return jnp.where((i < HD) == (h == 0), x, jnp.zeros_like(x))


def norm_forward(values, gain_vec, shift_vec):
    centre = values - jnp.mean(values, axis=-1, keepdims=True)
    scaled = lax.rsqrt(jnp.mean(centre * centre, axis=-1, keepdims=True) + EPSILON)
    unit_rows = centre * scaled
    return (unit_rows * gain_vec + shift_vec, unit_rows, scaled)


def norm_backward(grad_rows, unit_rows, scaled, gain_vec):
    grad_unit = grad_rows * gain_vec
    centred_grad = (
        grad_unit
        - jnp.mean(grad_unit, axis=-1, keepdims=True)
        - unit_rows * jnp.mean(grad_unit * unit_rows, axis=-1, keepdims=True)
    )
    return (
        scaled * centred_grad,
        jnp.sum(grad_rows * unit_rows, axis=0),
        jnp.sum(grad_rows, axis=0),
    )


def query_kernel(order, rays, lines, wq, normed, q):
    n, _, _ = norm_forward(rays[...].astype(F32), lines[0:1, :], lines[1:2, :])
    n = n.astype(BF)
    normed[...] = n
    q[...] = (dot(n, wq[...]) * (HD**-0.5 * LOG2E)).astype(BF)


def query_call(order, core, rays, lines, wq, share):
    rows, width = rays.shape
    cols = width // 2
    blocks = rows // share
    pre = jnp.concatenate([order, core[None]])
    return pl.pallas_call(
        query_kernel,
        grid_spec=pltpu.PrefetchScalarGridSpec(
            num_scalar_prefetch=1,
            grid=(blocks,),
            in_specs=[
                pl.BlockSpec((share, width), lambda i, o: (o[i], 0)),
                pl.BlockSpec(lines.shape, lambda i, o: (0, 0)),
                pl.BlockSpec((width, cols), lambda i, o: (0, o[blocks])),
            ],
            out_specs=[
                pl.BlockSpec((share, width), lambda i, o: (i, 0)),
                pl.BlockSpec((share, cols), lambda i, o: (i, 0)),
            ],
        ),
        out_shape=[
            jax.ShapeDtypeStruct((rows, width), BF),
            jax.ShapeDtypeStruct((rows, cols), BF),
        ],
        compiler_params=params(),
        cost_estimate=BRIEF,
        name="rays_query",
    )(pre, rays, lines, wq)


def keyval_kernel(core, own, far, wk, wv, k, v, kt, vt):
    x = jnp.where(pl.program_id(0) < pl.num_programs(0) // 2, own[...], far[...])
    kk = dot(x, wk[...]).astype(BF)
    vv = dot(x, wv[...]).astype(BF)
    k[...] = kk
    v[...] = vv
    kt[...] = kk.T
    vt[...] = vv.T


def keyval_call(core, own, far, wk, wv):
    rows, width = own.shape
    rows = 2 * rows
    cols = width // 2
    blk = 512
    half = rows // blk // 2
    return pl.pallas_call(
        keyval_kernel,
        grid_spec=pltpu.PrefetchScalarGridSpec(
            num_scalar_prefetch=1,
            grid=(rows // blk,),
            in_specs=[
                pl.BlockSpec((blk, width), lambda i, o: (jnp.minimum(i, half - 1), 0)),
                pl.BlockSpec((blk, width), lambda i, o: (jnp.maximum(i - half, 0), 0)),
                pl.BlockSpec((width, cols), lambda i, o: (0, o[0])),
                pl.BlockSpec((width, cols), lambda i, o: (0, o[0])),
            ],
            out_specs=[
                pl.BlockSpec((blk, cols), lambda i, o: (i, 0)),
                pl.BlockSpec((blk, cols), lambda i, o: (i, 0)),
                pl.BlockSpec((cols, blk), lambda i, o: (0, i)),
                pl.BlockSpec((cols, blk), lambda i, o: (0, i)),
            ],
        ),
        out_shape=[
            jax.ShapeDtypeStruct((rows, cols), BF),
            jax.ShapeDtypeStruct((rows, cols), BF),
            jax.ShapeDtypeStruct((cols, rows), BF),
            jax.ShapeDtypeStruct((cols, rows), BF),
        ],
        compiler_params=params(),
        cost_estimate=BRIEF,
        name="keys_values",
    )(core[None], own, far, wk, wv)


def attend_kernel(qb, k, vt, o, st, e, km, kn, spare, *, tc):
    tokens = k.shape[0]
    rb = qb.shape[0]
    chunks = [slice(c, c + tc) for c in range(0, tokens, tc)]

    @pl.when(pl.program_id(1) == 0)
    def _():
        for h in (0, 1):
            kh = head_half(k[...], h)
            km[h] = kh
            kf = kh.astype(F32)
            top = jnp.max(jnp.sum(kf * kf, axis=1, keepdims=True), axis=0, keepdims=True)
            kn[h : h + 1, :] = jnp.broadcast_to(top, (1, PAIR))

    qf = qb[...].astype(F32)
    bound = jnp.float32(0)
    for h in (0, 1):
        qn = jnp.max(jnp.sum(head_half(qf * qf, h), axis=1, keepdims=True), axis=0, keepdims=True)
        bound = jnp.maximum(bound, jnp.max(qn * kn[h : h + 1, :]))
    small = bound < SAFE_BOUND * SAFE_BOUND

    def scores(h, r):
        return dot(km[h, r, :], qb[...], NT)

    def mixed(h, r, low):
        cols = jnp.concatenate([vt[h * HD : (h + 1) * HD, r], jnp.ones((HD, tc), BF)], 0)
        return dot(cols, low)

    def finish(acc, shifts):
        outs = []
        for h in (0, 1):
            total = acc[h][HD : HD + 1]
            outs.append(acc[h][:HD] / total)
            st[h : h + 1, :] = shifts[h]
            st[h + 2 : h + 3, :] = shifts[h] + jnp.log2(total)
        o[...] = jnp.concatenate(outs, 0).T.astype(BF)

    @pl.when(small)
    def _():
        items = [(h, r) for h in (0, 1) for r in chunks]
        acc = [0.0, 0.0]
        ready = [scores(*items[0])]
        waiting = []
        for n, (h, r) in enumerate(items):
            if n + 1 < len(items):
                ready.append(scores(*items[n + 1]))
            low = jnp.exp2(ready.pop(0)).astype(BF)
            e[h, r, :] = low
            if waiting:
                g, *rest = waiting.pop()
                acc[g] = acc[g] + mixed(g, *rest)
            waiting.append((h, r, low))
        g, *rest = waiting.pop()
        acc[g] = acc[g] + mixed(g, *rest)
        finish(acc, [jnp.zeros((1, rb), F32)] * 2)

    @pl.when(jnp.logical_not(small))
    def _():
        acc = [0.0, 0.0]
        shifts = []
        for h in (0, 1):
            m = None
            for r in chunks:
                s = scores(h, r)
                spare[r, :] = s
                mc = jnp.max(s, axis=0, keepdims=True)
                m = mc if m is None else jnp.maximum(m, mc)
            shifts.append(m)
            for r in chunks:
                low = jnp.exp2(spare[r, :] - m).astype(BF)
                e[h, r, :] = low
                acc[h] = acc[h] + mixed(h, r, low)
        finish(acc, shifts)


def attend_call(q, k, vt, first_row, rows, name):
    tokens, cols = k.shape
    pairs = cols // PAIR
    rb = min(512, rows)
    off = first_row // rb
    return pl.pallas_call(
        functools.partial(attend_kernel, tc=min(1024, tokens)),
        grid=(pairs, rows // rb),
        in_specs=[
            pl.BlockSpec((rb, PAIR), lambda p, i: (i + off, p)),
            pl.BlockSpec((tokens, PAIR), lambda p, i: (0, p)),
            pl.BlockSpec((PAIR, tokens), lambda p, i: (p, 0)),
        ],
        out_specs=[
            pl.BlockSpec((rb, PAIR), lambda p, i: (i, p)),
            pl.BlockSpec((8, rb), lambda p, i: (p, i)),
            pl.BlockSpec((2, tokens, rb), lambda p, i: (p, 0, i)),
        ],
        out_shape=[
            jax.ShapeDtypeStruct((rows, cols), BF),
            jax.ShapeDtypeStruct((8 * pairs, rows), F32),
            jax.ShapeDtypeStruct((2 * pairs, tokens, rows), BF),
        ],
        scratch_shapes=[
            pltpu.VMEM((2, tokens, PAIR), BF),
            pltpu.VMEM((8, PAIR), F32),
            pltpu.VMEM((tokens, rb), F32),
        ],
        compiler_params=params(),
        cost_estimate=BRIEF,
        name=f"attend_{name}",
    )(q, k, vt)


def spread(rows2):
    rows = rows2.shape[1]
    return jnp.concatenate([jnp.broadcast_to(rows2[h : h + 1, :], (HD, rows)) for h in (0, 1)], 0)


def combine_kernel(*refs, parts, pairs):
    os, sts = refs[:parts], refs[parts : 2 * parts]
    att, low_own, low_send, lse = refs[2 * parts :]
    first = pl.program_id(0) < pl.num_programs(0) // 2
    lows = []
    for p in range(pairs):
        c = slice(p * PAIR, (p + 1) * PAIR)
        ls = [s[8 * p + 2 : 8 * p + 4, :] for s in sts]
        top = functools.reduce(jnp.maximum, ls)
        tot = top + jnp.log2(sum(jnp.exp2(x - top) for x in ls))
        acc = 0.0
        for o, x in zip(os, ls):
            acc = acc + o[:, c].astype(F32) * spread(jnp.exp2(x - tot)).T
        att[:, c] = acc
        lows.append(acc.astype(BF))
        lse[8 * p : 8 * p + 2, :] = tot
    low = jnp.concatenate(lows, 1)

    @pl.when(first)
    def _():
        low_own[...] = low

    @pl.when(jnp.logical_not(first))
    def _():
        low_send[...] = low


def combine_call(os, sts):
    parts = len(os)
    rows, cols = os[0].shape
    pairs = cols // PAIR
    blk = min(256, rows // 2)
    half = rows // blk // 2
    wide = pl.BlockSpec((blk, cols), lambda i: (i, 0))
    flat = pl.BlockSpec((8 * pairs, blk), lambda i: (0, i))
    return pl.pallas_call(
        functools.partial(combine_kernel, parts=parts, pairs=pairs),
        grid=(rows // blk,),
        in_specs=[wide] * parts + [flat] * parts,
        out_specs=[
            wide,
            pl.BlockSpec((blk, cols), lambda i: (jnp.minimum(i, half - 1), 0)),
            pl.BlockSpec((blk, cols), lambda i: (jnp.maximum(i - half, 0), 0)),
            flat,
        ],
        out_shape=[
            jax.ShapeDtypeStruct((rows, cols), F32),
            jax.ShapeDtypeStruct((rows // 2, cols), BF),
            jax.ShapeDtypeStruct((rows // 2, cols), BF),
            jax.ShapeDtypeStruct((8 * pairs, rows), F32),
        ],
        compiler_params=params(),
        cost_estimate=BRIEF,
        name="combine",
    )(*os, *sts)


def delta_kernel(own, far, att, lse, do, aux, *, pairs):
    both = jnp.where(pl.program_id(0) < pl.num_programs(0) // 2, own[...], far[...])
    do[...] = both
    for p in range(pairs):
        c = slice(p * PAIR, (p + 1) * PAIR)
        prod = (both[:, c].astype(F32) * att[:, c]).T
        aux[8 * p : 8 * p + 2, :] = lse[8 * p : 8 * p + 2, :]
        for h in (0, 1):
            aux[8 * p + 2 + h : 8 * p + 3 + h, :] = jnp.sum(
                prod[h * HD : (h + 1) * HD, :], axis=0, keepdims=True
            )


def delta_call(own, far, att, lse):
    rows, cols = att.shape
    pairs = cols // PAIR
    blk = min(256, rows // 2)
    half = rows // blk // 2
    wide = pl.BlockSpec((blk, cols), lambda i: (i, 0))
    flat = pl.BlockSpec((8 * pairs, blk), lambda i: (0, i))
    return pl.pallas_call(
        functools.partial(delta_kernel, pairs=pairs),
        grid=(2 * half,),
        in_specs=[
            pl.BlockSpec((blk, cols), lambda i: (jnp.minimum(i, half - 1), 0)),
            pl.BlockSpec((blk, cols), lambda i: (jnp.maximum(i - half, 0), 0)),
            wide,
            flat,
        ],
        out_specs=[wide, flat],
        out_shape=[
            jax.ShapeDtypeStruct((rows, cols), BF),
            jax.ShapeDtypeStruct((8 * pairs, rows), F32),
        ],
        compiler_params=params(),
        cost_estimate=BRIEF,
        name="deltas",
    )(own, far, att, lse)


def mlp_kernel(
    spots, low_own, low_far, rays, wo_own, wo_far, w_up, w_down, lines, og,
    mixed, grad_middle, do_own, do_far, active_low, grad_hidden, normed_low, branch, sums,
):
    gain_row = lines[2:3, :]
    up_rows = w_up.shape[1] // w_up.shape[0]
    b_up = jnp.concatenate([lines[5 + j : 6 + j, :] for j in range(up_rows)], 1)
    middle = rays[...].astype(F32) + dot(low_own[...], wo_own[...]) + dot(low_far[...], wo_far[...])
    normed, unit, scale = norm_forward(middle, gain_row, lines[3:4, :])
    normed = normed.astype(BF)
    normed_low[...] = normed
    hidden = dot(normed, w_up[...]) + b_up
    square = hidden * hidden
    t = jnp.tanh(GELU_A * hidden * (1.0 + GELU_B * square))
    active = (0.5 * hidden * (1.0 + t)).astype(BF)
    active_low[...] = active
    mixed[...] = (middle + dot(active, w_down[...]) + lines[4:5, :]).astype(BF)
    grad_active = dot(og[...], w_down[...], NT).astype(BF).astype(F32)
    slope = 0.5 * (1.0 + t) + (0.5 * GELU_A) * hidden * (1.0 - t * t) * (1.0 + 3.0 * GELU_B * square)
    gh = (grad_active * slope).astype(BF)
    grad_hidden[...] = gh
    back, grad_gain, grad_shift = norm_backward(dot(gh, w_up[...], NT), unit, scale, gain_row)
    grad_out = og[...].astype(F32)
    gm = grad_out + back
    grad_middle[...] = gm
    gb = gm.astype(BF)
    branch[...] = gb
    do_far[...] = dot(gb, wo_far[...], NT).astype(BF)
    do_own[...] = dot(gb, wo_own[...], NT).astype(BF)

    @pl.when(pl.program_id(0) == 0)
    def _():
        sums[...] = jnp.zeros_like(sums)

    width = gm.shape[1]
    sums[0:1, :] += grad_gain[None]
    sums[1:2, :] += grad_shift[None]
    sums[2:3, :] += jnp.sum(grad_out, axis=0, keepdims=True)
    up = jnp.sum(gh.astype(F32), axis=0, keepdims=True)
    for j in range(up.shape[1] // width):
        sums[3 + j : 4 + j, :] += up[:, j * width : (j + 1) * width]


def mlp_call(spots, low_own, low_far, rays, w_out, w_up, w_down, lines, og):
    rows, width = og.shape
    cols = low_own.shape[1]
    hidden = w_up.shape[1]
    blk = min(512, rows)
    n = rows // blk
    wide = lambda c: pl.BlockSpec((blk, c), lambda i, o: (i, 0))
    fixed = lambda *d: pl.BlockSpec(d, lambda i, o: (0, 0))
    out = lambda c, t: jax.ShapeDtypeStruct((rows, c), t)
    return pl.pallas_call(
        mlp_kernel,
        grid_spec=pltpu.PrefetchScalarGridSpec(
            num_scalar_prefetch=1,
            grid=(n,),
            in_specs=[
                wide(cols),
                wide(cols),
                pl.BlockSpec((blk, width), lambda i, o: (o[1] * n + i, 0)),
                pl.BlockSpec((cols, width), lambda i, o: (o[0], 0)),
                pl.BlockSpec((cols, width), lambda i, o: (1 - o[0], 0)),
                fixed(width, hidden),
                fixed(hidden, width),
                fixed(*lines.shape),
                wide(width),
            ],
            out_specs=[
                wide(width),
                wide(width),
                wide(cols),
                wide(cols),
                wide(hidden),
                wide(hidden),
                wide(width),
                wide(width),
                fixed(8, width),
            ],
        ),
        out_shape=[
            out(width, BF),
            out(width, F32),
            out(cols, BF),
            out(cols, BF),
            out(hidden, BF),
            out(hidden, BF),
            out(width, BF),
            out(width, BF),
            jax.ShapeDtypeStruct((8, width), F32),
        ],
        compiler_params=params(),
        cost_estimate=BRIEF,
        name="mlp",
    )(
        spots,
        low_own,
        low_far,
        rays,
        w_out,
        w_out,
        w_up,
        w_down,
        lines,
        og,
    )


def backward_kernel(e, do, q, st, aux, kt, v, *refs, pair0, fresh):
    dq, dk, dv = refs[-3:]

    @pl.when(pl.program_id(1) == 0)
    def _():
        if len(refs) == 3:
            dk[...] = jnp.zeros_like(dk)
            dv[...] = jnp.zeros_like(dv)
        else:
            new = pl.program_id(0) + pair0 >= fresh
            dk[...] = jnp.where(new, 0.0, refs[0][...])
            dv[...] = jnp.where(new, 0.0, refs[1][...])

    scw = spread(jnp.exp2(st[0:2, :] - aux[0:2, :]))
    sct = scw.T
    dos = (do[...].astype(F32) * sct).astype(BF)
    qs = (q[...].astype(F32) * (sct * LN2)).astype(BF)
    grads = []
    for h in (0, 1):
        dp = dot(head_half(v[...], h), do[...], NT)
        grads.append((e[h].astype(F32) * (dp - aux[h + 2 : h + 3, :])).astype(BF))
    dqt = jnp.concatenate([dot(kt[h * HD : (h + 1) * HD, :], grads[h]) for h in (0, 1)], 0)
    dq[...] = (dqt * (scw * HD**-0.5)).T.astype(BF)
    both = lambda a: jnp.concatenate([head_half(a, 0), head_half(a, 1)], 0)
    dv[...] += dot(jnp.concatenate([e[0], e[1]], 1), both(dos))
    dk[...] += dot(jnp.concatenate(grads, 1), both(qs))


def backward_call(e, do, q, st, aux, kt, v, carry, first_row, pair0, pairs, fresh, name):
    rows = do.shape[0]
    tokens, cols = v.shape
    rb = min(512, rows)
    off = first_row // rb
    whole = pl.BlockSpec((tokens, PAIR), lambda p, i: (0, p + pair0))
    carry = () if carry is None else tuple(carry)
    return pl.pallas_call(
        functools.partial(backward_kernel, pair0=pair0, fresh=fresh),
        grid=(pairs, rows // rb),
        in_specs=[
            pl.BlockSpec((2, tokens, rb), lambda p, i: (p + pair0, 0, i)),
            pl.BlockSpec((rb, PAIR), lambda p, i: (i, p + pair0)),
            pl.BlockSpec((rb, PAIR), lambda p, i: (i + off, p + pair0)),
            pl.BlockSpec((8, rb), lambda p, i: (p + pair0, i)),
            pl.BlockSpec((8, rb), lambda p, i: (p + pair0, i)),
            pl.BlockSpec((PAIR, tokens), lambda p, i: (p + pair0, 0)),
            pl.BlockSpec((tokens, PAIR), lambda p, i: (0, p + pair0)),
        ]
        + [whole] * len(carry),
        out_specs=[pl.BlockSpec((rb, PAIR), lambda p, i: (i, p)), whole, whole],
        out_shape=[
            jax.ShapeDtypeStruct((rows, pairs * PAIR), BF),
            jax.ShapeDtypeStruct((tokens, cols), F32),
            jax.ShapeDtypeStruct((tokens, cols), F32),
        ],
        input_output_aliases={7: 1, 8: 2} if carry else {},
        compiler_params=params(),
        cost_estimate=BRIEF,
        name=f"backward_{name}",
    )(e, do, q, st, aux, kt, v, *carry)


def halves(acc, mark, count, send, keep, col=0):
    blocks = 1 << count
    size = acc.shape[0] // blocks
    for j in range(blocks):
        dst = keep if j < blocks // 2 else send
        at = j % (blocks // 2) * size
        rows = pl.ds(pl.multiple_of((j ^ mark) * size, 16), size)
        dst[at : at + size, :] = acc[rows, col : col + dst.shape[1]].astype(BF)


def keyval_grad_kernel(marks, x_own, x_far, dk, dv, ko, kf, vo, vf, ks, kk, vs, vk, acc, *, count):
    i = pl.program_id(0)
    n = pl.num_programs(0)

    @pl.when(i == 0)
    def _():
        acc[...] = jnp.zeros_like(acc)

    a = dk[...].astype(BF)
    b = dv[...].astype(BF)

    @pl.when(i < n // 2)
    def _():
        kf[...] = a
        vf[...] = b

    @pl.when(i >= n // 2)
    def _():
        ko[...] = a
        vo[...] = b

    x = jnp.where(i < n // 2, x_far[...], x_own[...])
    acc[...] += dot(x, jnp.concatenate([a, b], 1), TN)

    @pl.when(i == n - 1)
    def _():
        halves(acc, marks[1], count, ks, kk)
        halves(acc, marks[2], count, vs, vk, a.shape[1])


def keyval_grad_call(marks, count, own, far, dk, dv):
    rows, width = own.shape
    rows = 2 * rows
    cols = dk.shape[1]
    blk = 512
    half = rows // blk // 2
    turn_rows = lambda i: ((i + half) % (2 * half), 0)
    wide = pl.BlockSpec((blk, cols), turn_rows)
    own_at = lambda c: pl.BlockSpec((blk, c), lambda i: (jnp.maximum(i - half, 0), 0))
    far_at = lambda c: pl.BlockSpec((blk, c), lambda i: (jnp.minimum(i, half - 1), 0))
    part = pl.BlockSpec((width // 2, cols), lambda i: (0, 0))
    return pl.pallas_call(
        functools.partial(keyval_grad_kernel, count=count),
        grid=(2 * half,),
        in_specs=[
            pl.BlockSpec(memory_space=pltpu.SMEM),
            own_at(width),
            far_at(width),
            wide,
            wide,
        ],
        out_specs=[own_at(cols), far_at(cols)] * 2 + [part] * 4,
        out_shape=[jax.ShapeDtypeStruct((rows // 2, cols), BF)] * 4
        + [jax.ShapeDtypeStruct((width // 2, cols), BF)] * 4,
        scratch_shapes=[pltpu.VMEM((width, 2 * cols), F32)],
        compiler_params=params(),
        cost_estimate=BRIEF,
        name="keyval_grad",
    )(marks, own, far, dk, dv)


def query_grad_kernel(marks, x, d0, d1, *refs, parts, count):
    own, far, send, keep = refs[-5:-1]
    acc = refs[-1]
    i = pl.program_id(0)
    a = jnp.concatenate([d0[...], d1[...]], 1)
    if parts:
        a = sum((r[...].astype(F32) for r in refs[:parts]), a.astype(F32)).astype(BF)
    g = dot(x[...], a, TN)

    @pl.when(i == 0)
    def _():
        own[...] = a
        acc[...] = g

    @pl.when(i == 1)
    def _():
        far[...] = a
        acc[...] += g
        halves(acc, marks[0], count, send, keep)


def query_grad_call(marks, count, x, d0, d1, parts, sends):
    rows = d0.shape[0]
    cols = d0.shape[1] + d1.shape[1]
    width = x.shape[1]
    blk = rows // 2
    k = len(sends)
    anywhere = pl.BlockSpec(memory_space=pl.ANY)
    wide = lambda c: pl.BlockSpec((blk, c), lambda i: (i, 0))
    fixed = pl.BlockSpec((blk, cols), lambda i: (0, 0))
    part = pl.BlockSpec((width // 2, cols), lambda i: (0, 0))
    return pl.pallas_call(
        functools.partial(query_grad_kernel, parts=len(parts), count=count),
        grid=(2,),
        in_specs=[pl.BlockSpec(memory_space=pltpu.SMEM), wide(width), wide(d0.shape[1]), wide(d1.shape[1])]
        + [wide(cols)] * len(parts)
        + [anywhere] * k,
        out_specs=[anywhere] * k + [fixed, fixed, part, part],
        out_shape=[jax.ShapeDtypeStruct(y.shape, y.dtype) for y in sends]
        + [jax.ShapeDtypeStruct((blk, cols), BF)] * 2
        + [jax.ShapeDtypeStruct((width // 2, cols), BF)] * 2,
        scratch_shapes=[pltpu.VMEM((width, cols), F32)],
        input_output_aliases={4 + len(parts) + i: i for i in range(k)},
        compiler_params=params(),
        cost_estimate=BRIEF,
        name="query_grad",
    )(marks, x, d0, d1, *parts, *sends)


def in_order(core, own, far):
    a, b = own[...], far[...]
    return jnp.concatenate([jnp.where(core == 0, a, b), jnp.where(core == 0, b, a)], 1)


def carried_grad_kernel(core, ids, ko, kf, vo, vf, wk, wv, out, table):
    acc = dot(in_order(core[0], ko, kf), wk[...], NT) + dot(in_order(core[0], vo, vf), wv[...], NT)
    out[...] = acc
    groups = table.shape[0]
    hot = lax.broadcasted_iota(jnp.int32, (groups, ids.shape[1]), 0) == ids[...]
    hot = hot.astype(F32).astype(BF)
    high = acc.astype(BF)
    rest = (acc - high.astype(F32)).astype(BF)

    @pl.when(pl.program_id(0) == 0)
    def _():
        table[...] = jnp.zeros_like(table)

    table[...] += dot(hot, high) + dot(hot, rest)


def carried_grad_call(core, ids, ko, kf, vo, vf, wk, wv, groups):
    rows, cols = ko.shape
    width = wk.shape[0]
    blk = 512
    wide = pl.BlockSpec((blk, cols), lambda i, o: (i, 0))
    weight = pl.BlockSpec((width, width), lambda i, o: (0, 0))
    return pl.pallas_call(
        carried_grad_kernel,
        grid_spec=pltpu.PrefetchScalarGridSpec(
            num_scalar_prefetch=1,
            grid=(rows // blk,),
            in_specs=[pl.BlockSpec((1, blk), lambda i, o: (0, i))] + [wide] * 4 + [weight] * 2,
            out_specs=[
                pl.BlockSpec((blk, width), lambda i, o: (i, 0)),
                pl.BlockSpec((groups, width), lambda i, o: (0, 0)),
            ],
        ),
        out_shape=[
            jax.ShapeDtypeStruct((rows, width), F32),
            jax.ShapeDtypeStruct((groups, width), F32),
        ],
        compiler_params=params(),
        cost_estimate=BRIEF,
        name="carried_grad",
    )(core[None], ids, ko, kf, vo, vf, wk, wv)


def rays_grad_kernel(spots, dqo, dqf, w, rays, middle, lines, out, sums):
    g = dot(in_order(spots[0], dqo, dqf), w[...], NT)
    gain_row = lines[0:1, :]
    _, unit, scale = norm_forward(rays[...].astype(F32), gain_row, lines[1:2, :])
    back, grad_gain, grad_shift = norm_backward(g, unit, scale, gain_row)
    out[...] = middle[...] + back

    @pl.when(pl.program_id(0) == 0)
    def _():
        sums[...] = jnp.zeros_like(sums)

    sums[0:1, :] += grad_gain[None]
    sums[1:2, :] += grad_shift[None]


def rays_grad_call(spots, dqo, dqf, w, rays, middle, lines):
    rows, cols = dqo.shape
    width = w.shape[0]
    blk = min(256, rows)
    n = rows // blk
    wide = lambda c: pl.BlockSpec((blk, c), lambda i, o: (i, 0))
    return pl.pallas_call(
        rays_grad_kernel,
        grid_spec=pltpu.PrefetchScalarGridSpec(
            num_scalar_prefetch=1,
            grid=(n,),
            in_specs=[
                wide(cols),
                wide(cols),
                pl.BlockSpec((width, width), lambda i, o: (0, 0)),
                pl.BlockSpec((blk, width), lambda i, o: (o[1] * n + i, 0)),
                wide(width),
                pl.BlockSpec(lines.shape, lambda i, o: (0, 0)),
            ],
            out_specs=[wide(width), pl.BlockSpec((8, width), lambda i, o: (0, 0))],
        ),
        out_shape=[
            jax.ShapeDtypeStruct((rows, width), F32),
            jax.ShapeDtypeStruct((8, width), F32),
        ],
        compiler_params=params(),
        cost_estimate=BRIEF,
        name="rays_grad",
    )(spots, dqo, dqf, w, rays, middle, lines)


def finish_kernel(marks, *refs, n, inner, size):
    core = marks[n]
    k = (len(refs) - 3 * n) // 2
    mines, fars, whole = refs[:n], refs[n : 2 * n], refs[2 * n : 2 * n + k]
    outs, wide = refs[2 * n + k : 3 * n + k], refs[3 * n + k :]
    for i, (mine, far, out) in enumerate(zip(mines, fars, outs)):
        cols = mine.shape[1]
        for j in range(inner):
            src = pl.ds(pl.multiple_of((j ^ (marks[i] & (inner - 1))) * size, 16), size)
            dst = slice(j * size, (j + 1) * size)
            out[dst, pl.ds(pl.multiple_of(core * cols, 128), cols)] = mine[src, :].astype(F32)
            out[dst, pl.ds(pl.multiple_of((1 - core) * cols, 128), cols)] = far[src, :].astype(F32)
    for src, dst in zip(whole, wide):
        dst[...] = src[...].astype(F32)


def finish_call(marks, count, mines, fars, whole):
    rows, cols = mines[0].shape
    n = len(mines)
    outer = min(2, count)
    inner = 1 << (count - outer)
    size = rows >> count
    blk = size * inner

    def place(k):
        return pl.BlockSpec((blk, cols), lambda i, m: (i ^ (m[k] // inner), 0))

    cuts = [pl.BlockSpec((x.shape[0] >> outer, x.shape[1]), lambda i, m: (i, 0)) for x in whole]
    return pl.pallas_call(
        functools.partial(finish_kernel, n=n, inner=inner, size=size),
        grid_spec=pltpu.PrefetchScalarGridSpec(
            num_scalar_prefetch=1,
            grid=(1 << outer,),
            in_specs=[place(k) for k in range(n)] * 2 + cuts,
            out_specs=[pl.BlockSpec((blk, 2 * cols), lambda i, m: (i, 0))] * n + cuts,
        ),
        out_shape=[jax.ShapeDtypeStruct((rows, 2 * cols), F32)] * n
        + [jax.ShapeDtypeStruct(x.shape, F32) for x in whole],
        compiler_params=params(),
        cost_estimate=BRIEF,
        name="finish",
    )(marks, *mines, *fars, *whole)


def pair_swap(x, step, sizes):
    axis, mask = step
    return lax.ppermute(x, axis, [(i, i ^ mask) for i in range(sizes[axis])])


def step_bit(step):
    axis, mask = step
    return (lax.axis_index(axis) // mask) % 2


def chip_steps(sizes):
    along = [("dp", 1 << j) for j in range(sizes["dp"].bit_length() - 1)]
    across = [("key", 2 << j) for j in range(sizes["key"].bit_length() - 2)]
    return along[:1] + across[:1] + along[1:2], along[2:] + across[1:]


def turn(first, i):
    i = i % len(first)
    return first[i:] + first[:i]


def halvings(rows, steps):
    count = 0
    while count < len(steps) and rows % 32 == 0:
        rows //= 2
        count += 1
    return count


def mark_of(steps, count):
    return sum(step_bit(x) << (count - 1 - j) for j, x in enumerate(steps[:count]))


def plus(a, b):
    return (a.astype(F32) + b.astype(F32)).astype(a.dtype)


def plus_after_kernel(a, b, _, out):
    half = out.shape[0]
    out[...] = plus(a[half:, :], b[half:, :])


def plus_after(a, b, after):
    whole = pl.BlockSpec(memory_space=pltpu.VMEM)
    return pl.pallas_call(
        plus_after_kernel,
        in_specs=[whole, whole, pl.BlockSpec(memory_space=pl.ANY)],
        out_specs=whole,
        out_shape=jax.ShapeDtypeStruct((a.shape[0] // 2, a.shape[1]), a.dtype),
        compiler_params=params(),
        cost_estimate=BRIEF,
        name="plus_after",
    )(a, b, after)


def tree_scatter(parts, steps, count, sizes, beside):
    sends = [p[0] for p in parts]
    keeps = [p[1] for p in parts]
    for j in range(len(steps[0])):
        recvs = [pair_swap(x, s[j], sizes) for x, s in zip(sends, steps)]
        for i, recv in enumerate(recvs):
            if j + 1 < count:
                half = recv.shape[0] // 2
                if j == 0 and i + 1 == len(steps):
                    sends[i] = plus_after(keeps[i], recv, beside)
                else:
                    sends[i] = plus(keeps[i][half:], recv[half:])
                keeps[i] = plus(keeps[i][:half], recv[:half])
            else:
                sends[i] = keeps[i] = plus(keeps[i], recv)
    return keeps


def join_after_kernel(a, b, _, out):
    half = a.shape[0]
    out[:half, :] = a[...]
    out[half:, :] = b[...]


def join_after(a, b, after):
    whole = pl.BlockSpec(memory_space=pltpu.VMEM)
    return pl.pallas_call(
        join_after_kernel,
        in_specs=[whole, whole, pl.BlockSpec(memory_space=pl.ANY)],
        out_specs=whole,
        out_shape=jax.ShapeDtypeStruct((2 * a.shape[0], a.shape[1]), a.dtype),
        compiler_params=params(),
        cost_estimate=BRIEF,
        name="join_after",
    )(a, b, after)


def tree_gather(mines, steps, count, sizes, small):
    turns = list(steps[0])
    for j in reversed(range(count)):
        recvs = [pair_swap(x, s[j], sizes) for x, s in zip(mines, steps)]
        while len(turns) > j:
            small = plus(small, pair_swap(small, turns.pop(0), sizes))
        pairs = list(zip(mines, recvs))
        mines = [jnp.concatenate(x, 0) for x in pairs[:-1]] + [join_after(*pairs[-1], small)]
    return mines, small


def local(
    ray_tokens,
    latents,
    group_ids,
    ln1_gain,
    ln1_shift,
    w_query,
    w_key,
    w_value,
    w_out,
    ln2_gain,
    ln2_shift,
    w_up,
    b_up,
    w_down,
    b_down,
    intrinsics,
    out_grad,
    *,
    sizes,
):
    keys = sizes["key"]
    share = out_grad.shape[0]
    width = ray_tokens.shape[1]
    cols = width // 2
    pairs = cols // PAIR
    chips = keys // 2
    chip_rows = 2 * share
    place = lax.axis_index("key")
    core = place % 2
    chip = place // 2

    def core_swap(x):
        return lax.ppermute(x, "key", [(i, i ^ 1) for i in range(keys)])

    def chip_shift(x, s):
        return lax.ppermute(x, "key", [(i, (i + 2 * s) % keys) for i in range(keys)])

    lookup = group_ids[0][:, None] == jnp.arange(intrinsics.shape[0], dtype=jnp.int32)[None, :]
    carried = (
        latents[0].astype(F32)
        + jnp.dot(lookup.astype(BF), intrinsics, preferred_element_type=F32)
    ).astype(BF)
    tokens = carried.shape[0]
    carried_far = core_swap(carried)
    lines = jnp.concatenate(
        [x.reshape(-1, width) for x in (ln1_gain, ln1_shift, ln2_gain, ln2_shift, b_down, b_up)], 0
    ).astype(F32)
    steps = jnp.arange(keys, dtype=jnp.int32)
    order = ((chip + steps // 2) % chips) * 2 + (core + steps % 2) % 2
    normed, queries = query_call(order, core, ray_tokens, lines, w_query, share)
    key_rows, value_rows, key_cols, value_cols = keyval_call(
        core, carried, carried_far, w_key, w_value
    )

    stats, exps, os, sts = [None] * chips, [None] * chips, [None] * chips, [None] * chips
    ordered = queries
    for t in [*range(1, chips), 0]:
        o, st, e = attend_call(
            ordered, key_rows, value_cols, t * chip_rows, chip_rows, "far" if t else "own"
        )
        stats[t], exps[t] = st, e
        if t:
            ordered, o, st = lax.optimization_barrier((ordered, o, st))
        os[t], sts[t] = (chip_shift(o, t), chip_shift(st, t)) if t else (o, st)
    att, low_own, low_send, lse = combine_call(os, sts)
    low_far = core_swap(low_send)
    spots = jnp.stack([core, place])
    output, grad_middle, do_own, do_far, active, grad_hidden, normed_two, branch, branch_sums = (
        mlp_call(
            spots,
            low_own,
            low_far,
            ray_tokens,
            w_out,
            w_up,
            w_down,
            lines,
            out_grad,
        )
    )
    do_chip, aux_chip = delta_call(do_own, core_swap(do_far), att, lse)
    attended_low = jnp.concatenate(
        [jnp.where(core == 0, low_own, low_far), jnp.where(core == 0, low_far, low_own)], 1
    )
    branch_grads = lax.psum(
        (
            dot(attended_low, branch, TN).astype(BF),
            dot(normed_two, grad_hidden, TN).astype(BF),
            dot(active, out_grad, TN).astype(BF),
        ),
        ("dp", "key"),
    )

    first, rest = chip_steps(sizes)
    steps = [turn(first, i) + rest for i in range(3)]
    count = halvings(width, steps[0])
    marks = jnp.stack([mark_of(x, count) for x in steps] + [core]).astype(jnp.int32)

    dos, auxs = [do_chip], [aux_chip]
    for t in range(1, chips):
        dos.append(chip_shift(do_chip, chips - t))
        auxs.append(chip_shift(aux_chip, chips - t))

    def back(t, carry, pair0, count, fresh, name):
        return backward_call(
            exps[t],
            dos[t],
            queries,
            stats[t],
            auxs[t],
            key_cols,
            value_rows,
            carry,
            t * chip_rows,
            pair0,
            count,
            fresh,
            name,
        )

    early = pairs - 1
    dq_first, *first_carry = back(0, None, 0, early, 0, "own_first")

    def rest_of_backward():
        carry = first_carry
        parts = []
        for t in range(1, chips):
            dq, *carry = back(t, carry, 0, pairs, early if t == 1 else pairs, "far")
            parts.append(chip_shift(dq, t))
        dq_rest, *carry = back(0, carry, early, pairs - early, pairs, "own_rest")
        keys_own, keys_far, values_own, values_far, key_send, key_keep, value_send, value_keep = (
            keyval_grad_call(marks, count, carried, carried_far, *carry)
        )
        tokens_far = [core_swap(x) for x in (keys_far, values_far)]
        key_send, value_send, queries_own, queries_far, query_send, query_keep = query_grad_call(
            marks, count, normed, dq_first, dq_rest, parts, (key_send, value_send)
        )
        queries_far = core_swap(queries_far)
        rays_grad, norm_sums = rays_grad_call(
            spots,
            queries_own,
            queries_far,
            w_query,
            ray_tokens,
            grad_middle,
            lines,
        )
        grad_carried, grad_table = carried_grad_call(
            core,
            group_ids,
            keys_own,
            tokens_far[0],
            values_own,
            tokens_far[1],
            w_key,
            w_value,
            intrinsics.shape[0],
        )
        small = jnp.concatenate([norm_sums, branch_sums, grad_table], 0)
        small = small + core_swap(small)
        sums = tree_scatter(
            [(query_send, query_keep), (key_send, key_keep), (value_send, value_keep)],
            steps,
            count,
            sizes,
            grad_table,
        )
        sums, small = tree_gather(sums, steps, count, sizes, small)
        far_sums = [core_swap(g) for g in sums]
        up_rows = b_up.shape[0] // width
        table_row = 8 + branch_sums.shape[0]
        grads = [
            small[0],
            small[1],
            small[8],
            small[9],
            small[11 : 11 + up_rows].reshape(-1),
            small[10],
            small[table_row:],
        ]
        return rays_grad, grad_carried, sums, far_sums, grads

    shapes = jax.eval_shape(rest_of_backward)
    rays_grad, grad_carried, sums, far_sums, grads = lax.cond(
        group_ids[0, 0] >= 0,
        rest_of_backward,
        lambda: jax.tree.map(lambda x: jnp.zeros(x.shape, x.dtype), shapes),
    )
    *attention_grads, grad_out, grad_up, grad_down = finish_call(
        marks, count, sums, far_sums, branch_grads
    )
    branch_grads = (grad_out, grad_up, grad_down)
    return (
        output,
        rays_grad,
        grad_carried[None],
        grads[0],
        grads[1],
        attention_grads[0],
        attention_grads[1],
        attention_grads[2],
        branch_grads[0],
        grads[2],
        grads[3],
        branch_grads[1],
        grads[4],
        branch_grads[2],
        grads[5],
        grads[6],
    )


def solution(mesh):
    rows = P(("dp", "key"), None)
    placed = (P("dp", None), P("dp", "key", None), P("dp", "key")) + (P(),) * 13 + (rows,)
    return jax.shard_map(
        functools.partial(local, sizes=dict(mesh.shape)),
        mesh=mesh,
        in_specs=placed,
        out_specs=(rows, rows, P("dp", "key", None)) + (P(),) * 13,
        check_vma=False,
    )
```
